128 devices in a mesh: var: 16 (over y_lo, z, core), samp: 8 (over y_hi, x).
Axes of the slice: x: 4, y: 4 (y_hi: 2, y_lo: 2; y = y_hi * 2 + y_lo), z: 4, core: 2. Of those that a mesh axis runs over, the one named last changes fastest.
Arguments:
- geno: bfloat16 [16384, 32768], P('samp', 'var'), may hold values from -5 to 5
- scale_index: int32 [128, 32768], P('samp', 'var'), may hold values from 0 to 15
- scale_table: float32 [16], replicated, may hold values from 0.25 to 4
- residual: float32 [8, 16384], P(None, 'samp'), may hold values from -6 to 6
- beta_active: float32 [8, 7168], P(None, 'var'), may hold values from -6 to 6
- block_inverse: float32 [32, 256, 256], P('var'), may hold values from -1 to 4
- active_ids: int32 [7168], P('var'), may hold values from 0 to 32767, as said below
- admit_ids: int32 [1024], P('var'), may hold values from 0 to 32767, as said below
Outputs:
- scores: float32 [8, 32768], P(None, 'var')
- coefficients: float32 [8, 8192], P(None, 'var')
- residual_out: float32 [8, 16384], P(None, 'samp')
The draws below stay inside these ranges and needn't reach their ends.
Inputs may be any that keep to these rules, and one draw needn't show every extreme that they name: Variant ids, all different from one another and from those of admit_ids. The fitting slots of one index of var are its 448 entries of active_ids followed by its 64 entries of admit_ids; of these 512 slots at most 64 name variants held by any one index of var, and for every index of var some one holder reaches exactly 64. `admit_ids`: variant ids, as for active_ids.
All inputs are finite; a program needn't handle non-finite values.
Results may differ from the reference program's by a relative error of at most 0.004.
Values may be sent and summed in bfloat16 or wider, within the bound.
No kernel may reach another device: no remote copies, remote signals or barrier semaphores. Data moves between devices by JAX's collectives and lax.ppermute only.
A program may use at most 128 MiB of HBM per device.

```python
import math
import jax
import jax.numpy as jnp
from jax import lax

PHENO = 8
BLOCK = 256
GROUP = 128
LEVELS = 16
PASSES = 3
VAR_DEV = 2048
ADM_DEV = 64
FIT_DEV = 512
ACT_DEV = 448
SAMPLES = 16384
VARIANTS = 32768
ACTIVE = 7168
FIT = 8192
NBLK = 32
N_VAR = 16


def fit_layout(key):
    base_key = jax.random.fold_in(key, 7)
    holders = N_VAR
    capacity = 2 * FIT_DEV // holders
    pairing = jax.vmap(lambda keyed: jax.random.permutation(keyed, holders))(jax.random.split(jax.random.fold_in(base_key, 1), holders))
    shares = jax.random.randint(jax.random.fold_in(base_key, 2), (holders, holders // 2), 0, capacity + 1, dtype=jnp.int32)
    shares = shares.at[:, 0].set(0)
    paired = jnp.stack([capacity - shares, shares], -1).reshape(holders, holders)
    rows_index = jnp.arange(holders, dtype=jnp.int32)[:, None]
    counts = jnp.zeros((holders, holders), jnp.int32).at[rows_index, pairing].set(paired)
    finish = jnp.cumsum(counts, 1)
    anchor = finish - counts
    slot_range = jnp.arange(FIT_DEV, dtype=jnp.int32)
    holder = jnp.sum((finish[:, None, :] <= slot_range[None, :, None]).astype(jnp.int32), -1)
    serial = slot_range[None, :] - jnp.take_along_axis(anchor, holder, 1)
    offsets = jnp.cumsum(counts, 0) - counts
    shuffled = jax.vmap(lambda keyed: jax.random.permutation(keyed, VAR_DEV))(jax.random.split(jax.random.fold_in(base_key, 3), holders))
    column = shuffled[holder, jnp.take_along_axis(offsets, holder, 1) + serial]
    chosen = holder * VAR_DEV + column
    reorder = jax.vmap(lambda keyed: jax.random.permutation(keyed, FIT_DEV))(jax.random.split(jax.random.fold_in(base_key, 4), holders))
    return jnp.take_along_axis(chosen, reorder, 1).astype(jnp.int32)


def draw_active_ids(key, part):
    return fit_layout(key)[:, :ACT_DEV].reshape(-1)


def draw_admit_ids(key, part):
    return fit_layout(key)[:, ACT_DEV:].reshape(-1)


def draw_block_inverse(key, part):
    noise = jax.random.normal(jax.random.fold_in(key, 11), (NBLK, BLOCK, BLOCK), jnp.float32)
    diagonal = jnp.exp(jax.random.uniform(jax.random.fold_in(key, 12), (NBLK, BLOCK), jnp.float32, 0.0, 0.6931))
    spread = 0.35
    symmetric = (noise + jnp.swapaxes(noise, 1, 2)) * (spread / (2.0 * BLOCK) ** 0.5)
    return jnp.eye(BLOCK, dtype=jnp.float32)[None, :, :] * diagonal[:, :, None] + symmetric


def set_ends(drawn, key, smallest, largest):
    longest = drawn.shape.index(max(drawn.shape))
    spots = []
    for shift in (0, 1):
        where = [jax.random.randint(jax.random.fold_in(key, axis), (), 0, length) for axis, length in enumerate(drawn.shape)]
        where[longest] = (where[longest] + shift) % drawn.shape[longest]
        spots.append(tuple(where))
    return drawn.at[spots[0]].set(smallest).at[spots[1]].set(largest)


def block_scale(own_key, extent, pieces, low, top_value):
    loudness, own = 1.0, jax.random.fold_in(own_key, 6)
    for dim, blocks in pieces:
        steps = jnp.exp(jax.random.uniform(jax.random.fold_in(own, dim), (blocks,), jnp.float32, low / len(pieces), top_value / len(pieces)))
        loudness = loudness * jnp.repeat(steps, extent[dim] // blocks).reshape([-1 if axis == dim else 1 for axis in range(len(extent))])
    return loudness


def gaussian(rng, extent, width, bound, shards=(), kind=jnp.bfloat16):
    entries = jax.random.normal(rng, extent, jnp.float32) * width
    if len(shards) > 0:
        entries = block_scale(rng, extent, shards, -0.22, 0.18) * entries
    return jnp.clip(entries, min=-bound, max=bound).astype(kind)


def setup_inputs(seed: int = 0) -> dict:
    key_of = jax.random.split(jax.random.key(seed), 9)
    geno = gaussian(key_of[0], (SAMPLES, VARIANTS), 1.0, 5.0, ((0, 8), (1, 16)))
    scale_index = set_ends(jax.random.randint(key_of[1], (SAMPLES // GROUP, VARIANTS), 0, LEVELS), jax.random.fold_in(key_of[1], 1), 0, LEVELS - 1).astype(jnp.int32)
    scale_table = jnp.clip(jnp.exp(jax.random.uniform(key_of[2], (LEVELS,), jnp.float32, math.log(0.25), math.log(4.0))), 0.25, 4.0)
    residual = gaussian(key_of[3], (PHENO, SAMPLES), 1.0, 6.0, ((1, 8),), jnp.float32)
    beta_active = gaussian(key_of[4], (PHENO, ACTIVE), 1.0, 6.0, ((1, 16),), jnp.float32)
    block_inverse = draw_block_inverse(jax.random.fold_in(key_of[8], 71), 0)
    active_ids = draw_active_ids(jax.random.fold_in(key_of[8], 71), 0)
    admit_ids = draw_admit_ids(jax.random.fold_in(key_of[8], 71), 0)
    return {"geno": geno, "scale_index": scale_index, "scale_table": scale_table, "residual": residual, "beta_active": beta_active, "block_inverse": block_inverse, "active_ids": active_ids, "admit_ids": admit_ids}


penalty = 0.5
epsilon = 1e-06

def dequantize(values, indices, lookup):
    groups = indices.shape[0]
    scales = lookup[indices]
    widened = values.reshape(groups, values.shape[0] // groups, values.shape[1]).astype(jnp.float32) * scales[:, None, :]
    return widened.reshape(values.shape).astype(jnp.bfloat16)

def reference(geno, scale_index, scale_table, residual, beta_active, block_inverse, active_ids, admit_ids):
    inv_root = 1.0 / math.sqrt(SAMPLES)
    resid_low = residual.astype(jnp.bfloat16)

    def screen_block(block_index):
        first_column = block_index * VAR_DEV
        values = lax.dynamic_slice_in_dim(geno, first_column, VAR_DEV, 1)
        indices = lax.dynamic_slice_in_dim(scale_index, first_column, VAR_DEV, 1)
        return jnp.dot(resid_low, dequantize(values, indices, scale_table), preferred_element_type=jnp.float32)
    blocks = lax.map(screen_block, jnp.arange(N_VAR, dtype=jnp.int32))
    scores = jnp.transpose(blocks, (1, 0, 2)).reshape(PHENO, VARIANTS) * inv_root
    fit_ids = jnp.concatenate([active_ids.reshape(N_VAR, ACT_DEV), admit_ids.reshape(N_VAR, ADM_DEV)], 1).reshape(FIT)
    fitting = dequantize(jnp.take(geno, fit_ids, axis=1), jnp.take(scale_index, fit_ids, axis=1), scale_table)
    coeffs = jnp.concatenate([beta_active.reshape(PHENO, N_VAR, ACT_DEV), jnp.zeros((PHENO, N_VAR, ADM_DEV), jnp.float32)], 2).reshape(PHENO, FIT)
    current = residual
    for pass_index in range(PASSES):
        gradient = jnp.dot(current.astype(jnp.bfloat16), fitting, preferred_element_type=jnp.float32) * inv_root
        inner_term = (gradient - penalty * coeffs).reshape(PHENO, NBLK, BLOCK)
        direction = jnp.einsum('bij,pbj->pbi', block_inverse, inner_term, precision=lax.Precision.HIGHEST)
        direction = direction.reshape(PHENO, FIT).astype(jnp.bfloat16)
        update = jnp.dot(direction, fitting.T, preferred_element_type=jnp.float32) * inv_root
        cross_sum = lax.optimization_barrier(jnp.sum(current * update, 1))
        square = lax.optimization_barrier(jnp.sum(update * update, 1)) + epsilon
        factor = (cross_sum / square)[:, None]
        current = current - factor * update
        coeffs = coeffs + factor * direction.astype(jnp.float32)
    return (scores, coeffs, current)
```

```python
import functools
import math

import jax
import jax.numpy as jnp
from jax import lax
from jax.experimental import pallas as pl
from jax.experimental.pallas import tpu as pltpu
from jax.sharding import Mesh
from jax.sharding import PartitionSpec as P

PASSES = 3
VAR = ("y_lo", "z", "core")
SAMP = ("y_hi", "x")
CHIPS = ("y_lo", "z")

CAP = 64
LANES = 128
ROWS = 256
HALF = 4

penalty = 0.5
epsilon = 1e-06
LIMIT = pltpu.CompilerParams(vmem_limit_bytes=48 * 1024 * 1024)
f32 = jnp.float32
bf16 = jnp.bfloat16


def iota(shape, dim):
    return lax.broadcasted_iota(jnp.int32, shape, dim)


def dot(a, b, **kw):
    return jnp.dot(a, b, preferred_element_type=f32, **kw)


def dot_t(a, b, **kw):
    return lax.dot_general(a, b, (((1,), (1,)), ((), ())), preferred_element_type=f32, **kw)


def thirds(x):
    high = x.astype(bf16)
    rest = x - high.astype(f32)
    mid = rest.astype(bf16)
    return high, mid, (rest - mid.astype(f32)).astype(bf16)


def swapped(x):
    here = (iota(x.shape, 0) // HALF) == (iota(x.shape, 1) // CAP)
    return jnp.where(here, x, pltpu.roll(pltpu.roll(x, HALF, 0), CAP, 1))


def column_row(packed):
    low = iota((1, LANES), 1) < CAP
    return jnp.concatenate(
        [
            jnp.where(low, packed[t : t + 1], packed[t + 1 : t + 2])
            for t in range(0, packed.shape[0], 2)
        ],
        1,
    )


def slot_maps(serial, holder, holders):
    fit = serial.shape[1]
    serial2 = jnp.concatenate([serial, serial], 1)
    holder2 = jnp.concatenate([holder, holder], 1)
    shape = (2 * CAP, 2 * fit)
    rows, cols = iota(shape, 0), iota(shape, 1)
    spread = ((rows // CAP) == (cols // fit)) & ((rows % CAP) == serial2)
    mask = (iota((holders * HALF, 2 * fit), 0) // HALF) == holder2
    return spread.astype(f32).astype(bf16), mask.astype(f32)


def layout_kernel(holder_ref, column_ref, serial_ref, packed_ref):
    holders = packed_ref.shape[0]
    fit = holder_ref.shape[1]
    holder = holder_ref[...]
    marks = (iota((holders, fit), 0) == holder).astype(f32)
    earlier = (iota((fit, fit), 0) < iota((fit, fit), 1)).astype(f32).astype(bf16)
    before = dot(marks.astype(bf16), earlier)
    serial = jnp.sum(before * marks, 0, keepdims=True).astype(jnp.int32)
    serial_ref[...] = serial
    spread, _ = slot_maps(serial, holder, holders)
    marks2 = jnp.concatenate([marks, marks], 1)
    column = column_ref[...] + 1
    parts = []
    for piece in (column // LANES, column % LANES):
        row = piece.astype(f32)
        row = jnp.concatenate([row, row], 1)
        parts.append(dot_t((marks2 * row).astype(bf16), spread))
    packed_ref[...] = (parts[0] * LANES + parts[1]).astype(jnp.int32)


def layout(holder, column, holders):
    return pl.pallas_call(
        layout_kernel,
        out_shape=(
            jax.ShapeDtypeStruct(holder.shape, jnp.int32),
            jax.ShapeDtypeStruct((holders, LANES), jnp.int32),
        ),
        compiler_params=LIMIT,
        name="layout",
    )(holder, column)


def look_up(table_ref, index_ref, scales_ref):
    index = index_ref[...]
    scales = jnp.full(index.shape, table_ref[0], f32)
    for level in range(1, table_ref.shape[0]):
        scales = jnp.where(index == level, table_ref[level], scales)
    scales_ref[...] = scales


def dequantized(geno_ref, scales_ref, step):
    rows = geno_ref.shape[0]
    group = 128
    out = []
    for g in range(rows // group):
        scale = scales_ref[pl.ds(step * (rows // group) + g, 1), :]
        wide = geno_ref[g * group : (g + 1) * group, :].astype(f32) * scale
        out.append(wide.astype(bf16))
    return jnp.concatenate(out, 0)


def screen_kernel(table_ref, geno_ref, index_ref, resid_ref, out_ref, scales_ref):
    step = pl.program_id(0)

    @pl.when(step == 0)
    def _():
        look_up(table_ref, index_ref, scales_ref)
        out_ref[...] = jnp.zeros_like(out_ref)

    out_ref[...] += dot(resid_ref[...].astype(bf16), dequantized(geno_ref, scales_ref, step))


def screen(table, geno, index, resid):
    samples, width = geno.shape
    phenos = resid.shape[0]
    return pl.pallas_call(
        screen_kernel,
        grid=(samples // ROWS,),
        in_specs=[
            pl.BlockSpec(memory_space=pltpu.SMEM),
            pl.BlockSpec((ROWS, width), lambda i: (i, 0)),
            pl.BlockSpec(index.shape, lambda i: (0, 0)),
            pl.BlockSpec((phenos, ROWS), lambda i: (0, i)),
        ],
        out_specs=pl.BlockSpec((phenos, width), lambda i: (0, 0)),
        out_shape=jax.ShapeDtypeStruct((phenos, width), f32),
        scratch_shapes=[pltpu.VMEM(index.shape, f32)],
        compiler_params=LIMIT,
        cost_estimate=pl.CostEstimate(
            flops=2 * phenos * samples * width, bytes_accessed=2 * samples * width, transcendentals=0
        ),
        name="screen",
    )(table, geno, index, resid)


def select_kernel(table_ref, packed_ref, geno_ref, index_ref, out_ref, scales_ref, pick_ref):
    step = pl.program_id(0)

    @pl.when(step == 0)
    def _():
        look_up(table_ref, index_ref, scales_ref)
        wanted = column_row(packed_ref[...])

        @pl.loop(0, pick_ref.shape[0], step=ROWS)
        def _(at):
            here = iota((ROWS, pick_ref.shape[1]), 0) + (at + 1) == wanted
            pick_ref[pl.ds(pl.multiple_of(at, ROWS), ROWS), :] = here.astype(f32).astype(bf16)

    out_ref[...] = dot(dequantized(geno_ref, scales_ref, step), pick_ref[...]).astype(bf16)


def select(table, packed, geno, index):
    samples, width = geno.shape
    held = packed.shape[0] * CAP
    return pl.pallas_call(
        select_kernel,
        grid=(samples // ROWS,),
        in_specs=[
            pl.BlockSpec(memory_space=pltpu.SMEM),
            pl.BlockSpec(packed.shape, lambda i: (0, 0)),
            pl.BlockSpec((ROWS, width), lambda i: (i, 0)),
            pl.BlockSpec(index.shape, lambda i: (0, 0)),
        ],
        out_specs=pl.BlockSpec((ROWS, held), lambda i: (i, 0)),
        out_shape=jax.ShapeDtypeStruct((samples, held), bf16),
        scratch_shapes=[pltpu.VMEM(index.shape, f32), pltpu.VMEM((width, held), bf16)],
        compiler_params=LIMIT,
        cost_estimate=pl.CostEstimate(
            flops=2 * samples * width * held, bytes_accessed=2 * samples * width, transcendentals=0
        ),
        name="select",
    )(table, packed, geno, index)


def pick_kernel(inv_root, parts_ref, packed_ref, scores_ref, pay_ref):
    scores = parts_ref[0]
    for j in range(1, parts_ref.shape[0]):
        scores = scores + parts_ref[j]
    scores = scores * inv_root
    scores_ref[...] = scores
    wanted = column_row(packed_ref[...])
    stacked = jnp.concatenate(thirds(scores), 0)
    phenos, width = scores.shape
    total = jnp.zeros((stacked.shape[0], wanted.shape[1]), f32)
    for at in range(0, width, ROWS):
        here = iota((ROWS, wanted.shape[1]), 0) + (at + 1) == wanted
        total += dot(stacked[:, at : at + ROWS], here.astype(f32).astype(bf16))
    held = total[:phenos] + total[phenos : 2 * phenos] + total[2 * phenos :]
    for t in range(wanted.shape[1] // LANES):
        pay_ref[8 * t : 8 * t + 8, :] = swapped(held[:, t * LANES : (t + 1) * LANES])


def pick(parts, packed, inv_root):
    return pl.pallas_call(
        functools.partial(pick_kernel, inv_root),
        out_shape=(
            jax.ShapeDtypeStruct(parts.shape[1:], f32),
            jax.ShapeDtypeStruct((packed.shape[0] * HALF, LANES), f32),
        ),
        compiler_params=LIMIT,
        name="pick",
    )(parts, packed)


def direction_step(data, serial_ref, holder_ref, inverse_ref, advance, wide_ref, d_ref, pay_ref):
    fit = serial_ref.shape[1]
    holders = data.shape[0] // HALF
    spread, mask = slot_maps(serial_ref[...], holder_ref[...], holders)
    high, mid, low = thirds(data)
    placed = (dot(high, spread) + dot(mid, spread) + dot(low, spread)) * mask
    placed = jnp.sum(placed.reshape(-1, 2 * HALF, 2 * fit), 0)
    arrived = placed[:HALF] + placed[HALF:]
    inner = advance(arrived)
    wide_ref[:HALF, :] = inner[:, :fit]
    wide_ref[HALF:, :] = inner[:, fit:]
    blocks, size = inverse_ref.shape[0], inverse_ref.shape[1]
    for b in range(blocks):
        moved = dot_t(
            wide_ref[:, b * size : (b + 1) * size], inverse_ref[b], precision=lax.Precision.HIGHEST
        )
        moved = moved.astype(bf16).astype(f32)
        d_ref[:, b * size : (b + 1) * size] = moved[:HALF]
        d_ref[:, fit + b * size : fit + (b + 1) * size] = moved[HALF:]
    d = d_ref[...]
    d = jnp.concatenate([d, d], 0)
    d = jnp.broadcast_to(d[None], (holders * HALF // d.shape[0], *d.shape)).reshape(mask.shape)
    pay_ref[...] = dot_t((d * mask).astype(bf16), spread)


def first_owner_kernel(
    data_ref, serial_ref, holder_ref, inverse_ref, beta_ref, pay_ref, g_ref, b_ref, d_ref, wide_ref
):
    fit = serial_ref.shape[1]
    active = beta_ref.shape[1]
    b_ref[...] = jnp.zeros_like(b_ref)
    b_ref[:, :active] = beta_ref[:HALF]
    b_ref[:, fit : fit + active] = beta_ref[HALF:]

    def advance(arrived):
        g_ref[...] = arrived
        return arrived - penalty * b_ref[...]

    direction_step(
        data_ref[...], serial_ref, holder_ref, inverse_ref, advance, wide_ref, d_ref, pay_ref
    )


def owner_kernel(
    data_ref,
    serial_ref,
    holder_ref,
    inverse_ref,
    g_in,
    b_in,
    d_in,
    pay_ref,
    g_ref,
    b_ref,
    d_ref,
    factor_ref,
    wide_ref,
    sum_ref,
    rows_ref,
    scalar_ref,
):
    fit = serial_ref.shape[1]
    chunk = sum_ref.shape[0]
    total = data_ref[:chunk, :]
    for at in range(chunk, data_ref.shape[0], chunk):
        total = total + data_ref[at : at + chunk, :]
    sum_ref[...] = total
    for k in range(chunk // (HALF + 1)):
        at = k * (HALF + 1)
        rows_ref[k * HALF : (k + 1) * HALF, :] = sum_ref[at : at + HALF, :]
        if k < scalar_ref.shape[0]:
            scalar_ref[k : k + 1, :] = sum_ref[at + HALF : at + HALF + 1, :]
    factor = scalar_ref[:, :1] / (scalar_ref[:, CAP : CAP + 1] + epsilon)
    factor_ref[...] = jnp.broadcast_to(factor, factor_ref.shape)
    low = iota((HALF, 2 * fit), 1) < fit
    factor = jnp.where(low, factor[:HALF], factor[HALF:])

    def advance(arrived):
        g_ref[...] = g_in[...] - factor * arrived
        b_ref[...] = b_in[...] + factor * d_in[...]
        return g_ref[...] - penalty * b_ref[...]

    direction_step(
        rows_ref[...], serial_ref, holder_ref, inverse_ref, advance, wide_ref, d_ref, pay_ref
    )


def owner(data, serial, holder, inverse, state):
    fit = serial.shape[1]
    phenos = 2 * HALF
    held = jax.ShapeDtypeStruct((HALF, 2 * fit), f32)
    wide = pltpu.VMEM((phenos, fit), f32)
    if len(state) == 1:
        return pl.pallas_call(
            first_owner_kernel,
            out_shape=(jax.ShapeDtypeStruct(data.shape, f32), held, held, held),
            scratch_shapes=[wide],
            compiler_params=LIMIT,
            name="owner_first",
        )(data, serial, holder, inverse, *state)
    holders = lax.axis_size(VAR)
    return pl.pallas_call(
        owner_kernel,
        out_shape=(
            jax.ShapeDtypeStruct((holders * HALF, LANES), f32),
            held,
            held,
            held,
            jax.ShapeDtypeStruct((phenos, LANES), f32),
        ),
        scratch_shapes=[
            wide,
            pltpu.VMEM((holders * (HALF + 1), LANES), f32),
            pltpu.VMEM((holders * HALF, LANES), f32),
            pltpu.VMEM((phenos, LANES), f32),
        ],
        compiler_params=LIMIT,
        name="owner_next",
    )(data, serial, holder, inverse, *state)


def update_kernel(pay_ref, columns_ref, out_ref):
    packed = jnp.concatenate(
        [swapped(pay_ref[at : at + 8, :]) for at in range(0, pay_ref.shape[0], 8)], 1
    )
    out_ref[...] = dot_t(packed.astype(bf16), columns_ref[...])


def partial_update(pay, columns):
    samples, held = columns.shape
    rows = 2 * ROWS
    return pl.pallas_call(
        update_kernel,
        grid=(samples // rows,),
        in_specs=[
            pl.BlockSpec(pay.shape, lambda i: (0, 0)),
            pl.BlockSpec((rows, held), lambda i: (i, 0)),
        ],
        out_specs=pl.BlockSpec((2 * HALF, rows), lambda i: (0, i)),
        out_shape=jax.ShapeDtypeStruct((2 * HALF, samples), f32),
        compiler_params=LIMIT,
        name="update",
    )(pay, columns)


def descent_kernel(inv_root, rank_ref, update_ref, resid_ref, columns_ref, out_ref, acc_ref, dots_ref):
    step = pl.program_id(0)
    phenos = update_ref.shape[0]

    @pl.when(step == 0)
    def _():
        acc_ref[...] = jnp.zeros_like(acc_ref)
        dots_ref[...] = jnp.zeros_like(dots_ref)

    update = update_ref[...]
    high = update.astype(bf16)
    low = (update - high.astype(f32)).astype(bf16)
    acc_ref[...] += dot(jnp.concatenate([high, low], 0), columns_ref[...])
    dots_ref[0] += resid_ref[...] * update
    dots_ref[1] += update * update

    @pl.when(step == pl.num_programs(0) - 1)
    def _():
        grad = (acc_ref[:phenos, :] + acc_ref[phenos:, :]) * inv_root
        cross = jnp.sum(dots_ref[0], 1, keepdims=True)
        square = jnp.sum(dots_ref[1], 1, keepdims=True)
        shape = (phenos, LANES)
        both = jnp.where(iota(shape, 1) < CAP, cross, square)
        mine = iota(shape, 0) == lax.rem(rank_ref[0], phenos)
        row = jnp.sum(jnp.where(mine, both, 0.0), 0, keepdims=True)
        chunk = HALF + 1
        owners = grad.shape[1] // CAP
        copies = out_ref.shape[0] // (chunk * owners)
        for t in range(owners // 2):
            pair = swapped(grad[:, t * LANES : (t + 1) * LANES])
            for n in range(copies):
                at = (n * owners + 2 * t) * chunk
                out_ref[at : at + HALF, :] = pair[:HALF]
                out_ref[at + HALF : at + HALF + 1, :] = row
                out_ref[at + chunk : at + chunk + HALF, :] = pair[HALF:]
                out_ref[at + chunk + HALF : at + 2 * chunk, :] = row


def descent(rank, update, resid, columns, inv_root, copies):
    samples, held = columns.shape
    phenos = update.shape[0]
    rows = 2 * ROWS
    out = (copies * (held // CAP) * (HALF + 1), LANES)
    return pl.pallas_call(
        functools.partial(descent_kernel, inv_root),
        grid=(samples // rows,),
        in_specs=[
            pl.BlockSpec(memory_space=pltpu.SMEM),
            pl.BlockSpec((phenos, rows), lambda i: (0, i)),
            pl.BlockSpec((phenos, rows), lambda i: (0, i)),
            pl.BlockSpec((rows, held), lambda i: (i, 0)),
        ],
        out_specs=pl.BlockSpec(out, lambda i: (0, 0)),
        out_shape=jax.ShapeDtypeStruct(out, f32),
        scratch_shapes=[
            pltpu.VMEM((2 * phenos, held), f32),
            pltpu.VMEM((2, phenos, rows), f32),
        ],
        compiler_params=LIMIT,
        name="descent",
    )(rank, update, resid, columns)


def to_all(x, axes):
    copies = jnp.broadcast_to(x[None], (lax.axis_size(axes), *x.shape))
    return lax.all_to_all(copies, axes, split_axis=0, concat_axis=0, tiled=True)


def exchange(pay, axes):
    count = lax.axis_size(axes)
    rows = pay.shape[0] // count
    shape = (count, rows, LANES) if rows == HALF else (count, 1, rows * LANES)
    return lax.all_to_all(
        pay.reshape(shape), axes, split_axis=0, concat_axis=0, tiled=True
    ).reshape(pay.shape)


def other_core(x):
    return lax.ppermute(x, "core", [(0, 1), (1, 0)])


def sum_over_var(part):
    first = lax.axis_index("core") == 0
    half = part.shape[1] // 2
    a, b = part[:, :half], part[:, half:]
    mine = jnp.where(first, a, b) + other_core(jnp.where(first, b, a))
    mine = jnp.sum(to_all(mine, CHIPS), 0)
    other = other_core(mine)
    return jnp.concatenate([jnp.where(first, mine, other), jnp.where(first, other, mine)], 1)


def on_device(
    geno, scale_index, scale_table, residual, beta_active, block_inverse, active_ids, admit_ids
):
    holders = lax.axis_size(VAR)
    rank = lax.axis_index(VAR).astype(jnp.int32).reshape(1)
    samples, width = geno.shape
    copies = lax.axis_size(SAMP)
    inv_root = 1.0 / math.sqrt(samples * copies)

    ids = jnp.concatenate([active_ids, admit_ids])[None]
    holder = ids // width
    serial, packed = layout(holder, ids % width, holders)
    packed = lax.all_to_all(
        packed.reshape(holders, 1, LANES), VAR, split_axis=0, concat_axis=0, tiled=True
    ).reshape(holders, LANES)

    parts = screen(scale_table, geno, scale_index, residual)
    columns = select(scale_table, packed, geno, scale_index)
    scores, pay = pick(to_all(parts, SAMP), packed, inv_root)

    pay, *state = owner(exchange(pay, VAR), serial, holder, block_inverse, (beta_active,))
    current = residual
    for pass_index in range(PASSES):
        update = sum_over_var(partial_update(exchange(pay, VAR), columns)) * inv_root
        if pass_index + 1 == PASSES:
            break
        data = descent(rank, update, current, columns, inv_root, copies)
        pay, *state, factor = owner(
            exchange(data, SAMP + VAR), serial, holder, block_inverse, state
        )
        current = current - factor[:, :1] * update

    _, coeffs, direction = state
    sums = jnp.concatenate([jnp.sum(current * update, 1), jnp.sum(update * update, 1)])
    sums = jnp.sum(to_all(sums[None], SAMP), (0, 1))
    phenos = residual.shape[0]
    factor = (sums[:phenos] / (sums[phenos:] + epsilon))[:, None]
    fit = serial.shape[1]
    both = lambda x: jnp.concatenate([x[:, :fit], x[:, fit:]], 0)
    return (scores, both(coeffs) + factor * both(direction), current - factor * update)


def solution(mesh):
    torus = Mesh(mesh.devices.reshape(2, 4, 2, 2, 4), VAR + SAMP)
    placed = (
        P(SAMP, VAR),
        P(SAMP, VAR),
        P(),
        P(None, SAMP),
        P(None, VAR),
        P(VAR, None, None),
        P(VAR),
        P(VAR),
    )
    return jax.shard_map(
        on_device,
        mesh=torus,
        in_specs=placed,
        out_specs=(P(None, VAR), P(None, VAR), P(None, SAMP)),
        check_vma=False,
    )
```

```python
import functools
import math

import jax
import jax.numpy as jnp
from jax import lax
from jax.experimental import pallas as pl
from jax.experimental.pallas import tpu as pltpu
from jax.sharding import Mesh
from jax.sharding import PartitionSpec as P

PASSES = 3
VAR = ("y_lo", "z", "core")
SAMP = ("y_hi", "x")
CHIPS = ("y_lo", "z")

CAP = 64
LANES = 128
ROWS = 256
HALF = 4

penalty = 0.5
epsilon = 1e-06
SMALL = pltpu.CompilerParams(vmem_limit_bytes=12 * 1024 * 1024)
MEDIUM = pltpu.CompilerParams(vmem_limit_bytes=46 * 1024 * 1024)
LARGE = pltpu.CompilerParams(vmem_limit_bytes=60 * 1024 * 1024)
f32 = jnp.float32
bf16 = jnp.bfloat16


def iota(shape, dim):
    return lax.broadcasted_iota(jnp.int32, shape, dim)


def dot(a, b, **kw):
    return jnp.dot(a, b, preferred_element_type=f32, **kw)


def dot_t(a, b, **kw):
    return lax.dot_general(a, b, (((1,), (1,)), ((), ())), preferred_element_type=f32, **kw)


def thirds(x):
    high = x.astype(bf16)
    rest = x - high.astype(f32)
    mid = rest.astype(bf16)
    return high, mid, (rest - mid.astype(f32)).astype(bf16)


def swapped(x):
    here = (iota(x.shape, 0) // HALF) == (iota(x.shape, 1) // CAP)
    return jnp.where(here, x, pltpu.roll(pltpu.roll(x, HALF, 0), CAP, 1))


def column_row(packed):
    low = iota((1, LANES), 1) < CAP
    return jnp.concatenate(
        [
            jnp.where(low, packed[t : t + 1], packed[t + 1 : t + 2])
            for t in range(0, packed.shape[0], 2)
        ],
        1,
    )


def slot_maps(serial, holder, holders):
    fit = serial.shape[1]
    serial2 = jnp.concatenate([serial, serial], 1)
    holder2 = jnp.concatenate([holder, holder], 1)
    shape = (2 * CAP, 2 * fit)
    rows, cols = iota(shape, 0), iota(shape, 1)
    spread = ((rows // CAP) == (cols // fit)) & ((rows % CAP) == serial2)
    mask = (iota((holders * HALF, 2 * fit), 0) // HALF) == holder2
    return spread.astype(f32).astype(bf16), mask.astype(f32)


def layout_kernel(
    width,
    place_ref,
    active_ref,
    admit_ref,
    holder_ref,
    serial_ref,
    packed_ref,
    rank_ref,
    core_ref,
    ids_ref,
):
    rank_ref[...] = jnp.full(rank_ref.shape, place_ref[0], jnp.int32)
    core_ref[...] = jnp.full(core_ref.shape, place_ref[1], jnp.int32)
    holders = packed_ref.shape[0]
    fit = holder_ref.shape[1]
    active = active_ref.shape[1]
    ids_ref[:, :active] = active_ref[...]
    ids_ref[:, active:] = admit_ref[...]
    ids = ids_ref[...]
    holder = ids // width
    holder_ref[...] = holder
    marks = (iota((holders, fit), 0) == holder).astype(f32)
    earlier = (iota((fit, fit), 0) < iota((fit, fit), 1)).astype(f32).astype(bf16)
    before = dot(marks.astype(bf16), earlier)
    serial = jnp.sum(before * marks, 0, keepdims=True).astype(jnp.int32)
    serial_ref[...] = serial
    spread, _ = slot_maps(serial, holder, holders)
    marks2 = jnp.concatenate([marks, marks], 1)
    column = ids - holder * width + 1
    parts = []
    for piece in (column // LANES, column % LANES):
        row = piece.astype(f32)
        row = jnp.concatenate([row, row], 1)
        parts.append(dot_t((marks2 * row).astype(bf16), spread))
    packed_ref[...] = (parts[0] * LANES + parts[1]).astype(jnp.int32)


def layout(place, active_ids, admit_ids, width, holders):
    row = jax.ShapeDtypeStruct((1, active_ids.size + admit_ids.size), jnp.int32)
    tile = jax.ShapeDtypeStruct((2 * HALF, LANES), jnp.int32)
    vmem = pl.BlockSpec(memory_space=pltpu.VMEM)
    return pl.pallas_call(
        functools.partial(layout_kernel, width),
        in_specs=[pl.BlockSpec(memory_space=pltpu.SMEM), vmem, vmem],
        out_shape=(row, row, jax.ShapeDtypeStruct((holders, LANES), jnp.int32), tile, tile),
        scratch_shapes=[pltpu.VMEM(row.shape, jnp.int32)],
        compiler_params=LARGE,
        name="layout",
    )(place, active_ids[None], admit_ids[None])


def look_up(table_ref, index_ref, scales_ref):
    index = index_ref[...]
    scales = jnp.full(index.shape, table_ref[0], f32)
    for level in range(1, table_ref.shape[0]):
        scales = jnp.where(index == level, table_ref[level], scales)
    scales_ref[...] = scales


def dequantized(geno_ref, scales_ref, step):
    rows = geno_ref.shape[0]
    group = 128
    out = []
    for g in range(rows // group):
        scale = scales_ref[pl.ds(step * (rows // group) + g, 1), :]
        wide = geno_ref[g * group : (g + 1) * group, :].astype(f32) * scale
        out.append(wide.astype(bf16))
    return jnp.concatenate(out, 0)


def screen_kernel(table_ref, geno_ref, index_ref, resid_ref, out_ref, scales_ref, acc_ref):
    step = pl.program_id(0)

    @pl.when(step == 0)
    def _():
        look_up(table_ref, index_ref, scales_ref)
        acc_ref[...] = jnp.zeros_like(acc_ref)

    acc_ref[...] += dot(resid_ref[...].astype(bf16), dequantized(geno_ref, scales_ref, step))

    @pl.when(step == pl.num_programs(0) - 1)
    def _():
        out_ref[...] = jnp.broadcast_to(acc_ref[...][None], out_ref.shape)


def screen(table, geno, index, resid, copies):
    samples, width = geno.shape
    phenos = resid.shape[0]
    return pl.pallas_call(
        screen_kernel,
        grid=(samples // ROWS,),
        in_specs=[
            pl.BlockSpec(memory_space=pltpu.SMEM),
            pl.BlockSpec((ROWS, width), lambda i: (i, 0)),
            pl.BlockSpec(index.shape, lambda i: (0, 0)),
            pl.BlockSpec((phenos, ROWS), lambda i: (0, i)),
        ],
        out_specs=pl.BlockSpec((copies, phenos, width), lambda i: (0, 0, 0)),
        out_shape=jax.ShapeDtypeStruct((copies, phenos, width), f32),
        scratch_shapes=[pltpu.VMEM(index.shape, f32), pltpu.VMEM((phenos, width), f32)],
        compiler_params=LARGE,
        cost_estimate=pl.CostEstimate(
            flops=2 * phenos * samples * width, bytes_accessed=2 * samples * width, transcendentals=0
        ),
        name="screen",
    )(table, geno, index, resid)


def select_kernel(table_ref, packed_ref, geno_ref, index_ref, out_ref, scales_ref, pick_ref):
    step = pl.program_id(0)

    @pl.when(step == 0)
    def _():
        look_up(table_ref, index_ref, scales_ref)
        wanted = column_row(packed_ref[...])

        @pl.loop(0, pick_ref.shape[0], step=ROWS)
        def _(at):
            here = iota((ROWS, pick_ref.shape[1]), 0) + (at + 1) == wanted
            pick_ref[pl.ds(pl.multiple_of(at, ROWS), ROWS), :] = here.astype(f32).astype(bf16)

    out_ref[...] = dot(dequantized(geno_ref, scales_ref, step), pick_ref[...]).astype(bf16)


def select(table, packed, geno, index):
    samples, width = geno.shape
    held = packed.shape[0] * CAP
    rows = 2 * ROWS
    return pl.pallas_call(
        select_kernel,
        grid=(samples // rows,),
        in_specs=[
            pl.BlockSpec(memory_space=pltpu.SMEM),
            pl.BlockSpec(packed.shape, lambda i: (0, 0)),
            pl.BlockSpec((rows, width), lambda i: (i, 0)),
            pl.BlockSpec(index.shape, lambda i: (0, 0)),
        ],
        out_specs=pl.BlockSpec((rows, held), lambda i: (i, 0)),
        out_shape=jax.ShapeDtypeStruct((samples, held), bf16),
        scratch_shapes=[pltpu.VMEM(index.shape, f32), pltpu.VMEM((width, held), bf16)],
        compiler_params=LARGE,
        cost_estimate=pl.CostEstimate(
            flops=2 * samples * width * held, bytes_accessed=2 * samples * width, transcendentals=0
        ),
        name="select",
    )(table, packed, geno, index)


def pick_kernel(inv_root, parts_ref, packed_hbm, scores_ref, pay_ref, packed_ref, sem):
    copy = pltpu.make_async_copy(packed_hbm, packed_ref, sem)
    copy.start()
    scores = parts_ref[0]
    for j in range(1, parts_ref.shape[0]):
        scores = scores + parts_ref[j]
    scores = scores * inv_root
    scores_ref[...] = scores
    copy.wait()
    wanted = column_row(packed_ref[...])
    stacked = jnp.concatenate(thirds(scores), 0)
    phenos, width = scores.shape
    total = jnp.zeros((stacked.shape[0], wanted.shape[1]), f32)
    for at in range(0, width, ROWS):
        here = iota((ROWS, wanted.shape[1]), 0) + (at + 1) == wanted
        total += dot(stacked[:, at : at + ROWS], here.astype(f32).astype(bf16))
    held = total[:phenos] + total[phenos : 2 * phenos] + total[2 * phenos :]
    for t in range(wanted.shape[1] // LANES):
        pay_ref[8 * t : 8 * t + 8, :] = swapped(held[:, t * LANES : (t + 1) * LANES])


def pick(parts, packed, inv_root):
    return pl.pallas_call(
        functools.partial(pick_kernel, inv_root),
        in_specs=[pl.BlockSpec(memory_space=pltpu.VMEM), pl.BlockSpec(memory_space=pltpu.HBM)],
        scratch_shapes=[pltpu.VMEM(packed.shape, packed.dtype), pltpu.SemaphoreType.DMA],
        out_shape=(
            jax.ShapeDtypeStruct(parts.shape[1:], f32),
            jax.ShapeDtypeStruct((packed.shape[0] * HALF, LANES), f32),
        ),
        compiler_params=SMALL,
        name="pick",
    )(parts, packed)


def direction_step(data, serial_ref, holder_ref, inverse_ref, advance, wide_ref, d_ref, pay_ref):
    fit = serial_ref.shape[1]
    holders = data.shape[0] // HALF
    spread, mask = slot_maps(serial_ref[...], holder_ref[...], holders)
    high, mid, low = thirds(data)
    placed = (dot(high, spread) + dot(mid, spread) + dot(low, spread)) * mask
    placed = jnp.sum(placed.reshape(-1, 2 * HALF, 2 * fit), 0)
    arrived = placed[:HALF] + placed[HALF:]
    inner = advance(arrived)
    wide_ref[:HALF, :] = inner[:, :fit]
    wide_ref[HALF:, :] = inner[:, fit:]
    blocks, size = inverse_ref.shape[0], inverse_ref.shape[1]
    for b in range(blocks):
        moved = dot_t(
            wide_ref[:, b * size : (b + 1) * size], inverse_ref[b], precision=lax.Precision.HIGHEST
        )
        moved = moved.astype(bf16).astype(f32)
        d_ref[:, b * size : (b + 1) * size] = moved[:HALF]
        d_ref[:, fit + b * size : fit + (b + 1) * size] = moved[HALF:]
    d = d_ref[...]
    d = jnp.concatenate([d, d], 0)
    d = jnp.broadcast_to(d[None], (holders * HALF // d.shape[0], *d.shape)).reshape(mask.shape)
    pay_ref[...] = dot_t((d * mask).astype(bf16), spread)


def first_owner_kernel(
    data_ref,
    serial_ref,
    holder_ref,
    inverse_ref,
    beta_ref,
    columns_hbm,
    pay_ref,
    g_ref,
    b_ref,
    d_ref,
    columns_ref,
    wide_ref,
    sem,
):
    copy = pltpu.make_async_copy(columns_hbm, columns_ref, sem)
    copy.start()
    fit = serial_ref.shape[1]
    active = beta_ref.shape[1]
    b_ref[...] = jnp.zeros_like(b_ref)
    b_ref[:, :active] = beta_ref[:HALF]
    b_ref[:, fit : fit + active] = beta_ref[HALF:]

    def advance(arrived):
        g_ref[...] = arrived
        return arrived - penalty * b_ref[...]

    direction_step(
        data_ref[...], serial_ref, holder_ref, inverse_ref, advance, wide_ref, d_ref, pay_ref
    )
    copy.wait()


def owner_kernel(
    data_ref,
    serial_ref,
    holder_ref,
    inverse_ref,
    g_in,
    b_in,
    d_in,
    resid_in,
    update_ref,
    pay_ref,
    g_ref,
    b_ref,
    d_ref,
    resid_ref,
    wide_ref,
    sum_ref,
    rows_ref,
    scalar_ref,
):
    fit = serial_ref.shape[1]
    chunk = sum_ref.shape[0]
    total = data_ref[:chunk, :]
    for at in range(chunk, data_ref.shape[0], chunk):
        total = total + data_ref[at : at + chunk, :]
    sum_ref[...] = total
    for k in range(chunk // (HALF + 1)):
        at = k * (HALF + 1)
        rows_ref[k * HALF : (k + 1) * HALF, :] = sum_ref[at : at + HALF, :]
        if k < scalar_ref.shape[0]:
            scalar_ref[k : k + 1, :] = sum_ref[at + HALF : at + HALF + 1, :]
    factor = scalar_ref[:, :1] / (scalar_ref[:, CAP : CAP + 1] + epsilon)
    resid_ref[...] = resid_in[...] - factor * update_ref[...]
    low = iota((HALF, 2 * fit), 1) < fit
    factor = jnp.where(low, factor[:HALF], factor[HALF:])

    def advance(arrived):
        g_ref[...] = g_in[...] - factor * arrived
        b_ref[...] = b_in[...] + factor * d_in[...]
        return g_ref[...] - penalty * b_ref[...]

    direction_step(
        rows_ref[...], serial_ref, holder_ref, inverse_ref, advance, wide_ref, d_ref, pay_ref
    )


def owner(data, serial, holder, inverse, state):
    fit = serial.shape[1]
    phenos = 2 * HALF
    held = jax.ShapeDtypeStruct((HALF, 2 * fit), f32)
    wide = pltpu.VMEM((phenos, fit), f32)
    if len(state) == 2:
        vmem = pl.BlockSpec(memory_space=pltpu.VMEM)
        columns = state[1]
        return pl.pallas_call(
            first_owner_kernel,
            in_specs=[vmem] * 5 + [pl.BlockSpec(memory_space=pltpu.HBM)],
            out_specs=(vmem,) * 5,
            out_shape=(
                jax.ShapeDtypeStruct(data.shape, f32),
                held,
                held,
                held,
                jax.ShapeDtypeStruct(columns.shape, columns.dtype),
            ),
            scratch_shapes=[wide, pltpu.SemaphoreType.DMA],
            compiler_params=MEDIUM,
            name="owner_first",
        )(data, serial, holder, inverse, *state)
    holders = lax.axis_size(VAR)
    return pl.pallas_call(
        owner_kernel,
        out_shape=(
            jax.ShapeDtypeStruct((holders * HALF, LANES), f32),
            held,
            held,
            held,
            jax.ShapeDtypeStruct(state[3].shape, f32),
        ),
        scratch_shapes=[
            wide,
            pltpu.VMEM((holders * (HALF + 1), LANES), f32),
            pltpu.VMEM((holders * HALF, LANES), f32),
            pltpu.VMEM((phenos, LANES), f32),
        ],
        compiler_params=SMALL,
        name="owner_next",
    )(data, serial, holder, inverse, *state)


def update_kernel(core_ref, pay_ref, columns_ref, keep_ref, send_ref):
    packed = jnp.concatenate(
        [swapped(pay_ref[at : at + 8, :]) for at in range(0, pay_ref.shape[0], 8)], 1
    ).astype(bf16)
    first = core_ref[:, :1] == 0
    half = keep_ref.shape[1]
    for at in range(0, half, ROWS):
        a = dot_t(packed, columns_ref[at : at + ROWS, :])
        b = dot_t(packed, columns_ref[half + at : half + at + ROWS, :])
        keep_ref[:, at : at + ROWS] = jnp.where(first, a, b)
        send_ref[:, at : at + ROWS] = jnp.where(first, b, a)


def partial_update(core, pay, columns):
    half = jax.ShapeDtypeStruct((2 * HALF, columns.shape[0] // 2), f32)
    return pl.pallas_call(
        update_kernel,
        out_shape=(half, half),
        compiler_params=SMALL,
        name="update",
    )(core, pay, columns)


def spread_kernel(keep_ref, arrived_ref, out_ref):
    out_ref[...] = jnp.broadcast_to((keep_ref[...] + arrived_ref[...])[None], out_ref.shape)


def spread(keep, arrived, copies):
    return pl.pallas_call(
        spread_kernel,
        out_shape=jax.ShapeDtypeStruct((copies, *keep.shape), f32),
        compiler_params=SMALL,
        name="spread",
    )(keep, arrived)


def total_kernel(parts_ref, out_ref):
    total = parts_ref[0]
    for n in range(1, parts_ref.shape[0]):
        total = total + parts_ref[n]
    out_ref[...] = total


def total(parts):
    return pl.pallas_call(
        total_kernel,
        out_shape=jax.ShapeDtypeStruct(parts.shape[1:], f32),
        compiler_params=SMALL,
        name="total",
    )(parts)


def whole_update(inv_root, core_ref, mine_ref, other_ref):
    first = core_ref[:, :1] == 0
    mine, other = mine_ref[...] * inv_root, other_ref[...] * inv_root
    return jnp.concatenate([jnp.where(first, mine, other), jnp.where(first, other, mine)], 1)


def step_sums(resid, update):
    cross = jnp.sum(resid * update, 1, keepdims=True)
    square = jnp.sum(update * update, 1, keepdims=True)
    return jnp.where(iota((update.shape[0], LANES), 1) < CAP, cross, square)


def descent_kernel(
    inv_root, rank_ref, core_ref, mine_ref, other_ref, resid_ref, columns_ref, out_ref, update_ref
):
    update = whole_update(inv_root, core_ref, mine_ref, other_ref)
    update_ref[...] = update
    phenos = update.shape[0]
    high = update.astype(bf16)
    low = (update - high.astype(f32)).astype(bf16)
    grad = dot(jnp.concatenate([high, low], 0), columns_ref[...])
    grad = (grad[:phenos] + grad[phenos:]) * inv_root
    both = step_sums(resid_ref[...], update)
    mine = iota(both.shape, 0) == lax.rem(rank_ref[...], phenos)
    row = jnp.sum(jnp.where(mine, both, 0.0), 0, keepdims=True)
    chunk = HALF + 1
    owners = grad.shape[1] // CAP
    copies = out_ref.shape[0] // (chunk * owners)
    for t in range(owners // 2):
        pair = swapped(grad[:, t * LANES : (t + 1) * LANES])
        for n in range(copies):
            at = (n * owners + 2 * t) * chunk
            out_ref[at : at + HALF, :] = pair[:HALF]
            out_ref[at + HALF : at + HALF + 1, :] = row
            out_ref[at + chunk : at + chunk + HALF, :] = pair[HALF:]
            out_ref[at + chunk + HALF : at + 2 * chunk, :] = row


def descent(rank, core, mine, other, resid, columns, inv_root, copies):
    out = (copies * (columns.shape[1] // CAP) * (HALF + 1), LANES)
    return pl.pallas_call(
        functools.partial(descent_kernel, inv_root),
        out_shape=(jax.ShapeDtypeStruct(out, f32), jax.ShapeDtypeStruct(resid.shape, f32)),
        compiler_params=SMALL,
        name="descent",
    )(rank, core, mine, other, resid, columns)


def settle_kernel(inv_root, core_ref, mine_ref, other_ref, resid_ref, sums_ref, update_ref):
    update = whole_update(inv_root, core_ref, mine_ref, other_ref)
    update_ref[...] = update
    sums_ref[...] = jnp.broadcast_to(step_sums(resid_ref[...], update)[None], sums_ref.shape)


def settle(core, mine, other, resid, inv_root, copies):
    return pl.pallas_call(
        functools.partial(settle_kernel, inv_root),
        out_shape=(
            jax.ShapeDtypeStruct((copies, resid.shape[0], LANES), f32),
            jax.ShapeDtypeStruct(resid.shape, f32),
        ),
        compiler_params=SMALL,
        name="settle",
    )(core, mine, other, resid)


def last_kernel(sums_ref, b_ref, d_ref, resid_ref, update_ref, coeffs_ref, out_ref):
    phenos, fit = coeffs_ref.shape
    total = sums_ref[0]
    for j in range(1, sums_ref.shape[0]):
        total = total + sums_ref[j]
    factor = total[:, :1] / (total[:, CAP : CAP + 1] + epsilon)
    for half in range(2):
        rows = slice(half * HALF, (half + 1) * HALF)
        cols = slice(half * fit, (half + 1) * fit)
        coeffs_ref[rows, :] = b_ref[:, cols] + factor[rows] * d_ref[:, cols]
    out_ref[...] = resid_ref[...] - factor * update_ref[...]


def last(sums, coeffs, direction, resid, update):
    phenos = resid.shape[0]
    return pl.pallas_call(
        last_kernel,
        out_shape=(
            jax.ShapeDtypeStruct((phenos, coeffs.shape[1] // 2), f32),
            jax.ShapeDtypeStruct(resid.shape, f32),
        ),
        compiler_params=SMALL,
        name="last",
    )(sums, coeffs, direction, resid, update)


def exchange(pay, axes):
    count = lax.axis_size(axes)
    rows = pay.shape[0] // count
    shape = (count, rows, LANES) if rows == HALF else (count, 1, rows * LANES)
    return lax.all_to_all(
        pay.reshape(shape), axes, split_axis=0, concat_axis=0, tiled=True
    ).reshape(pay.shape)


def other_core(x):
    return lax.ppermute(x, "core", [(0, 1), (1, 0)])


def on_device(
    geno, scale_index, scale_table, residual, beta_active, block_inverse, active_ids, admit_ids
):
    holders = lax.axis_size(VAR)
    place = jnp.stack([lax.axis_index(VAR), lax.axis_index("core")]).astype(jnp.int32)
    samples, width = geno.shape
    copies = lax.axis_size(SAMP)
    inv_root = 1.0 / math.sqrt(samples * copies)

    holder, serial, packed, rank, core = layout(place, active_ids, admit_ids, width, holders)
    packed = lax.all_to_all(
        packed.reshape(holders, 1, LANES), VAR, split_axis=0, concat_axis=0, tiled=True
    ).reshape(holders, LANES)

    parts = screen(scale_table, geno, scale_index, residual, copies)
    parts = lax.all_to_all(parts, SAMP, split_axis=0, concat_axis=0, tiled=True)
    columns = select(scale_table, packed, geno, scale_index)
    parts, columns = lax.optimization_barrier((parts, columns))
    scores, pay = pick(parts, packed, inv_root)

    pay, *state, columns = owner(
        exchange(pay, VAR), serial, holder, block_inverse, (beta_active, columns)
    )
    current = residual
    for pass_index in range(PASSES):
        keep, send = partial_update(core, exchange(pay, VAR), columns)
        mine = spread(keep, other_core(send), lax.axis_size(CHIPS))
        mine = total(lax.all_to_all(mine, CHIPS, split_axis=0, concat_axis=0, tiled=True))
        other = other_core(mine)
        if pass_index + 1 == PASSES:
            break
        data, update = descent(rank, core, mine, other, current, columns, inv_root, copies)
        pay, *state, current = owner(
            exchange(data, SAMP + VAR), serial, holder, block_inverse, (*state, current, update)
        )

    _, coeffs, direction = state
    sums, update = settle(core, mine, other, current, inv_root, copies)
    sums = lax.all_to_all(sums, SAMP, split_axis=0, concat_axis=0, tiled=True)
    return (scores, *last(sums, coeffs, direction, current, update))


def solution(mesh):
    torus = Mesh(mesh.devices.reshape(2, 4, 2, 2, 4), VAR + SAMP)
    placed = (
        P(SAMP, VAR),
        P(SAMP, VAR),
        P(),
        P(None, SAMP),
        P(None, VAR),
        P(VAR, None, None),
        P(VAR),
        P(VAR),
    )
    return jax.shard_map(
        on_device,
        mesh=torus,
        in_specs=placed,
        out_specs=(P(None, VAR), P(None, VAR), P(None, SAMP)),
        check_vma=False,
    )
```

```python
import functools
import math

import jax
import jax.numpy as jnp
from jax import lax
from jax.experimental import pallas as pl
from jax.experimental.pallas import tpu as pltpu
from jax.sharding import Mesh
from jax.sharding import PartitionSpec as P

PASSES = 3
VAR = ("y_lo", "z", "core")
SAMP = ("y_hi", "x")
CHIPS = ("y_lo", "z")

CAP = 64
LANES = 128
ROWS = 256
HALF = 4

penalty = 0.5
epsilon = 1e-06
SMALL = pltpu.CompilerParams(vmem_limit_bytes=12 * 1024 * 1024)
MEDIUM = pltpu.CompilerParams(vmem_limit_bytes=46 * 1024 * 1024)
LARGE = pltpu.CompilerParams(vmem_limit_bytes=60 * 1024 * 1024)
f32 = jnp.float32
bf16 = jnp.bfloat16


def iota(shape, dim):
    return lax.broadcasted_iota(jnp.int32, shape, dim)


def dot(a, b, **kw):
    return jnp.dot(a, b, preferred_element_type=f32, **kw)


def dot_t(a, b, **kw):
    return lax.dot_general(a, b, (((1,), (1,)), ((), ())), preferred_element_type=f32, **kw)


def thirds(x):
    high = x.astype(bf16)
    rest = x - high.astype(f32)
    mid = rest.astype(bf16)
    return high, mid, (rest - mid.astype(f32)).astype(bf16)


def swapped(x):
    here = (iota(x.shape, 0) // HALF) == (iota(x.shape, 1) // CAP)
    return jnp.where(here, x, pltpu.roll(pltpu.roll(x, HALF, 0), CAP, 1))


def column_row(packed):
    low = iota((1, LANES), 1) < CAP
    return jnp.concatenate(
        [
            jnp.where(low, packed[t : t + 1], packed[t + 1 : t + 2])
            for t in range(0, packed.shape[0], 2)
        ],
        1,
    )


def slot_maps(serial, holder, holders):
    fit = serial.shape[1]
    serial2 = jnp.concatenate([serial, serial], 1)
    holder2 = jnp.concatenate([holder, holder], 1)
    shape = (2 * CAP, 2 * fit)
    rows, cols = iota(shape, 0), iota(shape, 1)
    spread = ((rows // CAP) == (cols // fit)) & ((rows % CAP) == serial2)
    mask = (iota((holders * HALF, 2 * fit), 0) // HALF) == holder2
    return spread.astype(f32).astype(bf16), mask.astype(f32)


def layout_kernel(
    width,
    active_ref,
    admit_ref,
    holder_ref,
    serial_ref,
    packed_ref,
    rank_ref,
    core_ref,
    ids_ref,
):
    rank_ref[...] = jnp.full(rank_ref.shape, lax.axis_index(VAR), jnp.int32)
    core_ref[...] = jnp.full(core_ref.shape, lax.axis_index("core"), jnp.int32)
    holders = packed_ref.shape[0]
    fit = holder_ref.shape[1]
    active = active_ref.shape[1]
    ids_ref[:, :active] = active_ref[...]
    ids_ref[:, active:] = admit_ref[...]
    ids = ids_ref[...]
    holder = ids // width
    holder_ref[...] = holder
    marks = (iota((holders, fit), 0) == holder).astype(f32)
    earlier = (iota((fit, fit), 0) < iota((fit, fit), 1)).astype(f32).astype(bf16)
    before = dot(marks.astype(bf16), earlier)
    serial = jnp.sum(before * marks, 0, keepdims=True).astype(jnp.int32)
    serial_ref[...] = serial
    spread, _ = slot_maps(serial, holder, holders)
    marks2 = jnp.concatenate([marks, marks], 1)
    column = ids - holder * width + 1
    parts = []
    for piece in (column // LANES, column % LANES):
        row = piece.astype(f32)
        row = jnp.concatenate([row, row], 1)
        parts.append(dot_t((marks2 * row).astype(bf16), spread))
    packed_ref[...] = (parts[0] * LANES + parts[1]).astype(jnp.int32)


def layout(active_ids, admit_ids, width, holders):
    row = jax.ShapeDtypeStruct((1, active_ids.size + admit_ids.size), jnp.int32)
    tile = jax.ShapeDtypeStruct((2 * HALF, LANES), jnp.int32)
    vmem = pl.BlockSpec(memory_space=pltpu.VMEM)
    return pl.pallas_call(
        functools.partial(layout_kernel, width),
        in_specs=[vmem, vmem],
        out_shape=(row, row, jax.ShapeDtypeStruct((holders, LANES), jnp.int32), tile, tile),
        scratch_shapes=[pltpu.VMEM(row.shape, jnp.int32)],
        compiler_params=LARGE,
        name="layout",
    )(active_ids[None], admit_ids[None])


def look_up(table_ref, index_ref, scales_ref):
    index = index_ref[...]
    scales = jnp.full(index.shape, table_ref[0], f32)
    for level in range(1, table_ref.shape[0]):
        scales = jnp.where(index == level, table_ref[level], scales)
    scales_ref[...] = scales


def dequantized(geno_ref, scales_ref, step):
    rows = geno_ref.shape[0]
    group = 128
    out = []
    for g in range(rows // group):
        scale = scales_ref[pl.ds(step * (rows // group) + g, 1), :]
        wide = geno_ref[g * group : (g + 1) * group, :].astype(f32) * scale
        out.append(wide.astype(bf16))
    return jnp.concatenate(out, 0)


def screen_kernel(table_ref, geno_ref, index_ref, resid_ref, out_ref, x_ref, scales_ref, acc_ref):
    step = pl.program_id(0)

    @pl.when(step == 0)
    def _():
        look_up(table_ref, index_ref, scales_ref)
        acc_ref[...] = jnp.zeros_like(acc_ref)

    x = dequantized(geno_ref, scales_ref, step)
    x_ref[...] = x
    acc_ref[...] += dot(resid_ref[...].astype(bf16), x)

    @pl.when(step == pl.num_programs(0) - 1)
    def _():
        out_ref[...] = acc_ref[...]


def screen(table, geno, index, resid):
    samples, width = geno.shape
    phenos = resid.shape[0]
    return pl.pallas_call(
        screen_kernel,
        grid=(samples // ROWS,),
        in_specs=[
            pl.BlockSpec(memory_space=pltpu.SMEM),
            pl.BlockSpec((ROWS, width), lambda i: (i, 0)),
            pl.BlockSpec(index.shape, lambda i: (0, 0)),
            pl.BlockSpec((phenos, ROWS), lambda i: (0, i)),
        ],
        out_specs=(
            pl.BlockSpec((phenos, width), lambda i: (0, 0)),
            pl.BlockSpec((ROWS, width), lambda i: (i, 0)),
        ),
        out_shape=(
            jax.ShapeDtypeStruct((phenos, width), f32),
            jax.ShapeDtypeStruct((samples, width), bf16),
        ),
        scratch_shapes=[pltpu.VMEM(index.shape, f32), pltpu.VMEM((phenos, width), f32)],
        compiler_params=LARGE,
        cost_estimate=pl.CostEstimate(
            flops=2 * phenos * samples * width, bytes_accessed=2 * samples * width, transcendentals=0
        ),
        name="screen",
    )(table, geno, index, resid)


def select_kernel(packed_ref, x_ref, out_ref, pick_ref):
    @pl.when(pl.program_id(0) == 0)
    def _():
        wanted = column_row(packed_ref[...])

        @pl.loop(0, pick_ref.shape[0], step=ROWS)
        def _(at):
            here = iota((ROWS, pick_ref.shape[1]), 0) + (at + 1) == wanted
            pick_ref[pl.ds(pl.multiple_of(at, ROWS), ROWS), :] = here.astype(f32).astype(bf16)

    out_ref[...] = dot(x_ref[...], pick_ref[...]).astype(bf16)


def select(packed, x):
    samples, width = x.shape
    held = packed.shape[0] * CAP
    rows = 2 * ROWS
    return pl.pallas_call(
        select_kernel,
        grid=(samples // rows,),
        in_specs=[
            pl.BlockSpec(packed.shape, lambda i: (0, 0)),
            pl.BlockSpec((rows, width), lambda i: (i, 0)),
        ],
        out_specs=pl.BlockSpec((rows, held), lambda i: (i, 0)),
        out_shape=jax.ShapeDtypeStruct((samples, held), bf16),
        scratch_shapes=[pltpu.VMEM((width, held), bf16)],
        compiler_params=LARGE,
        cost_estimate=pl.CostEstimate(
            flops=2 * samples * width * held, bytes_accessed=2 * samples * width, transcendentals=0
        ),
        name="select",
    )(packed, x)


def pick_kernel(
    inv_root, own_ref, one_ref, two_ref, three_ref, packed_hbm, scores_ref, pay_ref, packed_ref, sem
):
    copy = pltpu.make_async_copy(packed_hbm, packed_ref, sem)
    copy.start()
    scores = ((own_ref[...] + two_ref[...]) + (one_ref[...] + three_ref[...])) * inv_root
    scores_ref[...] = scores
    copy.wait()
    wanted = column_row(packed_ref[...])
    stacked = jnp.concatenate(thirds(scores), 0)
    phenos, width = scores.shape
    total = jnp.zeros((stacked.shape[0], wanted.shape[1]), f32)
    for at in range(0, width, ROWS):
        here = iota((ROWS, wanted.shape[1]), 0) + (at + 1) == wanted
        total += dot(stacked[:, at : at + ROWS], here.astype(f32).astype(bf16))
    held = total[:phenos] + total[phenos : 2 * phenos] + total[2 * phenos :]
    for t in range(wanted.shape[1] // LANES):
        pay_ref[8 * t : 8 * t + 8, :] = swapped(held[:, t * LANES : (t + 1) * LANES])


def pick(parts, packed, inv_root):
    return pl.pallas_call(
        functools.partial(pick_kernel, inv_root),
        in_specs=[pl.BlockSpec(memory_space=pltpu.VMEM)] * 4
        + [pl.BlockSpec(memory_space=pltpu.HBM)],
        scratch_shapes=[pltpu.VMEM(packed.shape, packed.dtype), pltpu.SemaphoreType.DMA],
        out_shape=(
            jax.ShapeDtypeStruct(parts[0].shape, f32),
            jax.ShapeDtypeStruct((packed.shape[0] * HALF, LANES), f32),
        ),
        compiler_params=SMALL,
        name="pick",
    )(*parts, packed)


def direction_step(data, serial_ref, holder_ref, inverse_ref, advance, wide_ref, d_ref, pay_ref):
    fit = serial_ref.shape[1]
    holders = data.shape[0] // HALF
    spread, mask = slot_maps(serial_ref[...], holder_ref[...], holders)
    high, mid, low = thirds(data)
    placed = (dot(high, spread) + dot(mid, spread) + dot(low, spread)) * mask
    placed = jnp.sum(placed.reshape(-1, 2 * HALF, 2 * fit), 0)
    arrived = placed[:HALF] + placed[HALF:]
    inner = advance(arrived)
    wide_ref[:HALF, :] = inner[:, :fit]
    wide_ref[HALF:, :] = inner[:, fit:]
    blocks, size = inverse_ref.shape[0], inverse_ref.shape[1]
    for b in range(blocks):
        moved = dot_t(
            wide_ref[:, b * size : (b + 1) * size], inverse_ref[b], precision=lax.Precision.HIGHEST
        )
        moved = moved.astype(bf16).astype(f32)
        d_ref[:, b * size : (b + 1) * size] = moved[:HALF]
        d_ref[:, fit + b * size : fit + (b + 1) * size] = moved[HALF:]
    d = d_ref[...]
    d = jnp.concatenate([d, d], 0)
    d = jnp.broadcast_to(d[None], (holders * HALF // d.shape[0], *d.shape)).reshape(mask.shape)
    pay_ref[...] = dot_t((d * mask).astype(bf16), spread)


def first_owner_kernel(
    data_ref,
    serial_ref,
    holder_ref,
    inverse_ref,
    beta_ref,
    columns_hbm,
    pay_ref,
    g_ref,
    b_ref,
    d_ref,
    columns_ref,
    wide_ref,
    sem,
):
    copy = pltpu.make_async_copy(columns_hbm, columns_ref, sem)
    copy.start()
    fit = serial_ref.shape[1]
    active = beta_ref.shape[1]
    b_ref[...] = jnp.zeros_like(b_ref)
    b_ref[:, :active] = beta_ref[:HALF]
    b_ref[:, fit : fit + active] = beta_ref[HALF:]

    def advance(arrived):
        g_ref[...] = arrived
        return arrived - penalty * b_ref[...]

    direction_step(
        data_ref[...], serial_ref, holder_ref, inverse_ref, advance, wide_ref, d_ref, pay_ref
    )
    copy.wait()


def owner_kernel(
    data_ref,
    serial_ref,
    holder_ref,
    inverse_ref,
    g_in,
    b_in,
    d_in,
    resid_in,
    update_ref,
    pay_ref,
    g_ref,
    b_ref,
    d_ref,
    resid_ref,
    wide_ref,
    sum_ref,
    rows_ref,
    scalar_ref,
):
    fit = serial_ref.shape[1]
    chunk = sum_ref.shape[0]
    total = data_ref[:chunk, :]
    for at in range(chunk, data_ref.shape[0], chunk):
        total = total + data_ref[at : at + chunk, :]
    sum_ref[...] = total
    for k in range(chunk // (HALF + 1)):
        at = k * (HALF + 1)
        rows_ref[k * HALF : (k + 1) * HALF, :] = sum_ref[at : at + HALF, :]
        if k < scalar_ref.shape[0]:
            scalar_ref[k : k + 1, :] = sum_ref[at + HALF : at + HALF + 1, :]
    factor = scalar_ref[:, :1] / (scalar_ref[:, CAP : CAP + 1] + epsilon)
    resid_ref[...] = resid_in[...] - factor * update_ref[...]
    low = iota((HALF, 2 * fit), 1) < fit
    factor = jnp.where(low, factor[:HALF], factor[HALF:])

    def advance(arrived):
        g_ref[...] = g_in[...] - factor * arrived
        b_ref[...] = b_in[...] + factor * d_in[...]
        return g_ref[...] - penalty * b_ref[...]

    direction_step(
        rows_ref[...], serial_ref, holder_ref, inverse_ref, advance, wide_ref, d_ref, pay_ref
    )


def owner(data, serial, holder, inverse, state):
    fit = serial.shape[1]
    phenos = 2 * HALF
    held = jax.ShapeDtypeStruct((HALF, 2 * fit), f32)
    wide = pltpu.VMEM((phenos, fit), f32)
    if len(state) == 2:
        vmem = pl.BlockSpec(memory_space=pltpu.VMEM)
        columns = state[1]
        return pl.pallas_call(
            first_owner_kernel,
            in_specs=[vmem] * 5 + [pl.BlockSpec(memory_space=pltpu.HBM)],
            out_specs=(vmem,) * 5,
            out_shape=(
                jax.ShapeDtypeStruct(data.shape, f32),
                held,
                held,
                held,
                jax.ShapeDtypeStruct(columns.shape, columns.dtype),
            ),
            scratch_shapes=[wide, pltpu.SemaphoreType.DMA],
            compiler_params=MEDIUM,
            name="owner_first",
        )(data, serial, holder, inverse, *state)
    holders = lax.axis_size(VAR)
    return pl.pallas_call(
        owner_kernel,
        out_shape=(
            jax.ShapeDtypeStruct((holders * HALF, LANES), f32),
            held,
            held,
            held,
            jax.ShapeDtypeStruct(state[3].shape, f32),
        ),
        scratch_shapes=[
            wide,
            pltpu.VMEM((holders * (HALF + 1), LANES), f32),
            pltpu.VMEM((holders * HALF, LANES), f32),
            pltpu.VMEM((phenos, LANES), f32),
        ],
        compiler_params=SMALL,
        name="owner_next",
    )(data, serial, holder, inverse, *state)


def update_kernel(core_ref, pay_ref, columns_ref, keep_ref, send_ref):
    packed = jnp.concatenate(
        [swapped(pay_ref[at : at + 8, :]) for at in range(0, pay_ref.shape[0], 8)], 1
    ).astype(bf16)
    first = core_ref[:, :1] == 0
    half = keep_ref.shape[1]
    for at in range(0, half, ROWS):
        a = dot_t(packed, columns_ref[at : at + ROWS, :])
        b = dot_t(packed, columns_ref[half + at : half + at + ROWS, :])
        keep_ref[:, at : at + ROWS] = jnp.where(first, a, b)
        send_ref[:, at : at + ROWS] = jnp.where(first, b, a)


def partial_update(core, pay, columns):
    half = jax.ShapeDtypeStruct((2 * HALF, columns.shape[0] // 2), f32)
    return pl.pallas_call(
        update_kernel,
        out_shape=(half, half),
        compiler_params=SMALL,
        name="update",
    )(core, pay, columns)


def spread_kernel(keep_ref, arrived_ref, out_ref):
    out_ref[...] = jnp.broadcast_to((keep_ref[...] + arrived_ref[...])[None], out_ref.shape)


def spread(keep, arrived, copies):
    return pl.pallas_call(
        spread_kernel,
        out_shape=jax.ShapeDtypeStruct((copies, *keep.shape), f32),
        compiler_params=SMALL,
        name="spread",
    )(keep, arrived)


def total_kernel(parts_ref, out_ref):
    total = parts_ref[0]
    for n in range(1, parts_ref.shape[0]):
        total = total + parts_ref[n]
    out_ref[...] = total


def total(parts):
    return pl.pallas_call(
        total_kernel,
        out_shape=jax.ShapeDtypeStruct(parts.shape[1:], f32),
        compiler_params=SMALL,
        name="total",
    )(parts)


def whole_update(inv_root, core_ref, mine_ref, other_ref):
    first = core_ref[:, :1] == 0
    mine, other = mine_ref[...] * inv_root, other_ref[...] * inv_root
    return jnp.concatenate([jnp.where(first, mine, other), jnp.where(first, other, mine)], 1)


def step_sums(resid, update):
    cross = jnp.sum(resid * update, 1, keepdims=True)
    square = jnp.sum(update * update, 1, keepdims=True)
    return jnp.where(iota((update.shape[0], LANES), 1) < CAP, cross, square)


def descent_kernel(
    inv_root, rank_ref, core_ref, mine_ref, other_ref, resid_ref, columns_ref, out_ref, update_ref
):
    update = whole_update(inv_root, core_ref, mine_ref, other_ref)
    update_ref[...] = update
    phenos = update.shape[0]
    high = update.astype(bf16)
    low = (update - high.astype(f32)).astype(bf16)
    grad = dot(jnp.concatenate([high, low], 0), columns_ref[...])
    grad = (grad[:phenos] + grad[phenos:]) * inv_root
    both = step_sums(resid_ref[...], update)
    mine = iota(both.shape, 0) == lax.rem(rank_ref[...], phenos)
    row = jnp.sum(jnp.where(mine, both, 0.0), 0, keepdims=True)
    chunk = HALF + 1
    owners = grad.shape[1] // CAP
    copies = out_ref.shape[0] // (chunk * owners)
    for t in range(owners // 2):
        pair = swapped(grad[:, t * LANES : (t + 1) * LANES])
        for n in range(copies):
            at = (n * owners + 2 * t) * chunk
            out_ref[at : at + HALF, :] = pair[:HALF]
            out_ref[at + HALF : at + HALF + 1, :] = row
            out_ref[at + chunk : at + chunk + HALF, :] = pair[HALF:]
            out_ref[at + chunk + HALF : at + 2 * chunk, :] = row


def descent(rank, core, mine, other, resid, columns, inv_root, copies):
    out = (copies * (columns.shape[1] // CAP) * (HALF + 1), LANES)
    return pl.pallas_call(
        functools.partial(descent_kernel, inv_root),
        out_shape=(jax.ShapeDtypeStruct(out, f32), jax.ShapeDtypeStruct(resid.shape, f32)),
        compiler_params=SMALL,
        name="descent",
    )(rank, core, mine, other, resid, columns)


def settle_kernel(inv_root, core_ref, mine_ref, other_ref, resid_ref, sums_ref, update_ref):
    update = whole_update(inv_root, core_ref, mine_ref, other_ref)
    update_ref[...] = update
    sums_ref[...] = jnp.broadcast_to(step_sums(resid_ref[...], update)[None], sums_ref.shape)


def settle(core, mine, other, resid, inv_root, copies):
    return pl.pallas_call(
        functools.partial(settle_kernel, inv_root),
        out_shape=(
            jax.ShapeDtypeStruct((copies, resid.shape[0], LANES), f32),
            jax.ShapeDtypeStruct(resid.shape, f32),
        ),
        compiler_params=SMALL,
        name="settle",
    )(core, mine, other, resid)


def last_kernel(sums_ref, b_ref, d_ref, resid_ref, update_ref, coeffs_ref, out_ref):
    phenos, fit = coeffs_ref.shape
    total = sums_ref[0]
    for j in range(1, sums_ref.shape[0]):
        total = total + sums_ref[j]
    factor = total[:, :1] / (total[:, CAP : CAP + 1] + epsilon)
    for half in range(2):
        rows = slice(half * HALF, (half + 1) * HALF)
        cols = slice(half * fit, (half + 1) * fit)
        coeffs_ref[rows, :] = b_ref[:, cols] + factor[rows] * d_ref[:, cols]
    out_ref[...] = resid_ref[...] - factor * update_ref[...]


def last(sums, coeffs, direction, resid, update):
    phenos = resid.shape[0]
    return pl.pallas_call(
        last_kernel,
        out_shape=(
            jax.ShapeDtypeStruct((phenos, coeffs.shape[1] // 2), f32),
            jax.ShapeDtypeStruct(resid.shape, f32),
        ),
        compiler_params=SMALL,
        name="last",
    )(sums, coeffs, direction, resid, update)


def exchange(pay, axes):
    count = lax.axis_size(axes)
    rows = pay.shape[0] // count
    shape = (count, rows, LANES) if rows == HALF else (count, 1, rows * LANES)
    return lax.all_to_all(
        pay.reshape(shape), axes, split_axis=0, concat_axis=0, tiled=True
    ).reshape(pay.shape)


def shifted(x, axis, by=1):
    size = lax.axis_size(axis)
    return lax.ppermute(x, axis, [(i, (i + by) % size) for i in range(size)])


def on_device(
    geno, scale_index, scale_table, residual, beta_active, block_inverse, active_ids, admit_ids
):
    holders = lax.axis_size(VAR)
    samples, width = geno.shape
    copies = lax.axis_size(SAMP)
    inv_root = 1.0 / math.sqrt(samples * copies)

    part, x = screen(scale_table, geno, scale_index, residual)
    part, active_ids = lax.optimization_barrier((part, active_ids))
    part = part + shifted(part, "y_hi")
    parts = [part] + [shifted(part, "x", n) for n in range(1, lax.axis_size("x"))]

    holder, serial, packed, rank, core = layout(active_ids, admit_ids, width, holders)
    packed = lax.all_to_all(
        packed.reshape(holders, 1, LANES), VAR, split_axis=0, concat_axis=0, tiled=True
    ).reshape(holders, LANES)

    columns = select(packed, x)
    parts, columns = lax.optimization_barrier((parts, columns))
    scores, pay = pick(parts, packed, inv_root)
    pay, *state, columns = owner(
        exchange(pay, VAR), serial, holder, block_inverse, (beta_active, columns)
    )
    current = residual
    for pass_index in range(PASSES):
        keep, send = partial_update(core, exchange(pay, VAR), columns)
        mine = spread(keep, shifted(send, "core"), lax.axis_size(CHIPS))
        mine = total(lax.all_to_all(mine, CHIPS, split_axis=0, concat_axis=0, tiled=True))
        other = shifted(mine, "core")
        if pass_index + 1 == PASSES:
            break
        data, update = descent(rank, core, mine, other, current, columns, inv_root, copies)
        pay, *state, current = owner(
            exchange(data, SAMP + VAR), serial, holder, block_inverse, (*state, current, update)
        )

    _, coeffs, direction = state
    sums, update = settle(core, mine, other, current, inv_root, copies)
    sums = lax.all_to_all(sums, SAMP, split_axis=0, concat_axis=0, tiled=True)
    return (scores, *last(sums, coeffs, direction, current, update))


def solution(mesh):
    torus = Mesh(mesh.devices.reshape(2, 4, 2, 2, 4), VAR + SAMP)
    placed = (
        P(SAMP, VAR),
        P(SAMP, VAR),
        P(),
        P(None, SAMP),
        P(None, VAR),
        P(VAR, None, None),
        P(VAR),
        P(VAR),
    )
    return jax.shard_map(
        on_device,
        mesh=torus,
        in_specs=placed,
        out_specs=(P(None, VAR), P(None, VAR), P(None, SAMP)),
        check_vma=False,
    )
```

```python
import functools
import math

import jax
import jax.numpy as jnp
from jax import lax
from jax.experimental import pallas as pl
from jax.experimental.pallas import tpu as pltpu
from jax.sharding import Mesh
from jax.sharding import PartitionSpec as P

PASSES = 3
VAR = ("y_lo", "z", "core")
SAMP = ("y_hi", "x")
CHIPS = ("y_lo", "z")

CAP = 64
LANES = 128
ROWS = 256
HALF = 4

penalty = 0.5
epsilon = 1e-06
SMALL = pltpu.CompilerParams(vmem_limit_bytes=12 * 1024 * 1024)
MEDIUM = pltpu.CompilerParams(vmem_limit_bytes=50 * 1024 * 1024)
LARGE = pltpu.CompilerParams(vmem_limit_bytes=60 * 1024 * 1024)
f32 = jnp.float32
bf16 = jnp.bfloat16


def iota(shape, dim):
    return lax.broadcasted_iota(jnp.int32, shape, dim)


def dot(a, b, **kw):
    return jnp.dot(a, b, preferred_element_type=f32, **kw)


def dot_t(a, b, **kw):
    return lax.dot_general(a, b, (((1,), (1,)), ((), ())), preferred_element_type=f32, **kw)


def thirds(x):
    high = x.astype(bf16)
    rest = x - high.astype(f32)
    mid = rest.astype(bf16)
    return high, mid, (rest - mid.astype(f32)).astype(bf16)


def swapped(x):
    here = (iota(x.shape, 0) // HALF) == (iota(x.shape, 1) // CAP)
    return jnp.where(here, x, pltpu.roll(pltpu.roll(x, HALF, 0), CAP, 1))


def column_row(packed):
    low = iota((1, LANES), 1) < CAP
    return jnp.concatenate(
        [
            jnp.where(low, packed[t : t + 1], packed[t + 1 : t + 2])
            for t in range(0, packed.shape[0], 2)
        ],
        1,
    )


def slot_maps(serial, holder, holders):
    fit = serial.shape[1]
    serial2 = jnp.concatenate([serial, serial], 1)
    holder2 = jnp.concatenate([holder, holder], 1)
    shape = (2 * CAP, 2 * fit)
    rows, cols = iota(shape, 0), iota(shape, 1)
    spread = ((rows // CAP) == (cols // fit)) & ((rows % CAP) == serial2)
    mask = (iota((holders * HALF, 2 * fit), 0) // HALF) == holder2
    return spread.astype(f32).astype(bf16), mask.astype(f32)


def lay_out(width, active_ref, admit_ref, holder_ref, serial_ref, packed_ref, ids_ref):
    holders = packed_ref.shape[0]
    fit = holder_ref.shape[1]
    active = active_ref.shape[1]
    ids_ref[:, :active] = active_ref[...]
    ids_ref[:, active:] = admit_ref[...]
    ids = ids_ref[...]
    holder = ids // width
    holder_ref[...] = holder
    marks = (iota((holders, fit), 0) == holder).astype(f32)
    earlier = (iota((fit, fit), 0) < iota((fit, fit), 1)).astype(f32).astype(bf16)
    before = dot(marks.astype(bf16), earlier)
    serial = jnp.sum(before * marks, 0, keepdims=True).astype(jnp.int32)
    serial_ref[...] = serial
    spread, _ = slot_maps(serial, holder, holders)
    marks2 = jnp.concatenate([marks, marks], 1)
    column = ids - holder * width + 1
    parts = []
    for piece in (column // LANES, column % LANES):
        row = piece.astype(f32)
        row = jnp.concatenate([row, row], 1)
        parts.append(dot_t((marks2 * row).astype(bf16), spread))
    packed_ref[...] = (parts[0] * LANES + parts[1]).astype(jnp.int32)


def look_up(table_ref, index_ref, scales_ref):
    index = index_ref[...]
    scales = jnp.full(index.shape, table_ref[0], f32)
    for level in range(1, table_ref.shape[0]):
        scales = jnp.where(index == level, table_ref[level], scales)
    scales_ref[...] = scales


def dequantized(geno_ref, scales_ref, step):
    rows = geno_ref.shape[0]
    group = 128
    out = []
    for g in range(rows // group):
        scale = scales_ref[pl.ds(step * (rows // group) + g, 1), :]
        wide = geno_ref[g * group : (g + 1) * group, :].astype(f32) * scale
        out.append(wide.astype(bf16))
    return jnp.concatenate(out, 0)


def screen_kernel(
    table_ref,
    geno_ref,
    index_ref,
    resid_ref,
    active_ref,
    admit_ref,
    out_ref,
    holder_ref,
    serial_ref,
    packed_ref,
    rank_ref,
    core_ref,
    scales_ref,
    ids_ref,
):
    step = pl.program_id(0)

    @pl.when(step == 0)
    def _():
        rank_ref[...] = jnp.full(rank_ref.shape, lax.axis_index(VAR), jnp.int32)
        core_ref[...] = jnp.full(core_ref.shape, lax.axis_index("core"), jnp.int32)
        width = geno_ref.shape[1]
        lay_out(width, active_ref, admit_ref, holder_ref, serial_ref, packed_ref, ids_ref)
        look_up(table_ref, index_ref, scales_ref)
        out_ref[...] = jnp.zeros_like(out_ref)

    out_ref[...] += dot(resid_ref[...].astype(bf16), dequantized(geno_ref, scales_ref, step))


def screen(table, geno, index, resid, active_ids, admit_ids):
    samples, width = geno.shape
    phenos = resid.shape[0]
    active_ids, admit_ids = active_ids[None], admit_ids[None]
    fit = active_ids.size + admit_ids.size
    outs = [(phenos, width, f32), (1, fit, jnp.int32), (1, fit, jnp.int32)]
    outs += [(lax.axis_size(VAR), LANES, jnp.int32)] + [(2 * HALF, LANES, jnp.int32)] * 2
    whole = lambda shape: pl.BlockSpec(shape, lambda i: (0, 0))
    return pl.pallas_call(
        screen_kernel,
        grid=(samples // ROWS,),
        in_specs=[
            pl.BlockSpec(memory_space=pltpu.SMEM),
            pl.BlockSpec((ROWS, width), lambda i: (i, 0)),
            whole(index.shape),
            pl.BlockSpec((phenos, ROWS), lambda i: (0, i)),
            whole(active_ids.shape),
            whole(admit_ids.shape),
        ],
        out_specs=[whole(out[:2]) for out in outs],
        out_shape=[jax.ShapeDtypeStruct(out[:2], out[2]) for out in outs],
        scratch_shapes=[pltpu.VMEM(index.shape, f32), pltpu.VMEM((1, fit), jnp.int32)],
        compiler_params=LARGE,
        cost_estimate=pl.CostEstimate(
            flops=2 * phenos * samples * width, bytes_accessed=2 * samples * width, transcendentals=0
        ),
        name="screen",
    )(table, geno, index, resid, active_ids, admit_ids)


def select_kernel(first, table_ref, packed_ref, geno_ref, index_ref, out_ref, scales_ref, pick_ref):
    step = pl.program_id(0)

    @pl.when(step == 0)
    def _():
        look_up(table_ref, index_ref, scales_ref)
        wanted = column_row(packed_ref[...])

        @pl.loop(0, pick_ref.shape[0], step=ROWS)
        def _(at):
            here = iota((ROWS, pick_ref.shape[1]), 0) + (at + 1) == wanted
            pick_ref[pl.ds(pl.multiple_of(at, ROWS), ROWS), :] = here.astype(f32).astype(bf16)

    x = dequantized(geno_ref, scales_ref, first + step)
    out_ref[...] = dot(x, pick_ref[...]).astype(bf16)


def select(half, table, packed, geno, index, params):
    samples, width = geno.shape[0] // 2, geno.shape[1]
    held = packed.shape[0] * CAP
    rows = 2 * ROWS
    first = half * (samples // rows)
    return pl.pallas_call(
        functools.partial(select_kernel, first),
        grid=(samples // rows,),
        in_specs=[
            pl.BlockSpec(memory_space=pltpu.SMEM),
            pl.BlockSpec(packed.shape, lambda i: (0, 0)),
            pl.BlockSpec((rows, width), lambda i: (i + first, 0)),
            pl.BlockSpec(index.shape, lambda i: (0, 0)),
        ],
        out_specs=pl.BlockSpec((rows, held), lambda i: (i, 0)),
        out_shape=jax.ShapeDtypeStruct((samples, held), bf16),
        scratch_shapes=[pltpu.VMEM(index.shape, f32), pltpu.VMEM((width, held), bf16)],
        compiler_params=params,
        cost_estimate=pl.CostEstimate(
            flops=2 * samples * width * held, bytes_accessed=2 * samples * width, transcendentals=0
        ),
        name="select",
    )(table, packed, geno, index)


def pick_kernel(
    inv_root, own_ref, one_ref, two_ref, three_ref, packed_hbm, scores_ref, pay_ref, packed_ref, sem
):
    copy = pltpu.make_async_copy(packed_hbm, packed_ref, sem)
    copy.start()
    scores = ((own_ref[...] + two_ref[...]) + (one_ref[...] + three_ref[...])) * inv_root
    scores_ref[...] = scores
    copy.wait()
    wanted = column_row(packed_ref[...])
    stacked = jnp.concatenate(thirds(scores), 0)
    phenos, width = scores.shape
    total = jnp.zeros((stacked.shape[0], wanted.shape[1]), f32)
    for at in range(0, width, ROWS):
        here = iota((ROWS, wanted.shape[1]), 0) + (at + 1) == wanted
        total += dot(stacked[:, at : at + ROWS], here.astype(f32).astype(bf16))
    held = total[:phenos] + total[phenos : 2 * phenos] + total[2 * phenos :]
    for t in range(wanted.shape[1] // LANES):
        pay_ref[8 * t : 8 * t + 8, :] = swapped(held[:, t * LANES : (t + 1) * LANES])


def pick(parts, packed, inv_root):
    return pl.pallas_call(
        functools.partial(pick_kernel, inv_root),
        in_specs=[pl.BlockSpec(memory_space=pltpu.VMEM)] * 4
        + [pl.BlockSpec(memory_space=pltpu.HBM)],
        scratch_shapes=[pltpu.VMEM(packed.shape, packed.dtype), pltpu.SemaphoreType.DMA],
        out_shape=(
            jax.ShapeDtypeStruct(parts[0].shape, f32),
            jax.ShapeDtypeStruct((packed.shape[0] * HALF, LANES), f32),
        ),
        compiler_params=SMALL,
        name="pick",
    )(*parts, packed)


def direction_step(data, serial_ref, holder_ref, inverse_ref, advance, wide_ref, d_ref, pay_ref):
    fit = serial_ref.shape[1]
    holders = data.shape[0] // HALF
    spread, mask = slot_maps(serial_ref[...], holder_ref[...], holders)
    high, mid, low = thirds(data)
    placed = (dot(high, spread) + dot(mid, spread) + dot(low, spread)) * mask
    placed = jnp.sum(placed.reshape(-1, 2 * HALF, 2 * fit), 0)
    arrived = placed[:HALF] + placed[HALF:]
    inner = advance(arrived)
    wide_ref[:HALF, :] = inner[:, :fit]
    wide_ref[HALF:, :] = inner[:, fit:]
    blocks, size = inverse_ref.shape[0], inverse_ref.shape[1]
    for b in range(blocks):
        moved = dot_t(
            wide_ref[:, b * size : (b + 1) * size], inverse_ref[b], precision=lax.Precision.HIGHEST
        )
        moved = moved.astype(bf16).astype(f32)
        d_ref[:, b * size : (b + 1) * size] = moved[:HALF]
        d_ref[:, fit + b * size : fit + (b + 1) * size] = moved[HALF:]
    d = d_ref[...]
    d = jnp.concatenate([d, d], 0)
    d = jnp.broadcast_to(d[None], (holders * HALF // d.shape[0], *d.shape)).reshape(mask.shape)
    pay_ref[...] = dot_t((d * mask).astype(bf16), spread)


def first_owner_kernel(
    data_ref,
    serial_ref,
    holder_ref,
    inverse_ref,
    beta_ref,
    columns_hbm,
    pay_ref,
    b_ref,
    d_ref,
    g_ref,
    columns_ref,
    wide_ref,
    sem,
):
    copy = pltpu.make_async_copy(columns_hbm, columns_ref, sem)
    copy.start()
    fit = serial_ref.shape[1]
    active = beta_ref.shape[1]
    b_ref[...] = jnp.zeros_like(b_ref)
    b_ref[:, :active] = beta_ref[:HALF]
    b_ref[:, fit : fit + active] = beta_ref[HALF:]

    def advance(arrived):
        g_ref[...] = arrived
        return arrived - penalty * b_ref[...]

    direction_step(
        data_ref[...], serial_ref, holder_ref, inverse_ref, advance, wide_ref, d_ref, pay_ref
    )
    copy.wait()


def owner_kernel(
    data_ref,
    serial_ref,
    holder_ref,
    inverse_ref,
    b_in,
    d_in,
    g_in,
    resid_in,
    update_ref,
    pay_ref,
    b_ref,
    d_ref,
    resid_ref,
    g_ref,
    wide_ref,
    sum_ref,
    rows_ref,
    scalar_ref,
):
    fit = serial_ref.shape[1]
    chunk = sum_ref.shape[0]
    total = data_ref[:chunk, :]
    for at in range(chunk, data_ref.shape[0], chunk):
        total = total + data_ref[at : at + chunk, :]
    sum_ref[...] = total
    for k in range(chunk // (HALF + 1)):
        at = k * (HALF + 1)
        rows_ref[k * HALF : (k + 1) * HALF, :] = sum_ref[at : at + HALF, :]
        if k < scalar_ref.shape[0]:
            scalar_ref[k : k + 1, :] = sum_ref[at + HALF : at + HALF + 1, :]
    factor = scalar_ref[:, :1] / (scalar_ref[:, CAP : CAP + 1] + epsilon)
    resid_ref[...] = resid_in[...] - factor * update_ref[...]
    low = iota((HALF, 2 * fit), 1) < fit
    factor = jnp.where(low, factor[:HALF], factor[HALF:])

    def advance(arrived):
        g_ref[...] = g_in[...] - factor * arrived
        b_ref[...] = b_in[...] + factor * d_in[...]
        return g_ref[...] - penalty * b_ref[...]

    direction_step(
        rows_ref[...], serial_ref, holder_ref, inverse_ref, advance, wide_ref, d_ref, pay_ref
    )


def owner_first(data, serial, holder, inverse, beta, columns):
    fit = serial.shape[1]
    held = jax.ShapeDtypeStruct((HALF, 2 * fit), f32)
    vmem = pl.BlockSpec(memory_space=pltpu.VMEM)
    return pl.pallas_call(
        first_owner_kernel,
        in_specs=[vmem] * 5 + [pl.BlockSpec(memory_space=pltpu.HBM)],
        out_specs=(vmem,) * 5,
        out_shape=(
            jax.ShapeDtypeStruct(data.shape, f32),
            held,
            held,
            held,
            jax.ShapeDtypeStruct(columns.shape, columns.dtype),
        ),
        scratch_shapes=[pltpu.VMEM((2 * HALF, fit), f32), pltpu.SemaphoreType.DMA],
        compiler_params=MEDIUM,
        name="owner_first",
    )(data, serial, holder, inverse, beta, columns)


def owner_next(data, serial, holder, inverse, state, resid, update, final):
    fit = serial.shape[1]
    phenos = resid.shape[0]
    held = jax.ShapeDtypeStruct((HALF, 2 * fit), f32)
    rows = lax.axis_size(VAR) * HALF
    pay = jax.ShapeDtypeStruct((rows, LANES), f32)
    new_resid = jax.ShapeDtypeStruct(resid.shape, f32)
    return pl.pallas_call(
        owner_kernel,
        out_shape=(pay, held, held, new_resid) + (() if final else (held,)),
        scratch_shapes=([pltpu.VMEM(held.shape, f32)] if final else [])
        + [
            pltpu.VMEM((phenos, fit), f32),
            pltpu.VMEM((rows // HALF * (HALF + 1), LANES), f32),
            pltpu.VMEM((rows, LANES), f32),
            pltpu.VMEM((phenos, LANES), f32),
        ],
        compiler_params=SMALL,
        name="owner_next",
    )(data, serial, holder, inverse, *state, resid, update)


def update_kernel(core_ref, pay_ref, first_ref, second_ref, keep_ref, send_ref):
    packed = jnp.concatenate(
        [swapped(pay_ref[at : at + 8, :]) for at in range(0, pay_ref.shape[0], 8)], 1
    ).astype(bf16)
    first = core_ref[:, :1] == 0
    half = keep_ref.shape[1]
    for at in range(0, half, ROWS):
        a = dot_t(packed, first_ref[at : at + ROWS, :])
        b = dot_t(packed, second_ref[at : at + ROWS, :])
        keep_ref[:, at : at + ROWS] = jnp.where(first, a, b)
        send_ref[:, at : at + ROWS] = jnp.where(first, b, a)


def partial_update(core, pay, first, second):
    half = jax.ShapeDtypeStruct((2 * HALF, first.shape[0]), f32)
    return pl.pallas_call(
        update_kernel,
        out_shape=(half, half),
        compiler_params=SMALL,
        name="update",
    )(core, pay, first, second)


def spread_kernel(keep_ref, arrived_ref, out_ref):
    out_ref[...] = jnp.broadcast_to((keep_ref[...] + arrived_ref[...])[None], out_ref.shape)


def spread(keep, arrived, copies):
    return pl.pallas_call(
        spread_kernel,
        out_shape=jax.ShapeDtypeStruct((copies, *keep.shape), f32),
        compiler_params=SMALL,
        name="spread",
    )(keep, arrived)


def total_kernel(parts_ref, out_ref):
    total = parts_ref[0]
    for n in range(1, parts_ref.shape[0]):
        total = total + parts_ref[n]
    out_ref[...] = total


def total(parts):
    return pl.pallas_call(
        total_kernel,
        out_shape=jax.ShapeDtypeStruct(parts.shape[1:], f32),
        compiler_params=SMALL,
        name="total",
    )(parts)


def whole_update(inv_root, core_ref, mine_ref, other_ref):
    first = core_ref[:, :1] == 0
    mine, other = mine_ref[...] * inv_root, other_ref[...] * inv_root
    return jnp.concatenate([jnp.where(first, mine, other), jnp.where(first, other, mine)], 1)


def step_sums(resid, update):
    cross = jnp.sum(resid * update, 1, keepdims=True)
    square = jnp.sum(update * update, 1, keepdims=True)
    return jnp.where(iota((update.shape[0], LANES), 1) < CAP, cross, square)


def descent_kernel(
    inv_root,
    rank_ref,
    core_ref,
    mine_ref,
    other_ref,
    resid_ref,
    first_ref,
    second_ref,
    out_ref,
    update_ref,
):
    update = whole_update(inv_root, core_ref, mine_ref, other_ref)
    update_ref[...] = update
    phenos = update.shape[0]
    high = update.astype(bf16)
    low = (update - high.astype(f32)).astype(bf16)
    pair = jnp.concatenate([high, low], 0)
    half = first_ref.shape[0]
    grad = dot(pair[:, :half], first_ref[...]) + dot(pair[:, half:], second_ref[...])
    grad = (grad[:phenos] + grad[phenos:]) * inv_root
    both = step_sums(resid_ref[...], update)
    mine = iota(both.shape, 0) == lax.rem(rank_ref[...], phenos)
    row = jnp.sum(jnp.where(mine, both, 0.0), 0, keepdims=True)
    chunk = HALF + 1
    owners = grad.shape[1] // CAP
    copies = out_ref.shape[0] // (chunk * owners)
    for t in range(owners // 2):
        pair = swapped(grad[:, t * LANES : (t + 1) * LANES])
        for n in range(copies):
            at = (n * owners + 2 * t) * chunk
            out_ref[at : at + HALF, :] = pair[:HALF]
            out_ref[at + HALF : at + HALF + 1, :] = row
            out_ref[at + chunk : at + chunk + HALF, :] = pair[HALF:]
            out_ref[at + chunk + HALF : at + 2 * chunk, :] = row


def descent(rank, core, mine, other, resid, first, second, inv_root, copies):
    out = (copies * (first.shape[1] // CAP) * (HALF + 1), LANES)
    return pl.pallas_call(
        functools.partial(descent_kernel, inv_root),
        out_shape=(jax.ShapeDtypeStruct(out, f32), jax.ShapeDtypeStruct(resid.shape, f32)),
        compiler_params=SMALL,
        name="descent",
    )(rank, core, mine, other, resid, first, second)


def settle_kernel(inv_root, core_ref, mine_ref, other_ref, resid_ref, sums_ref, update_ref):
    update = whole_update(inv_root, core_ref, mine_ref, other_ref)
    update_ref[...] = update
    sums_ref[...] = jnp.broadcast_to(step_sums(resid_ref[...], update)[None], sums_ref.shape)


def settle(core, mine, other, resid, inv_root, copies):
    return pl.pallas_call(
        functools.partial(settle_kernel, inv_root),
        out_shape=(
            jax.ShapeDtypeStruct((copies, resid.shape[0], LANES), f32),
            jax.ShapeDtypeStruct(resid.shape, f32),
        ),
        compiler_params=SMALL,
        name="settle",
    )(core, mine, other, resid)


def last_kernel(sums_ref, b_ref, d_ref, resid_ref, update_ref, coeffs_ref, out_ref):
    phenos, fit = coeffs_ref.shape
    total = sums_ref[0]
    for j in range(1, sums_ref.shape[0]):
        total = total + sums_ref[j]
    factor = total[:, :1] / (total[:, CAP : CAP + 1] + epsilon)
    for half in range(2):
        rows = slice(half * HALF, (half + 1) * HALF)
        cols = slice(half * fit, (half + 1) * fit)
        coeffs_ref[rows, :] = b_ref[:, cols] + factor[rows] * d_ref[:, cols]
    out_ref[...] = resid_ref[...] - factor * update_ref[...]


def last(sums, coeffs, direction, resid, update):
    phenos = resid.shape[0]
    return pl.pallas_call(
        last_kernel,
        out_shape=(
            jax.ShapeDtypeStruct((phenos, coeffs.shape[1] // 2), f32),
            jax.ShapeDtypeStruct(resid.shape, f32),
        ),
        compiler_params=SMALL,
        name="last",
    )(sums, coeffs, direction, resid, update)


def exchange(pay, axes):
    count = lax.axis_size(axes)
    rows = pay.shape[0] // count
    shape = (count, rows, LANES) if rows == HALF else (count, 1, rows * LANES)
    return lax.all_to_all(
        pay.reshape(shape), axes, split_axis=0, concat_axis=0, tiled=True
    ).reshape(pay.shape)


def shifted(x, axis, by=1):
    size = lax.axis_size(axis)
    return lax.ppermute(x, axis, [(i, (i + by) % size) for i in range(size)])


def on_device(
    geno, scale_index, scale_table, residual, beta_active, block_inverse, active_ids, admit_ids
):
    holders = lax.axis_size(VAR)
    samples, width = geno.shape
    copies = lax.axis_size(SAMP)
    inv_root = 1.0 / math.sqrt(samples * copies)

    part, holder, serial, packed, rank, core = screen(
        scale_table, geno, scale_index, residual, active_ids, admit_ids
    )
    part = part + shifted(part, "y_hi")
    parts = [part] + [shifted(part, "x", n) for n in range(1, lax.axis_size("x"))]
    packed = lax.all_to_all(
        packed.reshape(holders, 1, LANES), VAR, split_axis=0, concat_axis=0, tiled=True
    ).reshape(holders, LANES)

    first = select(0, scale_table, packed, geno, scale_index, MEDIUM)
    parts, first = lax.optimization_barrier((parts, first))
    scores, pay = pick(parts, packed, inv_root)
    pay, packed = lax.optimization_barrier((pay, packed))
    second = select(1, scale_table, packed, geno, scale_index, LARGE)
    pay, *state, second = owner_first(
        exchange(pay, VAR), serial, holder, block_inverse, beta_active, second
    )
    current = residual
    for pass_index in range(PASSES):
        keep, send = partial_update(core, exchange(pay, VAR), first, second)
        mine = spread(keep, shifted(send, "core"), lax.axis_size(CHIPS))
        mine = total(lax.all_to_all(mine, CHIPS, split_axis=0, concat_axis=0, tiled=True))
        other = shifted(mine, "core")
        if pass_index + 1 == PASSES:
            break
        data, update = descent(rank, core, mine, other, current, first, second, inv_root, copies)
        pay, coeffs, direction, current, *gradient = owner_next(
            exchange(data, SAMP + VAR),
            serial,
            holder,
            block_inverse,
            state,
            current,
            update,
            pass_index + 2 == PASSES,
        )
        state = (coeffs, direction, *gradient)

    sums, update = settle(core, mine, other, current, inv_root, copies)
    sums = lax.all_to_all(sums, SAMP, split_axis=0, concat_axis=0, tiled=True)
    return (scores, *last(sums, coeffs, direction, current, update))


def solution(mesh):
    torus = Mesh(mesh.devices.reshape(2, 4, 2, 2, 4), VAR + SAMP)
    placed = (
        P(SAMP, VAR),
        P(SAMP, VAR),
        P(),
        P(None, SAMP),
        P(None, VAR),
        P(VAR, None, None),
        P(VAR),
        P(VAR),
    )
    return jax.shard_map(
        on_device,
        mesh=torus,
        in_specs=placed,
        out_specs=(P(None, VAR), P(None, VAR), P(None, SAMP)),
        check_vma=False,
    )
```

```python
import functools
import math

import jax
import jax.numpy as jnp
from jax import lax
from jax.experimental import pallas as pl
from jax.experimental.pallas import tpu as pltpu
from jax.sharding import Mesh
from jax.sharding import PartitionSpec as P

PASSES = 3
VAR = ("y_lo", "z", "core")
SAMP = ("y_hi", "x")
CHIPS = ("y_lo", "z")

CAP = 64
LANES = 128
ROWS = 256
HALF = 4

penalty = 0.5
epsilon = 1e-06
SMALL = pltpu.CompilerParams(vmem_limit_bytes=12 * 1024 * 1024)
MEDIUM = pltpu.CompilerParams(vmem_limit_bytes=48 * 1024 * 1024)
LARGE = pltpu.CompilerParams(vmem_limit_bytes=60 * 1024 * 1024)
f32 = jnp.float32
bf16 = jnp.bfloat16


def iota(shape, dim):
    return lax.broadcasted_iota(jnp.int32, shape, dim)


def dot(a, b, **kw):
    return jnp.dot(a, b, preferred_element_type=f32, **kw)


def dot_t(a, b, **kw):
    return lax.dot_general(a, b, (((1,), (1,)), ((), ())), preferred_element_type=f32, **kw)


def thirds(x):
    high = x.astype(bf16)
    rest = x - high.astype(f32)
    mid = rest.astype(bf16)
    return high, mid, (rest - mid.astype(f32)).astype(bf16)


def swapped(x):
    here = (iota(x.shape, 0) // HALF) == (iota(x.shape, 1) // CAP)
    return jnp.where(here, x, pltpu.roll(pltpu.roll(x, HALF, 0), CAP, 1))


def column_row(packed):
    low = iota((1, LANES), 1) < CAP
    return jnp.concatenate(
        [
            jnp.where(low, packed[t : t + 1], packed[t + 1 : t + 2])
            for t in range(0, packed.shape[0], 2)
        ],
        1,
    )


def slot_maps(serial, holder, holders):
    fit = serial.shape[1]
    serial2 = jnp.concatenate([serial, serial], 1)
    holder2 = jnp.concatenate([holder, holder], 1)
    shape = (2 * CAP, 2 * fit)
    rows, cols = iota(shape, 0), iota(shape, 1)
    spread = ((rows // CAP) == (cols // fit)) & ((rows % CAP) == serial2)
    mask = (iota((holders * HALF, 2 * fit), 0) // HALF) == holder2
    return spread.astype(f32).astype(bf16), mask.astype(f32)


def lay_out(width, active_ref, admit_ref, holder_ref, serial_ref, packed_ref, ids_ref):
    holders = packed_ref.shape[0]
    fit = holder_ref.shape[1]
    active = active_ref.shape[1]
    ids_ref[:, :active] = active_ref[...]
    ids_ref[:, active:] = admit_ref[...]
    ids = ids_ref[...]
    holder = ids // width
    holder_ref[...] = holder
    marks = (iota((holders, fit), 0) == holder).astype(f32)
    earlier = (iota((fit, fit), 0) < iota((fit, fit), 1)).astype(f32).astype(bf16)
    before = dot(marks.astype(bf16), earlier)
    serial = jnp.sum(before * marks, 0, keepdims=True).astype(jnp.int32)
    serial_ref[...] = serial
    spread, _ = slot_maps(serial, holder, holders)
    marks2 = jnp.concatenate([marks, marks], 1)
    column = ids - holder * width + 1
    parts = []
    for piece in (column // LANES, column % LANES):
        row = piece.astype(f32)
        row = jnp.concatenate([row, row], 1)
        parts.append(dot_t((marks2 * row).astype(bf16), spread))
    packed_ref[...] = (parts[0] * LANES + parts[1]).astype(jnp.int32)


def look_up(table_ref, index_ref, scales_ref):
    index = index_ref[...]
    scales = jnp.full(index.shape, table_ref[0], f32)
    for level in range(1, table_ref.shape[0]):
        scales = jnp.where(index == level, table_ref[level], scales)
    scales_ref[...] = scales


def dequantized(geno_ref, scales_ref, step):
    rows = geno_ref.shape[0]
    group = 128
    out = []
    for g in range(rows // group):
        scale = scales_ref[pl.ds(step * (rows // group) + g, 1), :]
        wide = geno_ref[g * group : (g + 1) * group, :].astype(f32) * scale
        out.append(wide.astype(bf16))
    return jnp.concatenate(out, 0)


def screen_kernel(
    table_ref,
    geno_ref,
    index_ref,
    resid_ref,
    active_ref,
    admit_ref,
    out_ref,
    holder_ref,
    serial_ref,
    packed_ref,
    rank_ref,
    core_ref,
    scales_ref,
    ids_ref,
):
    step = pl.program_id(0)

    @pl.when(step == 0)
    def _():
        rank_ref[...] = jnp.full(rank_ref.shape, lax.axis_index(VAR), jnp.int32)
        core_ref[...] = jnp.full(core_ref.shape, lax.axis_index("core"), jnp.int32)
        width = geno_ref.shape[1]
        lay_out(width, active_ref, admit_ref, holder_ref, serial_ref, packed_ref, ids_ref)
        look_up(table_ref, index_ref, scales_ref)
        out_ref[...] = jnp.zeros_like(out_ref)

    out_ref[...] += dot(resid_ref[...].astype(bf16), dequantized(geno_ref, scales_ref, step))


def screen(table, geno, index, resid, active_ids, admit_ids):
    samples, width = geno.shape
    phenos = resid.shape[0]
    active_ids, admit_ids = active_ids[None], admit_ids[None]
    fit = active_ids.size + admit_ids.size
    outs = [(phenos, width, f32), (1, fit, jnp.int32), (1, fit, jnp.int32)]
    outs += [(lax.axis_size(VAR), LANES, jnp.int32)] + [(2 * HALF, LANES, jnp.int32)] * 2
    whole = lambda shape: pl.BlockSpec(shape, lambda i: (0, 0))
    return pl.pallas_call(
        screen_kernel,
        grid=(samples // ROWS,),
        in_specs=[
            pl.BlockSpec(memory_space=pltpu.SMEM),
            pl.BlockSpec((ROWS, width), lambda i: (i, 0)),
            whole(index.shape),
            pl.BlockSpec((phenos, ROWS), lambda i: (0, i)),
            whole(active_ids.shape),
            whole(admit_ids.shape),
        ],
        out_specs=[whole(out[:2]) for out in outs],
        out_shape=[jax.ShapeDtypeStruct(out[:2], out[2]) for out in outs],
        scratch_shapes=[pltpu.VMEM(index.shape, f32), pltpu.VMEM((1, fit), jnp.int32)],
        compiler_params=LARGE,
        cost_estimate=pl.CostEstimate(
            flops=2 * phenos * samples * width, bytes_accessed=2 * samples * width, transcendentals=0
        ),
        name="screen",
    )(table, geno, index, resid, active_ids, admit_ids)


def select_kernel(first, table_ref, packed_ref, geno_ref, index_ref, out_ref, scales_ref, pick_ref):
    step = pl.program_id(0)

    @pl.when(step == 0)
    def _():
        look_up(table_ref, index_ref, scales_ref)
        wanted = column_row(packed_ref[...])

        @pl.loop(0, pick_ref.shape[0], step=ROWS)
        def _(at):
            here = iota((ROWS, pick_ref.shape[1]), 0) + (at + 1) == wanted
            pick_ref[pl.ds(pl.multiple_of(at, ROWS), ROWS), :] = here.astype(f32).astype(bf16)

    x = dequantized(geno_ref, scales_ref, first + step)
    out_ref[...] = dot(x, pick_ref[...]).astype(bf16)


def select(half, table, packed, geno, index, params):
    samples, width = geno.shape[0] // 2, geno.shape[1]
    held = packed.shape[0] * CAP
    rows = 2 * ROWS
    first = half * (samples // rows)
    return pl.pallas_call(
        functools.partial(select_kernel, first),
        grid=(samples // rows,),
        in_specs=[
            pl.BlockSpec(memory_space=pltpu.SMEM),
            pl.BlockSpec(packed.shape, lambda i: (0, 0)),
            pl.BlockSpec((rows, width), lambda i: (i + first, 0)),
            pl.BlockSpec(index.shape, lambda i: (0, 0)),
        ],
        out_specs=pl.BlockSpec((rows, held), lambda i: (i, 0)),
        out_shape=jax.ShapeDtypeStruct((samples, held), bf16),
        scratch_shapes=[pltpu.VMEM(index.shape, f32), pltpu.VMEM((width, held), bf16)],
        compiler_params=params,
        cost_estimate=pl.CostEstimate(
            flops=2 * samples * width * held, bytes_accessed=2 * samples * width, transcendentals=0
        ),
        name="select",
    )(table, packed, geno, index)


def pick_kernel(inv_root, part_ref, packed_ref, pay_ref):
    part = part_ref[...] * inv_root
    wanted = column_row(packed_ref[...])
    stacked = jnp.concatenate(thirds(part), 0)
    phenos, width = part.shape
    total = jnp.zeros((stacked.shape[0], wanted.shape[1]), f32)
    for at in range(0, width, ROWS):
        here = iota((ROWS, wanted.shape[1]), 0) + (at + 1) == wanted
        total += dot(stacked[:, at : at + ROWS], here.astype(f32).astype(bf16))
    held = total[:phenos] + total[phenos : 2 * phenos] + total[2 * phenos :]
    rows = packed_ref.shape[0] * HALF
    for t in range(wanted.shape[1] // LANES):
        pair = swapped(held[:, t * LANES : (t + 1) * LANES])
        for at in range(8 * t, pay_ref.shape[0], rows):
            pay_ref[at : at + 8, :] = pair


def pick(part, packed, inv_root, copies):
    return pl.pallas_call(
        functools.partial(pick_kernel, inv_root),
        out_shape=jax.ShapeDtypeStruct((copies * packed.shape[0] * HALF, LANES), f32),
        compiler_params=SMALL,
        name="pick",
    )(part, packed)


def tally_kernel(inv_root, own_ref, one_ref, two_ref, three_ref, scores_ref):
    scores_ref[...] = ((own_ref[...] + two_ref[...]) + (one_ref[...] + three_ref[...])) * inv_root


def tally(parts, inv_root):
    return pl.pallas_call(
        functools.partial(tally_kernel, inv_root),
        out_shape=jax.ShapeDtypeStruct(parts[0].shape, f32),
        compiler_params=SMALL,
        name="tally",
    )(*parts)


def direction_step(data, serial_ref, holder_ref, inverse_ref, advance, wide_ref, d_ref, pay_ref):
    fit = serial_ref.shape[1]
    holders = data.shape[0] // HALF
    spread, mask = slot_maps(serial_ref[...], holder_ref[...], holders)
    high, mid, low = thirds(data)
    placed = (dot(high, spread) + dot(mid, spread) + dot(low, spread)) * mask
    placed = jnp.sum(placed.reshape(-1, 2 * HALF, 2 * fit), 0)
    arrived = placed[:HALF] + placed[HALF:]
    inner = advance(arrived)
    wide_ref[:HALF, :] = inner[:, :fit]
    wide_ref[HALF:, :] = inner[:, fit:]
    blocks, size = inverse_ref.shape[0], inverse_ref.shape[1]
    for b in range(blocks):
        moved = dot_t(
            wide_ref[:, b * size : (b + 1) * size], inverse_ref[b], precision=lax.Precision.HIGHEST
        )
        moved = moved.astype(bf16).astype(f32)
        d_ref[:, b * size : (b + 1) * size] = moved[:HALF]
        d_ref[:, fit + b * size : fit + (b + 1) * size] = moved[HALF:]
    d = d_ref[...]
    d = jnp.concatenate([d, d], 0)
    d = jnp.broadcast_to(d[None], (holders * HALF // d.shape[0], *d.shape)).reshape(mask.shape)
    pay_ref[...] = dot_t((d * mask).astype(bf16), spread)


def first_owner_kernel(
    data_ref,
    serial_ref,
    holder_ref,
    inverse_ref,
    beta_ref,
    pay_ref,
    b_ref,
    d_ref,
    g_ref,
    wide_ref,
):
    rows = pay_ref.shape[0]
    data = data_ref[:rows, :]
    for at in range(rows, data_ref.shape[0], rows):
        data = data + data_ref[at : at + rows, :]
    fit = serial_ref.shape[1]
    active = beta_ref.shape[1]
    b_ref[...] = jnp.zeros_like(b_ref)
    b_ref[:, :active] = beta_ref[:HALF]
    b_ref[:, fit : fit + active] = beta_ref[HALF:]

    def advance(arrived):
        g_ref[...] = arrived
        return arrived - penalty * b_ref[...]

    direction_step(data, serial_ref, holder_ref, inverse_ref, advance, wide_ref, d_ref, pay_ref)


def owner_kernel(
    data_ref,
    serial_ref,
    holder_ref,
    inverse_ref,
    b_in,
    d_in,
    g_in,
    resid_in,
    update_ref,
    pay_ref,
    b_ref,
    d_ref,
    resid_ref,
    g_ref,
    wide_ref,
    sum_ref,
    rows_ref,
    scalar_ref,
):
    fit = serial_ref.shape[1]
    chunk = sum_ref.shape[0]
    total = data_ref[:chunk, :]
    for at in range(chunk, data_ref.shape[0], chunk):
        total = total + data_ref[at : at + chunk, :]
    sum_ref[...] = total
    for k in range(chunk // (HALF + 1)):
        at = k * (HALF + 1)
        rows_ref[k * HALF : (k + 1) * HALF, :] = sum_ref[at : at + HALF, :]
        if k < scalar_ref.shape[0]:
            scalar_ref[k : k + 1, :] = sum_ref[at + HALF : at + HALF + 1, :]
    factor = scalar_ref[:, :1] / (scalar_ref[:, CAP : CAP + 1] + epsilon)
    resid_ref[...] = resid_in[...] - factor * update_ref[...]
    low = iota((HALF, 2 * fit), 1) < fit
    factor = jnp.where(low, factor[:HALF], factor[HALF:])

    def advance(arrived):
        g_ref[...] = g_in[...] - factor * arrived
        b_ref[...] = b_in[...] + factor * d_in[...]
        return g_ref[...] - penalty * b_ref[...]

    direction_step(
        rows_ref[...], serial_ref, holder_ref, inverse_ref, advance, wide_ref, d_ref, pay_ref
    )


def owner_first(data, serial, holder, inverse, beta):
    fit = serial.shape[1]
    held = jax.ShapeDtypeStruct((HALF, 2 * fit), f32)
    pay = jax.ShapeDtypeStruct((lax.axis_size(VAR) * HALF, LANES), f32)
    return pl.pallas_call(
        first_owner_kernel,
        out_shape=(pay, held, held, held),
        scratch_shapes=[pltpu.VMEM((2 * HALF, fit), f32)],
        compiler_params=SMALL,
        name="owner_first",
    )(data, serial, holder, inverse, beta)


def owner_next(data, serial, holder, inverse, state, resid, update, final):
    fit = serial.shape[1]
    phenos = resid.shape[0]
    held = jax.ShapeDtypeStruct((HALF, 2 * fit), f32)
    rows = lax.axis_size(VAR) * HALF
    pay = jax.ShapeDtypeStruct((rows, LANES), f32)
    new_resid = jax.ShapeDtypeStruct(resid.shape, f32)
    return pl.pallas_call(
        owner_kernel,
        out_shape=(pay, held, held, new_resid) + (() if final else (held,)),
        scratch_shapes=([pltpu.VMEM(held.shape, f32)] if final else [])
        + [
            pltpu.VMEM((phenos, fit), f32),
            pltpu.VMEM((rows // HALF * (HALF + 1), LANES), f32),
            pltpu.VMEM((rows, LANES), f32),
            pltpu.VMEM((phenos, LANES), f32),
        ],
        compiler_params=SMALL,
        name="owner_next",
    )(data, serial, holder, inverse, *state, resid, update)


def update_kernel(core_ref, pay_ref, first_ref, second_ref, keep_ref, send_ref, ready=None):
    packed = jnp.concatenate(
        [swapped(pay_ref[at : at + 8, :]) for at in range(0, pay_ref.shape[0], 8)], 1
    ).astype(bf16)
    mine = core_ref[:, :1] == 0
    blocks = range(0, keep_ref.shape[1], ROWS)
    early = [dot_t(packed, first_ref[at : at + ROWS, :]) for at in blocks]
    if ready is not None:
        ready()
    for a, at in zip(early, blocks):
        b = dot_t(packed, second_ref[at : at + ROWS, :])
        keep_ref[:, at : at + ROWS] = jnp.where(mine, a, b)
        send_ref[:, at : at + ROWS] = jnp.where(mine, b, a)


def partial_update(core, pay, first, second):
    half = jax.ShapeDtypeStruct((2 * HALF, first.shape[0]), f32)
    return pl.pallas_call(
        update_kernel,
        out_shape=(half, half),
        compiler_params=SMALL,
        name="update",
    )(core, pay, first, second)


def fetching_kernel(
    core_ref, pay_ref, first_ref, second_hbm, keep_ref, send_ref, second_ref, sem
):
    copy = pltpu.make_async_copy(second_hbm, second_ref, sem)
    copy.start()
    update_kernel(core_ref, pay_ref, first_ref, second_ref, keep_ref, send_ref, copy.wait)


def first_update(core, pay, first, second):
    half = jax.ShapeDtypeStruct((2 * HALF, first.shape[0]), f32)
    vmem = pl.BlockSpec(memory_space=pltpu.VMEM)
    return pl.pallas_call(
        fetching_kernel,
        in_specs=[vmem] * 3 + [pl.BlockSpec(memory_space=pltpu.HBM)],
        out_specs=(vmem,) * 3,
        out_shape=(half, half, jax.ShapeDtypeStruct(second.shape, second.dtype)),
        scratch_shapes=[pltpu.SemaphoreType.DMA],
        compiler_params=MEDIUM,
        name="update_first",
    )(core, pay, first, second)


def spread_kernel(keep_ref, arrived_ref, out_ref):
    out_ref[...] = jnp.broadcast_to((keep_ref[...] + arrived_ref[...])[None], out_ref.shape)


def spread(keep, arrived, copies):
    return pl.pallas_call(
        spread_kernel,
        out_shape=jax.ShapeDtypeStruct((copies, *keep.shape), f32),
        compiler_params=SMALL,
        name="spread",
    )(keep, arrived)


def total_kernel(parts_ref, out_ref):
    total = parts_ref[0]
    for n in range(1, parts_ref.shape[0]):
        total = total + parts_ref[n]
    out_ref[...] = total


def total(parts):
    return pl.pallas_call(
        total_kernel,
        out_shape=jax.ShapeDtypeStruct(parts.shape[1:], f32),
        compiler_params=SMALL,
        name="total",
    )(parts)


def whole_update(inv_root, core_ref, mine_ref, other_ref):
    first = core_ref[:, :1] == 0
    mine, other = mine_ref[...] * inv_root, other_ref[...] * inv_root
    return jnp.concatenate([jnp.where(first, mine, other), jnp.where(first, other, mine)], 1)


def step_sums(resid, update):
    cross = jnp.sum(resid * update, 1, keepdims=True)
    square = jnp.sum(update * update, 1, keepdims=True)
    return jnp.where(iota((update.shape[0], LANES), 1) < CAP, cross, square)


def descent_kernel(
    inv_root,
    rank_ref,
    core_ref,
    mine_ref,
    other_ref,
    resid_ref,
    first_ref,
    second_ref,
    out_ref,
    update_ref,
):
    update = whole_update(inv_root, core_ref, mine_ref, other_ref)
    update_ref[...] = update
    phenos = update.shape[0]
    high = update.astype(bf16)
    low = (update - high.astype(f32)).astype(bf16)
    pair = jnp.concatenate([high, low], 0)
    half = first_ref.shape[0]
    grad = dot(pair[:, :half], first_ref[...]) + dot(pair[:, half:], second_ref[...])
    grad = (grad[:phenos] + grad[phenos:]) * inv_root
    both = step_sums(resid_ref[...], update)
    mine = iota(both.shape, 0) == lax.rem(rank_ref[...], phenos)
    row = jnp.sum(jnp.where(mine, both, 0.0), 0, keepdims=True)
    chunk = HALF + 1
    owners = grad.shape[1] // CAP
    copies = out_ref.shape[0] // (chunk * owners)
    for t in range(owners // 2):
        pair = swapped(grad[:, t * LANES : (t + 1) * LANES])
        for n in range(copies):
            at = (n * owners + 2 * t) * chunk
            out_ref[at : at + HALF, :] = pair[:HALF]
            out_ref[at + HALF : at + HALF + 1, :] = row
            out_ref[at + chunk : at + chunk + HALF, :] = pair[HALF:]
            out_ref[at + chunk + HALF : at + 2 * chunk, :] = row


def descent(rank, core, mine, other, resid, first, second, inv_root, copies):
    out = (copies * (first.shape[1] // CAP) * (HALF + 1), LANES)
    return pl.pallas_call(
        functools.partial(descent_kernel, inv_root),
        out_shape=(jax.ShapeDtypeStruct(out, f32), jax.ShapeDtypeStruct(resid.shape, f32)),
        compiler_params=SMALL,
        name="descent",
    )(rank, core, mine, other, resid, first, second)


def settle_kernel(inv_root, core_ref, mine_ref, resid_ref, sums_ref):
    half = mine_ref.shape[1]
    resid = jnp.where(core_ref[:, :1] == 0, resid_ref[:, :half], resid_ref[:, half:])
    sums = step_sums(resid, mine_ref[...] * inv_root)
    sums_ref[...] = jnp.broadcast_to(sums[None], sums_ref.shape)


def settle(core, mine, resid, inv_root, copies):
    return pl.pallas_call(
        functools.partial(settle_kernel, inv_root),
        out_shape=jax.ShapeDtypeStruct((copies, resid.shape[0], LANES), f32),
        compiler_params=SMALL,
        name="settle",
    )(core, mine, resid)


def last_kernel(
    inv_root, sums_ref, core_ref, mine_ref, other_ref, b_ref, d_ref, resid_ref, coeffs_ref, out_ref
):
    phenos, fit = coeffs_ref.shape
    total = sums_ref[0]
    for j in range(1, sums_ref.shape[0]):
        total = total + sums_ref[j]
    factor = total[:, :1] / (total[:, CAP : CAP + 1] + epsilon)
    for half in range(2):
        rows = slice(half * HALF, (half + 1) * HALF)
        cols = slice(half * fit, (half + 1) * fit)
        coeffs_ref[rows, :] = b_ref[:, cols] + factor[rows] * d_ref[:, cols]
    update = whole_update(inv_root, core_ref, mine_ref, other_ref)
    out_ref[...] = resid_ref[...] - factor * update


def last(sums, core, mine, other, coeffs, direction, resid, inv_root):
    phenos = resid.shape[0]
    return pl.pallas_call(
        functools.partial(last_kernel, inv_root),
        out_shape=(
            jax.ShapeDtypeStruct((phenos, coeffs.shape[1] // 2), f32),
            jax.ShapeDtypeStruct(resid.shape, f32),
        ),
        compiler_params=SMALL,
        name="last",
    )(sums, core, mine, other, coeffs, direction, resid)


def exchange(pay, axes):
    count = lax.axis_size(axes)
    rows = pay.shape[0] // count
    shape = (count, rows, LANES) if rows == HALF else (count, 1, rows * LANES)
    return lax.all_to_all(
        pay.reshape(shape), axes, split_axis=0, concat_axis=0, tiled=True
    ).reshape(pay.shape)


def shifted(x, axis, by=1):
    size = lax.axis_size(axis)
    return lax.ppermute(x, axis, [(i, (i + by) % size) for i in range(size)])


def on_device(
    geno, scale_index, scale_table, residual, beta_active, block_inverse, active_ids, admit_ids
):
    holders = lax.axis_size(VAR)
    samples, width = geno.shape
    copies = lax.axis_size(SAMP)
    inv_root = 1.0 / math.sqrt(samples * copies)

    part, holder, serial, packed, rank, core = screen(
        scale_table, geno, scale_index, residual, active_ids, admit_ids
    )
    packed = lax.all_to_all(
        packed.reshape(holders, 1, LANES), VAR, split_axis=0, concat_axis=0, tiled=True
    ).reshape(holders, LANES)

    pay = pick(part, packed, inv_root, copies)
    pay, packed, part = lax.optimization_barrier((pay, packed, part))
    part = part + shifted(part, "y_hi")
    first = select(0, scale_table, packed, geno, scale_index, MEDIUM)
    data, first, part = lax.optimization_barrier((exchange(pay, SAMP + VAR), first, part))
    pay, *state = owner_first(data, serial, holder, block_inverse, beta_active)
    parts = [part] + [shifted(part, "x", n) for n in range(1, lax.axis_size("x"))]
    pay, packed = lax.optimization_barrier((pay, packed))
    second = select(1, scale_table, packed, geno, scale_index, LARGE)
    pay, second, parts = lax.optimization_barrier((exchange(pay, VAR), second, parts))
    scores = tally(parts, inv_root)
    current = residual
    for pass_index in range(PASSES):
        if pass_index == 0:
            keep, send, second = first_update(core, pay, first, second)
        else:
            keep, send = partial_update(core, exchange(pay, VAR), first, second)
        mine = spread(keep, shifted(send, "core"), lax.axis_size(CHIPS))
        mine = total(lax.all_to_all(mine, CHIPS, split_axis=0, concat_axis=0, tiled=True))
        other = shifted(mine, "core")
        if pass_index + 1 == PASSES:
            break
        data, update = descent(rank, core, mine, other, current, first, second, inv_root, copies)
        pay, coeffs, direction, current, *gradient = owner_next(
            exchange(data, SAMP + VAR),
            serial,
            holder,
            block_inverse,
            state,
            current,
            update,
            pass_index + 2 == PASSES,
        )
        state = (coeffs, direction, *gradient)

    sums = settle(core, mine, current, inv_root, 2 * copies)
    sums = lax.all_to_all(sums, ("core",) + SAMP, split_axis=0, concat_axis=0, tiled=True)
    return (scores, *last(sums, core, mine, other, coeffs, direction, current, inv_root))


def solution(mesh):
    torus = Mesh(mesh.devices.reshape(2, 4, 2, 2, 4), VAR + SAMP)
    placed = (
        P(SAMP, VAR),
        P(SAMP, VAR),
        P(),
        P(None, SAMP),
        P(None, VAR),
        P(VAR, None, None),
        P(VAR),
        P(VAR),
    )
    return jax.shard_map(
        on_device,
        mesh=torus,
        in_specs=placed,
        out_specs=(P(None, VAR), P(None, VAR), P(None, SAMP)),
        check_vma=False,
    )
```

```python
import functools
import math

import jax
import jax.numpy as jnp
from jax import lax
from jax.experimental import pallas as pl
from jax.experimental.pallas import tpu as pltpu
from jax.sharding import Mesh
from jax.sharding import PartitionSpec as P

PASSES = 3
VAR = ("y_lo", "z", "core")
SAMP = ("y_hi", "x")
CHIPS = ("y_lo", "z")

CAP = 64
LANES = 128
ROWS = 256
HALF = 4

penalty = 0.5
epsilon = 1e-06
SMALL = pltpu.CompilerParams(vmem_limit_bytes=12 * 1024 * 1024)
MEDIUM = pltpu.CompilerParams(vmem_limit_bytes=50 * 1024 * 1024)
WIDE = pltpu.CompilerParams(vmem_limit_bytes=52 * 1024 * 1024)
LARGE = pltpu.CompilerParams(vmem_limit_bytes=60 * 1024 * 1024)
f32 = jnp.float32
bf16 = jnp.bfloat16


def iota(shape, dim):
    return lax.broadcasted_iota(jnp.int32, shape, dim)


def dot(a, b, **kw):
    return jnp.dot(a, b, preferred_element_type=f32, **kw)


def dot_t(a, b, **kw):
    return lax.dot_general(a, b, (((1,), (1,)), ((), ())), preferred_element_type=f32, **kw)


def thirds(x):
    high = x.astype(bf16)
    rest = x - high.astype(f32)
    mid = rest.astype(bf16)
    return high, mid, (rest - mid.astype(f32)).astype(bf16)


def swapped(x):
    here = (iota(x.shape, 0) // HALF) == (iota(x.shape, 1) // CAP)
    return jnp.where(here, x, pltpu.roll(pltpu.roll(x, HALF, 0), CAP, 1))


def column_row(packed):
    low = iota((1, LANES), 1) < CAP
    return jnp.concatenate(
        [
            jnp.where(low, packed[t : t + 1], packed[t + 1 : t + 2])
            for t in range(0, packed.shape[0], 2)
        ],
        1,
    )


def slot_maps(serial, holder, holders):
    fit = serial.shape[1]
    serial2 = jnp.concatenate([serial, serial], 1)
    holder2 = jnp.concatenate([holder, holder], 1)
    shape = (2 * CAP, 2 * fit)
    rows, cols = iota(shape, 0), iota(shape, 1)
    spread = ((rows // CAP) == (cols // fit)) & ((rows % CAP) == serial2)
    mask = (iota((holders * HALF, 2 * fit), 0) // HALF) == holder2
    return spread.astype(f32).astype(bf16), mask.astype(f32)


def lay_out(width, active_ref, admit_ref, holder_ref, serial_ref, packed_ref, ids_ref):
    holders = packed_ref.shape[0]
    fit = holder_ref.shape[1]
    active = active_ref.shape[1]
    ids_ref[:, :active] = active_ref[...]
    ids_ref[:, active:] = admit_ref[...]
    ids = ids_ref[...]
    holder = ids // width
    holder_ref[...] = holder
    marks = (iota((holders, fit), 0) == holder).astype(f32)
    earlier = (iota((fit, fit), 0) < iota((fit, fit), 1)).astype(f32).astype(bf16)
    before = dot(marks.astype(bf16), earlier)
    serial = jnp.sum(before * marks, 0, keepdims=True).astype(jnp.int32)
    serial_ref[...] = serial
    spread, _ = slot_maps(serial, holder, holders)
    marks2 = jnp.concatenate([marks, marks], 1)
    column = ids - holder * width + 1
    parts = []
    for piece in (column // LANES, column % LANES):
        row = piece.astype(f32)
        row = jnp.concatenate([row, row], 1)
        parts.append(dot_t((marks2 * row).astype(bf16), spread))
    packed_ref[...] = (parts[0] * LANES + parts[1]).astype(jnp.int32)


def look_up(table_ref, index_ref, scales_ref):
    index = index_ref[...]
    scales = jnp.full(index.shape, table_ref[0], f32)
    for level in range(1, table_ref.shape[0]):
        scales = jnp.where(index == level, table_ref[level], scales)
    scales_ref[...] = scales


def dequantized(geno_ref, scales_ref, first):
    rows = geno_ref.shape[0]
    group = 128
    out = []
    for g in range(rows // group):
        scale = scales_ref[pl.ds(first // group + g, 1), :]
        wide = geno_ref[g * group : (g + 1) * group, :].astype(f32) * scale
        out.append(wide.astype(bf16))
    return jnp.concatenate(out, 0)


def screen_kernel(
    table_ref,
    geno_ref,
    index_ref,
    resid_ref,
    active_ref,
    admit_ref,
    out_ref,
    holder_ref,
    serial_ref,
    packed_ref,
    rank_ref,
    core_ref,
    scales_ref,
    ids_ref,
):
    step = pl.program_id(0)

    @pl.when(step == 0)
    def _():
        rank_ref[...] = jnp.full(rank_ref.shape, lax.axis_index(VAR), jnp.int32)
        core_ref[...] = jnp.full(core_ref.shape, lax.axis_index("core"), jnp.int32)
        width = geno_ref.shape[1]
        lay_out(width, active_ref, admit_ref, holder_ref, serial_ref, packed_ref, ids_ref)
        look_up(table_ref, index_ref, scales_ref)
        out_ref[...] = jnp.zeros_like(out_ref)

    out_ref[...] += dot(resid_ref[...].astype(bf16), dequantized(geno_ref, scales_ref, step * ROWS))


def screen(table, geno, index, resid, active_ids, admit_ids):
    samples, width = geno.shape
    phenos = resid.shape[0]
    active_ids, admit_ids = active_ids[None], admit_ids[None]
    fit = active_ids.size + admit_ids.size
    outs = [(phenos, width, f32), (1, fit, jnp.int32), (1, fit, jnp.int32)]
    outs += [(lax.axis_size(VAR), LANES, jnp.int32)] + [(2 * HALF, LANES, jnp.int32)] * 2
    whole = lambda shape: pl.BlockSpec(shape, lambda i: (0, 0))
    return pl.pallas_call(
        screen_kernel,
        grid=(samples // ROWS,),
        in_specs=[
            pl.BlockSpec(memory_space=pltpu.SMEM),
            pl.BlockSpec((ROWS, width), lambda i: (i, 0)),
            whole(index.shape),
            pl.BlockSpec((phenos, ROWS), lambda i: (0, i)),
            whole(active_ids.shape),
            whole(admit_ids.shape),
        ],
        out_specs=[whole(out[:2]) for out in outs],
        out_shape=[jax.ShapeDtypeStruct(out[:2], out[2]) for out in outs],
        scratch_shapes=[pltpu.VMEM(index.shape, f32), pltpu.VMEM((1, fit), jnp.int32)],
        compiler_params=LARGE,
        cost_estimate=pl.CostEstimate(
            flops=2 * phenos * samples * width, bytes_accessed=2 * samples * width, transcendentals=0
        ),
        name="screen",
    )(table, geno, index, resid, active_ids, admit_ids)


def select_kernel(
    own, table_ref, packed_ref, index_ref, geno_hbm, out_ref, scales_ref, pick_ref, geno_ref, sems
):
    samples = out_ref.shape[0]
    chunks, rows = geno_ref.shape[:2]
    core = lax.axis_index("core")
    first = (core if own else 1 - core) * samples
    copies = []
    for n in range(chunks):
        at = pl.multiple_of(first + n * rows, rows)
        copies.append(
            pltpu.make_async_copy(geno_hbm.at[pl.ds(at, rows)], geno_ref.at[n], sems.at[n])
        )
        copies[n].start()
    look_up(table_ref, index_ref, scales_ref)
    wanted = column_row(packed_ref[...])

    @pl.loop(0, pick_ref.shape[0], step=ROWS)
    def _(at):
        here = iota((ROWS, pick_ref.shape[1]), 0) + (at + 1) == wanted
        pick_ref[pl.ds(pl.multiple_of(at, ROWS), ROWS), :] = here.astype(f32).astype(bf16)

    for n in range(chunks):
        copies[n].wait()
        x = dequantized(geno_ref.at[n], scales_ref, first + n * rows)
        out_ref[n * rows : (n + 1) * rows, :] = dot(x, pick_ref[...]).astype(bf16)


def select(own, table, packed, geno, index, params):
    samples, width = geno.shape[0] // 2, geno.shape[1]
    held = packed.shape[0] * CAP
    chunks = 2
    vmem = pl.BlockSpec(memory_space=pltpu.VMEM)
    return pl.pallas_call(
        functools.partial(select_kernel, own),
        in_specs=[
            pl.BlockSpec(memory_space=pltpu.SMEM),
            vmem,
            vmem,
            pl.BlockSpec(memory_space=pltpu.HBM),
        ],
        out_specs=vmem,
        out_shape=jax.ShapeDtypeStruct((samples, held), bf16),
        scratch_shapes=[
            pltpu.VMEM(index.shape, f32),
            pltpu.VMEM((width, held), bf16),
            pltpu.VMEM((chunks, samples // chunks, width), bf16),
            pltpu.SemaphoreType.DMA((chunks,)),
        ],
        compiler_params=params,
        cost_estimate=pl.CostEstimate(
            flops=2 * samples * width * held, bytes_accessed=2 * samples * width, transcendentals=0
        ),
        name="select",
    )(table, packed, index, geno)


def pick_kernel(
    inv_root, own_ref, one_ref, two_ref, three_ref, packed_ref, scores_ref, pay_ref
):
    scores = ((own_ref[...] + two_ref[...]) + (one_ref[...] + three_ref[...])) * inv_root
    scores_ref[...] = scores
    wanted = column_row(packed_ref[...])
    stacked = jnp.concatenate(thirds(scores), 0)
    phenos, width = scores.shape
    total = jnp.zeros((stacked.shape[0], wanted.shape[1]), f32)
    for at in range(0, width, ROWS):
        here = iota((ROWS, wanted.shape[1]), 0) + (at + 1) == wanted
        total += dot(stacked[:, at : at + ROWS], here.astype(f32).astype(bf16))
    held = total[:phenos] + total[phenos : 2 * phenos] + total[2 * phenos :]
    for t in range(wanted.shape[1] // LANES):
        pay_ref[8 * t : 8 * t + 8, :] = swapped(held[:, t * LANES : (t + 1) * LANES])


def pick(parts, packed, inv_root):
    return pl.pallas_call(
        functools.partial(pick_kernel, inv_root),
        out_shape=(
            jax.ShapeDtypeStruct(parts[0].shape, f32),
            jax.ShapeDtypeStruct((packed.shape[0] * HALF, LANES), f32),
        ),
        compiler_params=SMALL,
        name="pick",
    )(*parts, packed)


def direction_step(data, serial_ref, holder_ref, inverse_ref, advance, wide_ref, d_ref, pay_ref):
    fit = serial_ref.shape[1]
    holders = data.shape[0] // HALF
    spread, mask = slot_maps(serial_ref[...], holder_ref[...], holders)
    high, mid, low = thirds(data)
    placed = (dot(high, spread) + dot(mid, spread) + dot(low, spread)) * mask
    placed = jnp.sum(placed.reshape(-1, 2 * HALF, 2 * fit), 0)
    arrived = placed[:HALF] + placed[HALF:]
    inner = advance(arrived)
    wide_ref[:HALF, :] = inner[:, :fit]
    wide_ref[HALF:, :] = inner[:, fit:]
    blocks, size = inverse_ref.shape[0], inverse_ref.shape[1]
    for b in range(blocks):
        moved = dot_t(
            wide_ref[:, b * size : (b + 1) * size], inverse_ref[b], precision=lax.Precision.HIGHEST
        )
        moved = moved.astype(bf16).astype(f32)
        d_ref[:, b * size : (b + 1) * size] = moved[:HALF]
        d_ref[:, fit + b * size : fit + (b + 1) * size] = moved[HALF:]
    d = d_ref[...]
    d = jnp.concatenate([d, d], 0)
    d = jnp.broadcast_to(d[None], (holders * HALF // d.shape[0], *d.shape)).reshape(mask.shape)
    pay_ref[...] = dot_t((d * mask).astype(bf16), spread)


def first_owner_kernel(
    data_ref,
    serial_ref,
    holder_ref,
    inverse_ref,
    beta_ref,
    columns_hbm,
    pay_ref,
    b_ref,
    d_ref,
    g_ref,
    columns_ref,
    wide_ref,
    sem,
):
    copy = pltpu.make_async_copy(columns_hbm, columns_ref, sem)
    copy.start()
    fit = serial_ref.shape[1]
    active = beta_ref.shape[1]
    b_ref[...] = jnp.zeros_like(b_ref)
    b_ref[:, :active] = beta_ref[:HALF]
    b_ref[:, fit : fit + active] = beta_ref[HALF:]

    def advance(arrived):
        g_ref[...] = arrived
        return arrived - penalty * b_ref[...]

    direction_step(
        data_ref[...], serial_ref, holder_ref, inverse_ref, advance, wide_ref, d_ref, pay_ref
    )
    copy.wait()


def owner_kernel(
    data_ref,
    serial_ref,
    holder_ref,
    inverse_ref,
    b_in,
    d_in,
    g_in,
    resid_in,
    update_ref,
    pay_ref,
    b_ref,
    d_ref,
    resid_ref,
    g_ref,
    wide_ref,
    sum_ref,
    rows_ref,
    scalar_ref,
):
    fit = serial_ref.shape[1]
    chunk = sum_ref.shape[0]
    total = data_ref[:chunk, :]
    for at in range(chunk, data_ref.shape[0], chunk):
        total = total + data_ref[at : at + chunk, :]
    sum_ref[...] = total
    for k in range(chunk // (HALF + 1)):
        at = k * (HALF + 1)
        rows_ref[k * HALF : (k + 1) * HALF, :] = sum_ref[at : at + HALF, :]
        if k < scalar_ref.shape[0]:
            scalar_ref[k : k + 1, :] = sum_ref[at + HALF : at + HALF + 1, :]
    factor = scalar_ref[:, :1] / (scalar_ref[:, CAP : CAP + 1] + epsilon)
    resid_ref[...] = resid_in[...] - factor * update_ref[...]
    low = iota((HALF, 2 * fit), 1) < fit
    factor = jnp.where(low, factor[:HALF], factor[HALF:])

    def advance(arrived):
        g_ref[...] = g_in[...] - factor * arrived
        b_ref[...] = b_in[...] + factor * d_in[...]
        return g_ref[...] - penalty * b_ref[...]

    direction_step(
        rows_ref[...], serial_ref, holder_ref, inverse_ref, advance, wide_ref, d_ref, pay_ref
    )


def owner_first(data, serial, holder, inverse, beta, columns):
    fit = serial.shape[1]
    held = jax.ShapeDtypeStruct((HALF, 2 * fit), f32)
    vmem = pl.BlockSpec(memory_space=pltpu.VMEM)
    return pl.pallas_call(
        first_owner_kernel,
        in_specs=[vmem] * 5 + [pl.BlockSpec(memory_space=pltpu.HBM)],
        out_specs=(vmem,) * 5,
        out_shape=(
            jax.ShapeDtypeStruct(data.shape, f32),
            held,
            held,
            held,
            jax.ShapeDtypeStruct(columns.shape, columns.dtype),
        ),
        scratch_shapes=[pltpu.VMEM((2 * HALF, fit), f32), pltpu.SemaphoreType.DMA],
        compiler_params=MEDIUM,
        name="owner_first",
    )(data, serial, holder, inverse, beta, columns)


def owner_next(data, serial, holder, inverse, state, resid, update, final):
    fit = serial.shape[1]
    phenos = resid.shape[0]
    held = jax.ShapeDtypeStruct((HALF, 2 * fit), f32)
    rows = lax.axis_size(VAR) * HALF
    pay = jax.ShapeDtypeStruct((rows, LANES), f32)
    new_resid = jax.ShapeDtypeStruct(resid.shape, f32)
    return pl.pallas_call(
        owner_kernel,
        out_shape=(pay, held, held, new_resid) + (() if final else (held,)),
        scratch_shapes=([pltpu.VMEM(held.shape, f32)] if final else [])
        + [
            pltpu.VMEM((phenos, fit), f32),
            pltpu.VMEM((rows // HALF * (HALF + 1), LANES), f32),
            pltpu.VMEM((rows, LANES), f32),
            pltpu.VMEM((phenos, LANES), f32),
        ],
        compiler_params=SMALL,
        name="owner_next",
    )(data, serial, holder, inverse, *state, resid, update)


def update_kernel(pay_ref, columns_ref, out_ref):
    packed = jnp.concatenate(
        [swapped(pay_ref[at : at + 8, :]) for at in range(0, pay_ref.shape[0], 8)], 1
    ).astype(bf16)
    for at in range(0, out_ref.shape[1], ROWS):
        out_ref[:, at : at + ROWS] = dot_t(packed, columns_ref[at : at + ROWS, :])


def partial_update(pay, columns):
    samples, held = columns.shape
    return pl.pallas_call(
        update_kernel,
        out_shape=jax.ShapeDtypeStruct((2 * HALF, samples), f32),
        compiler_params=SMALL,
        cost_estimate=pl.CostEstimate(
            flops=512 * samples * held, bytes_accessed=2 * samples * held, transcendentals=0
        ),
        name="update",
    )(pay, columns)


def spread_kernel(keep_ref, arrived_ref, out_ref):
    out_ref[...] = jnp.broadcast_to((keep_ref[...] + arrived_ref[...])[None], out_ref.shape)


def spread(keep, arrived, copies):
    return pl.pallas_call(
        spread_kernel,
        out_shape=jax.ShapeDtypeStruct((copies, *keep.shape), f32),
        compiler_params=SMALL,
        name="spread",
    )(keep, arrived)


def total_kernel(parts_ref, out_ref):
    total = parts_ref[0]
    for n in range(1, parts_ref.shape[0]):
        total = total + parts_ref[n]
    out_ref[...] = total


def total(parts):
    return pl.pallas_call(
        total_kernel,
        out_shape=jax.ShapeDtypeStruct(parts.shape[1:], f32),
        compiler_params=SMALL,
        name="total",
    )(parts)


def whole_update(inv_root, core_ref, mine_ref, other_ref):
    first = core_ref[:, :1] == 0
    mine, other = mine_ref[...] * inv_root, other_ref[...] * inv_root
    return jnp.concatenate([jnp.where(first, mine, other), jnp.where(first, other, mine)], 1)


def step_sums(resid, update):
    cross = jnp.sum(resid * update, 1, keepdims=True)
    square = jnp.sum(update * update, 1, keepdims=True)
    return jnp.where(iota((update.shape[0], LANES), 1) < CAP, cross, square)


def two_parts(update):
    high = update.astype(bf16)
    return jnp.concatenate([high, (update - high.astype(f32)).astype(bf16)], 0)


def gradient_kernel(inv_root, mine_ref, columns_ref, out_ref):
    out_ref[...] = dot(two_parts(mine_ref[...] * inv_root), columns_ref[...])


def own_gradient(mine, columns, inv_root):
    samples, held = columns.shape
    return pl.pallas_call(
        functools.partial(gradient_kernel, inv_root),
        out_shape=jax.ShapeDtypeStruct((2 * mine.shape[0], held), f32),
        compiler_params=SMALL,
        cost_estimate=pl.CostEstimate(
            flops=512 * samples * held, bytes_accessed=2 * samples * held, transcendentals=0
        ),
        name="gradient",
    )(mine, columns)


def descent_kernel(
    inv_root,
    rank_ref,
    core_ref,
    mine_ref,
    other_ref,
    resid_ref,
    own_ref,
    columns_ref,
    out_ref,
    update_ref,
):
    update = whole_update(inv_root, core_ref, mine_ref, other_ref)
    update_ref[...] = update
    phenos = update.shape[0]
    grad = own_ref[...] + dot(two_parts(other_ref[...] * inv_root), columns_ref[...])
    grad = (grad[:phenos] + grad[phenos:]) * inv_root
    both = step_sums(resid_ref[...], update)
    mine = iota(both.shape, 0) == lax.rem(rank_ref[...], phenos)
    row = jnp.sum(jnp.where(mine, both, 0.0), 0, keepdims=True)
    chunk = HALF + 1
    owners = grad.shape[1] // CAP
    copies = out_ref.shape[0] // (chunk * owners)
    for t in range(owners // 2):
        pair = swapped(grad[:, t * LANES : (t + 1) * LANES])
        for n in range(copies):
            at = (n * owners + 2 * t) * chunk
            out_ref[at : at + HALF, :] = pair[:HALF]
            out_ref[at + HALF : at + HALF + 1, :] = row
            out_ref[at + chunk : at + chunk + HALF, :] = pair[HALF:]
            out_ref[at + chunk + HALF : at + 2 * chunk, :] = row


def descent(rank, core, mine, other, resid, own, columns, inv_root, copies):
    out = (copies * (columns.shape[1] // CAP) * (HALF + 1), LANES)
    return pl.pallas_call(
        functools.partial(descent_kernel, inv_root),
        out_shape=(jax.ShapeDtypeStruct(out, f32), jax.ShapeDtypeStruct(resid.shape, f32)),
        compiler_params=SMALL,
        name="descent",
    )(rank, core, mine, other, resid, own, columns)


def settle_kernel(inv_root, core_ref, mine_ref, resid_ref, sums_ref):
    half = mine_ref.shape[1]
    resid = jnp.where(core_ref[:, :1] == 0, resid_ref[:, :half], resid_ref[:, half:])
    sums = step_sums(resid, mine_ref[...] * inv_root)
    sums_ref[...] = jnp.broadcast_to(sums[None], sums_ref.shape)


def settle(core, mine, resid, inv_root, copies):
    return pl.pallas_call(
        functools.partial(settle_kernel, inv_root),
        out_shape=jax.ShapeDtypeStruct((copies, resid.shape[0], LANES), f32),
        compiler_params=SMALL,
        name="settle",
    )(core, mine, resid)


def last_kernel(
    inv_root, sums_ref, core_ref, mine_ref, other_ref, b_ref, d_ref, resid_ref, coeffs_ref, out_ref
):
    phenos, fit = coeffs_ref.shape
    total = sums_ref[0]
    for j in range(1, sums_ref.shape[0]):
        total = total + sums_ref[j]
    factor = total[:, :1] / (total[:, CAP : CAP + 1] + epsilon)
    for half in range(2):
        rows = slice(half * HALF, (half + 1) * HALF)
        cols = slice(half * fit, (half + 1) * fit)
        coeffs_ref[rows, :] = b_ref[:, cols] + factor[rows] * d_ref[:, cols]
    update = whole_update(inv_root, core_ref, mine_ref, other_ref)
    out_ref[...] = resid_ref[...] - factor * update


def last(sums, core, mine, other, coeffs, direction, resid, inv_root):
    phenos = resid.shape[0]
    return pl.pallas_call(
        functools.partial(last_kernel, inv_root),
        out_shape=(
            jax.ShapeDtypeStruct((phenos, coeffs.shape[1] // 2), f32),
            jax.ShapeDtypeStruct(resid.shape, f32),
        ),
        compiler_params=SMALL,
        name="last",
    )(sums, core, mine, other, coeffs, direction, resid)


def exchange(pay, axes):
    count = lax.axis_size(axes)
    rows = pay.shape[0] // count
    shape = (count, rows, LANES) if rows == HALF else (count, 1, rows * LANES)
    return lax.all_to_all(
        pay.reshape(shape), axes, split_axis=0, concat_axis=0, tiled=True
    ).reshape(pay.shape)


def shifted(x, axis, by=1):
    size = lax.axis_size(axis)
    return lax.ppermute(x, axis, [(i, (i + by) % size) for i in range(size)])


def on_device(
    geno, scale_index, scale_table, residual, beta_active, block_inverse, active_ids, admit_ids
):
    holders = lax.axis_size(VAR)
    samples, width = geno.shape
    copies = lax.axis_size(SAMP)
    inv_root = 1.0 / math.sqrt(samples * copies)

    part, holder, serial, packed, rank, core = screen(
        scale_table, geno, scale_index, residual, active_ids, admit_ids
    )
    part = part + shifted(part, "y_hi")
    parts = [part] + [shifted(part, "x", n) for n in range(1, lax.axis_size("x"))]
    packed = lax.all_to_all(
        packed.reshape(holders, 1, LANES), VAR, split_axis=0, concat_axis=0, tiled=True
    ).reshape(holders, LANES)

    away = select(False, scale_table, packed, geno, scale_index, MEDIUM)
    parts, away = lax.optimization_barrier((parts, away))
    scores, pay = pick(parts, packed, inv_root)
    pay, packed = lax.optimization_barrier((pay, packed))
    home = select(True, scale_table, packed, geno, scale_index, WIDE)
    pay, *state, home = owner_first(
        exchange(pay, VAR), serial, holder, block_inverse, beta_active, home
    )
    current = residual
    for pass_index in range(PASSES):
        pay = exchange(pay, VAR)
        arrived = shifted(partial_update(pay, away), "core")
        mine = spread(partial_update(pay, home), arrived, lax.axis_size(CHIPS))
        mine = total(lax.all_to_all(mine, CHIPS, split_axis=0, concat_axis=0, tiled=True))
        other = shifted(mine, "core")
        if pass_index + 1 == PASSES:
            break
        own = own_gradient(mine, home, inv_root)
        data, update = descent(rank, core, mine, other, current, own, away, inv_root, copies)
        pay, coeffs, direction, current, *gradient = owner_next(
            exchange(data, SAMP + VAR),
            serial,
            holder,
            block_inverse,
            state,
            current,
            update,
            pass_index + 2 == PASSES,
        )
        state = (coeffs, direction, *gradient)

    sums = settle(core, mine, current, inv_root, 2 * copies)
    sums = lax.all_to_all(sums, ("core",) + SAMP, split_axis=0, concat_axis=0, tiled=True)
    return (scores, *last(sums, core, mine, other, coeffs, direction, current, inv_root))


def solution(mesh):
    torus = Mesh(mesh.devices.reshape(2, 4, 2, 2, 4), VAR + SAMP)
    placed = (
        P(SAMP, VAR),
        P(SAMP, VAR),
        P(),
        P(None, SAMP),
        P(None, VAR),
        P(VAR, None, None),
        P(VAR),
        P(VAR),
    )
    return jax.shard_map(
        on_device,
        mesh=torus,
        in_specs=placed,
        out_specs=(P(None, VAR), P(None, VAR), P(None, SAMP)),
        check_vma=False,
    )
```

```python
import functools
import math

import jax
import jax.numpy as jnp
from jax import lax
from jax.experimental import pallas as pl
from jax.experimental.pallas import tpu as pltpu
from jax.sharding import Mesh
from jax.sharding import PartitionSpec as P

PASSES = 3
VAR = ("y_lo", "z", "core")
SAMP = ("y_hi", "x")
CHIPS = ("y_lo", "z")

CAP = 64
LANES = 128
ROWS = 256
HALF = 4

penalty = 0.5
epsilon = 1e-06
SMALL = pltpu.CompilerParams(vmem_limit_bytes=12 * 1024 * 1024)
MEDIUM = pltpu.CompilerParams(vmem_limit_bytes=50 * 1024 * 1024)
WIDE = pltpu.CompilerParams(vmem_limit_bytes=52 * 1024 * 1024)
LARGE = pltpu.CompilerParams(vmem_limit_bytes=60 * 1024 * 1024)
f32 = jnp.float32
bf16 = jnp.bfloat16


def iota(shape, dim):
    return lax.broadcasted_iota(jnp.int32, shape, dim)


def dot(a, b, **kw):
    return jnp.dot(a, b, preferred_element_type=f32, **kw)


def dot_t(a, b, **kw):
    return lax.dot_general(a, b, (((1,), (1,)), ((), ())), preferred_element_type=f32, **kw)


def thirds(x):
    high = x.astype(bf16)
    rest = x - high.astype(f32)
    mid = rest.astype(bf16)
    return high, mid, (rest - mid.astype(f32)).astype(bf16)


def swapped(x):
    here = (iota(x.shape, 0) // HALF) == (iota(x.shape, 1) // CAP)
    return jnp.where(here, x, pltpu.roll(pltpu.roll(x, HALF, 0), CAP, 1))


def column_row(packed):
    low = iota((1, LANES), 1) < CAP
    return jnp.concatenate(
        [
            jnp.where(low, packed[t : t + 1], packed[t + 1 : t + 2])
            for t in range(0, packed.shape[0], 2)
        ],
        1,
    )


def slot_maps(serial, holder, holders):
    fit = serial.shape[1]
    serial2 = jnp.concatenate([serial, serial], 1)
    holder2 = jnp.concatenate([holder, holder], 1)
    shape = (2 * CAP, 2 * fit)
    rows, cols = iota(shape, 0), iota(shape, 1)
    spread = ((rows // CAP) == (cols // fit)) & ((rows % CAP) == serial2)
    mask = (iota((holders * HALF, 2 * fit), 0) // HALF) == holder2
    return spread.astype(f32).astype(bf16), mask.astype(f32)


def lay_out(width, active_ref, admit_ref, holder_ref, serial_ref, packed_ref, ids_ref):
    holders = packed_ref.shape[0]
    fit = holder_ref.shape[1]
    active = active_ref.shape[1]
    ids_ref[:, :active] = active_ref[...]
    ids_ref[:, active:] = admit_ref[...]
    ids = ids_ref[...]
    holder = ids // width
    holder_ref[...] = holder
    marks = (iota((holders, fit), 0) == holder).astype(f32)
    earlier = (iota((fit, fit), 0) < iota((fit, fit), 1)).astype(f32).astype(bf16)
    before = dot(marks.astype(bf16), earlier)
    serial = jnp.sum(before * marks, 0, keepdims=True).astype(jnp.int32)
    serial_ref[...] = serial
    spread, _ = slot_maps(serial, holder, holders)
    marks2 = jnp.concatenate([marks, marks], 1)
    column = ids - holder * width + 1
    parts = []
    for piece in (column // LANES, column % LANES):
        row = piece.astype(f32)
        row = jnp.concatenate([row, row], 1)
        parts.append(dot_t((marks2 * row).astype(bf16), spread))
    packed_ref[...] = (parts[0] * LANES + parts[1]).astype(jnp.int32)


def look_up(table_ref, index_ref, scales_ref):
    index = index_ref[...]
    scales = jnp.full(index.shape, table_ref[0], f32)
    for level in range(1, table_ref.shape[0]):
        scales = jnp.where(index == level, table_ref[level], scales)
    scales_ref[...] = scales


def dequantized(geno_ref, scales_ref, first):
    rows = geno_ref.shape[0]
    group = 128
    out = []
    for g in range(rows // group):
        scale = scales_ref[pl.ds(first // group + g, 1), :]
        wide = geno_ref[g * group : (g + 1) * group, :].astype(f32) * scale
        out.append(wide.astype(bf16))
    return jnp.concatenate(out, 0)


def screen_kernel(
    table_ref,
    active_ref,
    admit_ref,
    index_hbm,
    resid_hbm,
    geno_hbm,
    out_ref,
    holder_ref,
    serial_ref,
    packed_ref,
    rank_ref,
    core_ref,
    index_ref,
    resid_ref,
    geno_ref,
    scales_ref,
    ids_ref,
    sems,
):
    chunks, rows, width = geno_ref.shape
    pieces = [(index_hbm, index_ref), (resid_hbm, resid_ref)]
    pieces += [(geno_hbm.at[pl.ds(n * rows, rows)], geno_ref.at[n]) for n in range(chunks)]
    copies = [pltpu.make_async_copy(*piece, sems.at[n]) for n, piece in enumerate(pieces)]
    for copy in copies:
        copy.start()
    rank_ref[...] = jnp.full(rank_ref.shape, lax.axis_index(VAR), jnp.int32)
    core_ref[...] = jnp.full(core_ref.shape, lax.axis_index("core"), jnp.int32)
    lay_out(width, active_ref, admit_ref, holder_ref, serial_ref, packed_ref, ids_ref)
    copies[0].wait()
    look_up(table_ref, index_ref, scales_ref)
    copies[1].wait()
    scores = jnp.zeros(out_ref.shape, f32)
    for n in range(chunks):
        copies[2 + n].wait()
        x = dequantized(geno_ref.at[n], scales_ref, n * rows)
        scores += dot(resid_ref[:, n * rows : (n + 1) * rows].astype(bf16), x)
    out_ref[...] = scores


def screen(table, geno, index, resid, active_ids, admit_ids):
    samples, width = geno.shape
    phenos = resid.shape[0]
    active_ids, admit_ids = active_ids[None], admit_ids[None]
    fit = active_ids.size + admit_ids.size
    tile = (2 * HALF, LANES)
    integers = [(1, fit), (1, fit), (lax.axis_size(VAR), LANES), tile, tile]
    chunks = 8
    vmem = pl.BlockSpec(memory_space=pltpu.VMEM)
    hbm = pl.BlockSpec(memory_space=pltpu.HBM)
    return pl.pallas_call(
        screen_kernel,
        in_specs=[pl.BlockSpec(memory_space=pltpu.SMEM), vmem, vmem, hbm, hbm, hbm],
        out_shape=[jax.ShapeDtypeStruct((phenos, width), f32)]
        + [jax.ShapeDtypeStruct(shape, jnp.int32) for shape in integers],
        scratch_shapes=[
            pltpu.VMEM(index.shape, jnp.int32),
            pltpu.VMEM(resid.shape, f32),
            pltpu.VMEM((chunks, samples // chunks, width), bf16),
            pltpu.VMEM(index.shape, f32),
            pltpu.VMEM((1, fit), jnp.int32),
            pltpu.SemaphoreType.DMA((2 + chunks,)),
        ],
        compiler_params=LARGE,
        cost_estimate=pl.CostEstimate(
            flops=2 * phenos * samples * width, bytes_accessed=2 * samples * width, transcendentals=0
        ),
        name="screen",
    )(table, active_ids, admit_ids, index, resid, geno)


def select_kernel(
    own,
    table_ref,
    packed_ref,
    index_ref,
    geno_hbm,
    out_ref,
    scales_ref,
    pick_ref,
    geno_ref,
    sems,
    piece_ref=None,
    out_sems=None,
):
    samples = out_ref.shape[0]
    chunks, rows = geno_ref.shape[:2]
    core = lax.axis_index("core")
    first = (core if own else 1 - core) * samples
    copies = []
    for n in range(chunks):
        at = pl.multiple_of(first + n * rows, rows)
        copies.append(
            pltpu.make_async_copy(geno_hbm.at[pl.ds(at, rows)], geno_ref.at[n], sems.at[n])
        )
        copies[n].start()
    look_up(table_ref, index_ref, scales_ref)
    wanted = column_row(packed_ref[...])

    @pl.loop(0, pick_ref.shape[0], step=ROWS)
    def _(at):
        here = iota((ROWS, pick_ref.shape[1]), 0) + (at + 1) == wanted
        pick_ref[pl.ds(pl.multiple_of(at, ROWS), ROWS), :] = here.astype(f32).astype(bf16)

    outs = []
    for n in range(chunks):
        copies[n].wait()
        x = dequantized(geno_ref.at[n], scales_ref, first + n * rows)
        piece = dot(x, pick_ref[...]).astype(bf16)
        there = pl.ds(n * rows, rows)
        if piece_ref is None:
            out_ref[there, :] = piece
        else:
            piece_ref[n] = piece
            outs.append(
                pltpu.make_async_copy(piece_ref.at[n], out_ref.at[there], out_sems.at[n])
            )
            outs[n].start()
    for out in outs:
        out.wait()


def select(own, table, packed, geno, index, params):
    samples, width = geno.shape[0] // 2, geno.shape[1]
    held = packed.shape[0] * CAP
    chunks = 4 if own else 2
    rows = samples // chunks
    vmem = pl.BlockSpec(memory_space=pltpu.VMEM)
    pieces = [pltpu.VMEM((chunks, rows, held), bf16), pltpu.SemaphoreType.DMA((chunks,))]
    return pl.pallas_call(
        functools.partial(select_kernel, own),
        in_specs=[
            pl.BlockSpec(memory_space=pltpu.SMEM),
            vmem,
            vmem,
            pl.BlockSpec(memory_space=pltpu.HBM),
        ],
        out_specs=pl.BlockSpec(memory_space=pltpu.HBM) if own else vmem,
        out_shape=jax.ShapeDtypeStruct((samples, held), bf16),
        scratch_shapes=[
            pltpu.VMEM(index.shape, f32),
            pltpu.VMEM((width, held), bf16),
            pltpu.VMEM((chunks, rows, width), bf16),
            pltpu.SemaphoreType.DMA((chunks,)),
            *(pieces if own else ()),
        ],
        compiler_params=params,
        cost_estimate=pl.CostEstimate(
            flops=2 * samples * width * held, bytes_accessed=2 * samples * width, transcendentals=0
        ),
        name="select",
    )(table, packed, index, geno)


def pick_kernel(
    inv_root, own_ref, one_ref, two_ref, three_ref, packed_ref, scores_ref, pay_ref
):
    scores = ((own_ref[...] + two_ref[...]) + (one_ref[...] + three_ref[...])) * inv_root
    scores_ref[...] = scores
    wanted = column_row(packed_ref[...])
    stacked = jnp.concatenate(thirds(scores), 0)
    phenos, width = scores.shape
    total = jnp.zeros((stacked.shape[0], wanted.shape[1]), f32)
    for at in range(0, width, ROWS):
        here = iota((ROWS, wanted.shape[1]), 0) + (at + 1) == wanted
        total += dot(stacked[:, at : at + ROWS], here.astype(f32).astype(bf16))
    held = total[:phenos] + total[phenos : 2 * phenos] + total[2 * phenos :]
    for t in range(wanted.shape[1] // LANES):
        pay_ref[8 * t : 8 * t + 8, :] = swapped(held[:, t * LANES : (t + 1) * LANES])


def pick(parts, packed, inv_root):
    return pl.pallas_call(
        functools.partial(pick_kernel, inv_root),
        out_shape=(
            jax.ShapeDtypeStruct(parts[0].shape, f32),
            jax.ShapeDtypeStruct((packed.shape[0] * HALF, LANES), f32),
        ),
        compiler_params=SMALL,
        name="pick",
    )(*parts, packed)


def direction_step(data, serial_ref, holder_ref, inverse_ref, advance, wide_ref, d_ref, pay_ref):
    fit = serial_ref.shape[1]
    holders = data.shape[0] // HALF
    spread, mask = slot_maps(serial_ref[...], holder_ref[...], holders)
    high, mid, low = thirds(data)
    placed = (dot(high, spread) + dot(mid, spread) + dot(low, spread)) * mask
    placed = jnp.sum(placed.reshape(-1, 2 * HALF, 2 * fit), 0)
    arrived = placed[:HALF] + placed[HALF:]
    inner = advance(arrived)
    wide_ref[:HALF, :] = inner[:, :fit]
    wide_ref[HALF:, :] = inner[:, fit:]
    blocks, size = inverse_ref.shape[0], inverse_ref.shape[1]
    for b in range(blocks):
        moved = dot_t(
            wide_ref[:, b * size : (b + 1) * size], inverse_ref[b], precision=lax.Precision.HIGHEST
        )
        moved = moved.astype(bf16).astype(f32)
        d_ref[:, b * size : (b + 1) * size] = moved[:HALF]
        d_ref[:, fit + b * size : fit + (b + 1) * size] = moved[HALF:]
    d = d_ref[...]
    d = jnp.concatenate([d, d], 0)
    d = jnp.broadcast_to(d[None], (holders * HALF // d.shape[0], *d.shape)).reshape(mask.shape)
    pay_ref[...] = dot_t((d * mask).astype(bf16), spread)


def first_owner_kernel(
    data_ref,
    serial_ref,
    holder_ref,
    inverse_ref,
    beta_ref,
    columns_hbm,
    pay_ref,
    b_ref,
    d_ref,
    g_ref,
    columns_ref,
    wide_ref,
    sem,
):
    copy = pltpu.make_async_copy(columns_hbm, columns_ref, sem)
    copy.start()
    fit = serial_ref.shape[1]
    active = beta_ref.shape[1]
    b_ref[...] = jnp.zeros_like(b_ref)
    b_ref[:, :active] = beta_ref[:HALF]
    b_ref[:, fit : fit + active] = beta_ref[HALF:]

    def advance(arrived):
        g_ref[...] = arrived
        return arrived - penalty * b_ref[...]

    direction_step(
        data_ref[...], serial_ref, holder_ref, inverse_ref, advance, wide_ref, d_ref, pay_ref
    )
    copy.wait()


def owner_kernel(
    data_ref,
    serial_ref,
    holder_ref,
    inverse_ref,
    b_in,
    d_in,
    g_in,
    resid_in,
    update_ref,
    pay_ref,
    b_ref,
    d_ref,
    resid_ref,
    g_ref,
    wide_ref,
    sum_ref,
    rows_ref,
    scalar_ref,
):
    fit = serial_ref.shape[1]
    chunk = sum_ref.shape[0]
    total = data_ref[:chunk, :]
    for at in range(chunk, data_ref.shape[0], chunk):
        total = total + data_ref[at : at + chunk, :]
    sum_ref[...] = total
    for k in range(chunk // (HALF + 1)):
        at = k * (HALF + 1)
        rows_ref[k * HALF : (k + 1) * HALF, :] = sum_ref[at : at + HALF, :]
        if k < scalar_ref.shape[0]:
            scalar_ref[k : k + 1, :] = sum_ref[at + HALF : at + HALF + 1, :]
    factor = scalar_ref[:, :1] / (scalar_ref[:, CAP : CAP + 1] + epsilon)
    resid_ref[...] = resid_in[...] - factor * update_ref[...]
    low = iota((HALF, 2 * fit), 1) < fit
    factor = jnp.where(low, factor[:HALF], factor[HALF:])

    def advance(arrived):
        g_ref[...] = g_in[...] - factor * arrived
        b_ref[...] = b_in[...] + factor * d_in[...]
        return g_ref[...] - penalty * b_ref[...]

    direction_step(
        rows_ref[...], serial_ref, holder_ref, inverse_ref, advance, wide_ref, d_ref, pay_ref
    )


def owner_first(data, serial, holder, inverse, beta, columns):
    fit = serial.shape[1]
    held = jax.ShapeDtypeStruct((HALF, 2 * fit), f32)
    vmem = pl.BlockSpec(memory_space=pltpu.VMEM)
    return pl.pallas_call(
        first_owner_kernel,
        in_specs=[vmem] * 5 + [pl.BlockSpec(memory_space=pltpu.HBM)],
        out_specs=(vmem,) * 5,
        out_shape=(
            jax.ShapeDtypeStruct(data.shape, f32),
            held,
            held,
            held,
            jax.ShapeDtypeStruct(columns.shape, columns.dtype),
        ),
        scratch_shapes=[pltpu.VMEM((2 * HALF, fit), f32), pltpu.SemaphoreType.DMA],
        compiler_params=MEDIUM,
        name="owner_first",
    )(data, serial, holder, inverse, beta, columns)


def owner_next(data, serial, holder, inverse, state, resid, update, final):
    fit = serial.shape[1]
    phenos = resid.shape[0]
    held = jax.ShapeDtypeStruct((HALF, 2 * fit), f32)
    rows = lax.axis_size(VAR) * HALF
    pay = jax.ShapeDtypeStruct((rows, LANES), f32)
    new_resid = jax.ShapeDtypeStruct(resid.shape, f32)
    return pl.pallas_call(
        owner_kernel,
        out_shape=(pay, held, held, new_resid) + (() if final else (held,)),
        scratch_shapes=([pltpu.VMEM(held.shape, f32)] if final else [])
        + [
            pltpu.VMEM((phenos, fit), f32),
            pltpu.VMEM((rows // HALF * (HALF + 1), LANES), f32),
            pltpu.VMEM((rows, LANES), f32),
            pltpu.VMEM((phenos, LANES), f32),
        ],
        compiler_params=SMALL,
        name="owner_next",
    )(data, serial, holder, inverse, *state, resid, update)


def update_kernel(pay_ref, columns_ref, out_ref):
    packed = jnp.concatenate(
        [swapped(pay_ref[at : at + 8, :]) for at in range(0, pay_ref.shape[0], 8)], 1
    ).astype(bf16)
    for at in range(0, out_ref.shape[1], ROWS):
        out_ref[:, at : at + ROWS] = dot_t(packed, columns_ref[at : at + ROWS, :])


def partial_update(pay, columns):
    samples, held = columns.shape
    return pl.pallas_call(
        update_kernel,
        out_shape=jax.ShapeDtypeStruct((2 * HALF, samples), f32),
        compiler_params=SMALL,
        cost_estimate=pl.CostEstimate(
            flops=512 * samples * held, bytes_accessed=2 * samples * held, transcendentals=0
        ),
        name="update",
    )(pay, columns)


def spread_kernel(keep_ref, arrived_ref, out_ref):
    out_ref[...] = jnp.broadcast_to((keep_ref[...] + arrived_ref[...])[None], out_ref.shape)


def spread(keep, arrived, copies):
    return pl.pallas_call(
        spread_kernel,
        out_shape=jax.ShapeDtypeStruct((copies, *keep.shape), f32),
        compiler_params=SMALL,
        name="spread",
    )(keep, arrived)


def total_kernel(parts_ref, out_ref):
    total = parts_ref[0]
    for n in range(1, parts_ref.shape[0]):
        total = total + parts_ref[n]
    out_ref[...] = total


def total(parts):
    return pl.pallas_call(
        total_kernel,
        out_shape=jax.ShapeDtypeStruct(parts.shape[1:], f32),
        compiler_params=SMALL,
        name="total",
    )(parts)


def whole_update(inv_root, core_ref, mine_ref, other_ref):
    first = core_ref[:, :1] == 0
    mine, other = mine_ref[...] * inv_root, other_ref[...] * inv_root
    return jnp.concatenate([jnp.where(first, mine, other), jnp.where(first, other, mine)], 1)


def step_sums(resid, update):
    cross = jnp.sum(resid * update, 1, keepdims=True)
    square = jnp.sum(update * update, 1, keepdims=True)
    return jnp.where(iota((update.shape[0], LANES), 1) < CAP, cross, square)


def two_parts(update):
    high = update.astype(bf16)
    return jnp.concatenate([high, (update - high.astype(f32)).astype(bf16)], 0)


def gradient_kernel(inv_root, mine_ref, columns_ref, out_ref):
    out_ref[...] = dot(two_parts(mine_ref[...] * inv_root), columns_ref[...])


def own_gradient(mine, columns, inv_root):
    samples, held = columns.shape
    return pl.pallas_call(
        functools.partial(gradient_kernel, inv_root),
        out_shape=jax.ShapeDtypeStruct((2 * mine.shape[0], held), f32),
        compiler_params=SMALL,
        cost_estimate=pl.CostEstimate(
            flops=512 * samples * held, bytes_accessed=2 * samples * held, transcendentals=0
        ),
        name="gradient",
    )(mine, columns)


def descent_kernel(
    inv_root,
    rank_ref,
    core_ref,
    mine_ref,
    other_ref,
    resid_ref,
    own_ref,
    columns_ref,
    out_ref,
    update_ref,
):
    update = whole_update(inv_root, core_ref, mine_ref, other_ref)
    update_ref[...] = update
    phenos = update.shape[0]
    grad = own_ref[...] + dot(two_parts(other_ref[...] * inv_root), columns_ref[...])
    grad = (grad[:phenos] + grad[phenos:]) * inv_root
    both = step_sums(resid_ref[...], update)
    mine = iota(both.shape, 0) == lax.rem(rank_ref[...], phenos)
    row = jnp.sum(jnp.where(mine, both, 0.0), 0, keepdims=True)
    chunk = HALF + 1
    owners = grad.shape[1] // CAP
    copies = out_ref.shape[0] // (chunk * owners)
    for t in range(owners // 2):
        pair = swapped(grad[:, t * LANES : (t + 1) * LANES])
        for n in range(copies):
            at = (n * owners + 2 * t) * chunk
            out_ref[at : at + HALF, :] = pair[:HALF]
            out_ref[at + HALF : at + HALF + 1, :] = row
            out_ref[at + chunk : at + chunk + HALF, :] = pair[HALF:]
            out_ref[at + chunk + HALF : at + 2 * chunk, :] = row


def descent(rank, core, mine, other, resid, own, columns, inv_root, copies):
    out = (copies * (columns.shape[1] // CAP) * (HALF + 1), LANES)
    return pl.pallas_call(
        functools.partial(descent_kernel, inv_root),
        out_shape=(jax.ShapeDtypeStruct(out, f32), jax.ShapeDtypeStruct(resid.shape, f32)),
        compiler_params=SMALL,
        name="descent",
    )(rank, core, mine, other, resid, own, columns)


def settle_kernel(inv_root, core_ref, mine_ref, resid_ref, sums_ref):
    half = mine_ref.shape[1]
    resid = jnp.where(core_ref[:, :1] == 0, resid_ref[:, :half], resid_ref[:, half:])
    sums = step_sums(resid, mine_ref[...] * inv_root)
    sums_ref[...] = jnp.broadcast_to(sums[None], sums_ref.shape)


def settle(core, mine, resid, inv_root, copies):
    return pl.pallas_call(
        functools.partial(settle_kernel, inv_root),
        out_shape=jax.ShapeDtypeStruct((copies, resid.shape[0], LANES), f32),
        compiler_params=SMALL,
        name="settle",
    )(core, mine, resid)


def last_kernel(
    inv_root, sums_ref, core_ref, mine_ref, other_ref, b_ref, d_ref, resid_ref, coeffs_ref, out_ref
):
    phenos, fit = coeffs_ref.shape
    total = sums_ref[0]
    for j in range(1, sums_ref.shape[0]):
        total = total + sums_ref[j]
    factor = total[:, :1] / (total[:, CAP : CAP + 1] + epsilon)
    for half in range(2):
        rows = slice(half * HALF, (half + 1) * HALF)
        cols = slice(half * fit, (half + 1) * fit)
        coeffs_ref[rows, :] = b_ref[:, cols] + factor[rows] * d_ref[:, cols]
    update = whole_update(inv_root, core_ref, mine_ref, other_ref)
    out_ref[...] = resid_ref[...] - factor * update


def last(sums, core, mine, other, coeffs, direction, resid, inv_root):
    phenos = resid.shape[0]
    return pl.pallas_call(
        functools.partial(last_kernel, inv_root),
        out_shape=(
            jax.ShapeDtypeStruct((phenos, coeffs.shape[1] // 2), f32),
            jax.ShapeDtypeStruct(resid.shape, f32),
        ),
        compiler_params=SMALL,
        name="last",
    )(sums, core, mine, other, coeffs, direction, resid)


def exchange(pay, axes):
    count = lax.axis_size(axes)
    rows = pay.shape[0] // count
    shape = (count, rows, LANES) if rows == HALF else (count, 1, rows * LANES)
    return lax.all_to_all(
        pay.reshape(shape), axes, split_axis=0, concat_axis=0, tiled=True
    ).reshape(pay.shape)


def shifted(x, axis, by=1):
    size = lax.axis_size(axis)
    return lax.ppermute(x, axis, [(i, (i + by) % size) for i in range(size)])


def on_device(
    geno, scale_index, scale_table, residual, beta_active, block_inverse, active_ids, admit_ids
):
    holders = lax.axis_size(VAR)
    samples, width = geno.shape
    copies = lax.axis_size(SAMP)
    inv_root = 1.0 / math.sqrt(samples * copies)

    part, holder, serial, packed, rank, core = screen(
        scale_table, geno, scale_index, residual, active_ids, admit_ids
    )
    part = part + shifted(part, "y_hi")
    parts = [part] + [shifted(part, "x", n) for n in range(1, lax.axis_size("x"))]
    packed = lax.all_to_all(
        packed.reshape(holders, 1, LANES), VAR, split_axis=0, concat_axis=0, tiled=True
    ).reshape(holders, LANES)

    away = select(False, scale_table, packed, geno, scale_index, MEDIUM)
    parts, away = lax.optimization_barrier((parts, away))
    scores, pay = pick(parts, packed, inv_root)
    pay, packed = lax.optimization_barrier((pay, packed))
    home = select(True, scale_table, packed, geno, scale_index, WIDE)
    pay, *state, home = owner_first(
        exchange(pay, VAR), serial, holder, block_inverse, beta_active, home
    )
    current = residual
    for pass_index in range(PASSES):
        pay = exchange(pay, VAR)
        arrived = shifted(partial_update(pay, away), "core")
        mine = spread(partial_update(pay, home), arrived, lax.axis_size(CHIPS))
        mine = total(lax.all_to_all(mine, CHIPS, split_axis=0, concat_axis=0, tiled=True))
        other = shifted(mine, "core")
        if pass_index + 1 == PASSES:
            break
        own = own_gradient(mine, home, inv_root)
        data, update = descent(rank, core, mine, other, current, own, away, inv_root, copies)
        pay, coeffs, direction, current, *gradient = owner_next(
            exchange(data, SAMP + VAR),
            serial,
            holder,
            block_inverse,
            state,
            current,
            update,
            pass_index + 2 == PASSES,
        )
        state = (coeffs, direction, *gradient)

    sums = settle(core, mine, current, inv_root, 2 * copies)
    sums, other = lax.optimization_barrier((sums, other))
    sums = lax.all_to_all(sums, ("core",) + SAMP, split_axis=0, concat_axis=0, tiled=True)
    return (scores, *last(sums, core, mine, other, coeffs, direction, current, inv_root))


def solution(mesh):
    torus = Mesh(mesh.devices.reshape(2, 4, 2, 2, 4), VAR + SAMP)
    placed = (
        P(SAMP, VAR),
        P(SAMP, VAR),
        P(),
        P(None, SAMP),
        P(None, VAR),
        P(VAR, None, None),
        P(VAR),
        P(VAR),
    )
    return jax.shard_map(
        on_device,
        mesh=torus,
        in_specs=placed,
        out_specs=(P(None, VAR), P(None, VAR), P(None, SAMP)),
        check_vma=False,
    )
```

```python
import functools
import math

import jax
import jax.numpy as jnp
from jax import lax
from jax.experimental import pallas as pl
from jax.experimental.pallas import tpu as pltpu
from jax.sharding import Mesh
from jax.sharding import PartitionSpec as P

PASSES = 3
VAR = ("y_lo", "z", "core")
SAMP = ("y_hi", "x")
CHIPS = ("y_lo", "z")

CAP = 64
LANES = 128
ROWS = 256
HALF = 4

penalty = 0.5
epsilon = 1e-06
SMALL = pltpu.CompilerParams(vmem_limit_bytes=12 * 1024 * 1024)
MEDIUM = pltpu.CompilerParams(vmem_limit_bytes=48 * 1024 * 1024)
WIDE = pltpu.CompilerParams(vmem_limit_bytes=53 * 1024 * 1024)
LARGE = pltpu.CompilerParams(vmem_limit_bytes=60 * 1024 * 1024)
f32 = jnp.float32
bf16 = jnp.bfloat16


def iota(shape, dim):
    return lax.broadcasted_iota(jnp.int32, shape, dim)


def dot(a, b, **kw):
    return jnp.dot(a, b, preferred_element_type=f32, **kw)


def dot_t(a, b, **kw):
    return lax.dot_general(a, b, (((1,), (1,)), ((), ())), preferred_element_type=f32, **kw)


def thirds(x):
    high = x.astype(bf16)
    rest = x - high.astype(f32)
    mid = rest.astype(bf16)
    return high, mid, (rest - mid.astype(f32)).astype(bf16)


def swapped(x):
    here = (iota(x.shape, 0) // HALF) == (iota(x.shape, 1) // CAP)
    return jnp.where(here, x, pltpu.roll(pltpu.roll(x, HALF, 0), CAP, 1))


def column_row(packed):
    low = iota((1, LANES), 1) < CAP
    return jnp.concatenate(
        [
            jnp.where(low, packed[t : t + 1], packed[t + 1 : t + 2])
            for t in range(0, packed.shape[0], 2)
        ],
        1,
    )


def slot_maps(serial, holder, holders):
    fit = serial.shape[1]
    serial2 = jnp.concatenate([serial, serial], 1)
    holder2 = jnp.concatenate([holder, holder], 1)
    shape = (2 * CAP, 2 * fit)
    rows, cols = iota(shape, 0), iota(shape, 1)
    spread = ((rows // CAP) == (cols // fit)) & ((rows % CAP) == serial2)
    mask = (iota((holders * HALF, 2 * fit), 0) // HALF) == holder2
    return spread.astype(f32).astype(bf16), mask.astype(f32)


def lay_out(width, active_ref, admit_ref, holder_ref, serial_ref, packed_ref, ids_ref):
    holders = packed_ref.shape[0]
    fit = holder_ref.shape[1]
    active = active_ref.shape[1]
    ids_ref[:, :active] = active_ref[...]
    ids_ref[:, active:] = admit_ref[...]
    ids = ids_ref[...]
    holder = ids // width
    holder_ref[...] = holder
    marks = (iota((holders, fit), 0) == holder).astype(f32)
    earlier = (iota((fit, fit), 0) < iota((fit, fit), 1)).astype(f32).astype(bf16)
    before = dot(marks.astype(bf16), earlier)
    serial = jnp.sum(before * marks, 0, keepdims=True).astype(jnp.int32)
    serial_ref[...] = serial
    spread, _ = slot_maps(serial, holder, holders)
    marks2 = jnp.concatenate([marks, marks], 1)
    column = ids - holder * width + 1
    parts = []
    for piece in (column // LANES, column % LANES):
        row = piece.astype(f32)
        row = jnp.concatenate([row, row], 1)
        parts.append(dot_t((marks2 * row).astype(bf16), spread))
    packed_ref[...] = (parts[0] * LANES + parts[1]).astype(jnp.int32)


def look_up(table_ref, index_ref, scales_ref):
    index = index_ref[...]
    scales = jnp.full(index.shape, table_ref[0], f32)
    for level in range(1, table_ref.shape[0]):
        scales = jnp.where(index == level, table_ref[level], scales)
    scales_ref[...] = scales


def dequantized(geno_ref, scales_ref, first):
    rows = geno_ref.shape[0]
    group = 128
    out = []
    for g in range(rows // group):
        scale = scales_ref[pl.ds(first // group + g, 1), :]
        wide = geno_ref[g * group : (g + 1) * group, :].astype(f32) * scale
        out.append(wide.astype(bf16))
    return jnp.concatenate(out, 0)


def screen_kernel(
    table_ref,
    active_ref,
    admit_ref,
    index_hbm,
    resid_hbm,
    geno_hbm,
    out_ref,
    holder_ref,
    serial_ref,
    packed_ref,
    rank_ref,
    core_ref,
    index_ref,
    resid_ref,
    geno_ref,
    scales_ref,
    ids_ref,
    sems,
):
    chunks, rows, width = geno_ref.shape
    pieces = [(index_hbm, index_ref), (resid_hbm, resid_ref)]
    pieces += [(geno_hbm.at[pl.ds(n * rows, rows)], geno_ref.at[n]) for n in range(chunks)]
    copies = [pltpu.make_async_copy(*piece, sems.at[n]) for n, piece in enumerate(pieces)]
    for copy in copies:
        copy.start()
    rank_ref[...] = jnp.full(rank_ref.shape, lax.axis_index(VAR), jnp.int32)
    core_ref[...] = jnp.full(core_ref.shape, lax.axis_index("core"), jnp.int32)
    lay_out(width, active_ref, admit_ref, holder_ref, serial_ref, packed_ref, ids_ref)
    copies[0].wait()
    look_up(table_ref, index_ref, scales_ref)
    copies[1].wait()
    scores = jnp.zeros(out_ref.shape, f32)
    for n in range(chunks):
        copies[2 + n].wait()
        x = dequantized(geno_ref.at[n], scales_ref, n * rows)
        scores += dot(resid_ref[:, n * rows : (n + 1) * rows].astype(bf16), x)
    out_ref[...] = scores


def screen(table, geno, index, resid, active_ids, admit_ids):
    samples, width = geno.shape
    phenos = resid.shape[0]
    active_ids, admit_ids = active_ids[None], admit_ids[None]
    fit = active_ids.size + admit_ids.size
    tile = (2 * HALF, LANES)
    integers = [(1, fit), (1, fit), (lax.axis_size(VAR), LANES), tile, tile]
    chunks = 8
    vmem = pl.BlockSpec(memory_space=pltpu.VMEM)
    hbm = pl.BlockSpec(memory_space=pltpu.HBM)
    return pl.pallas_call(
        screen_kernel,
        in_specs=[pl.BlockSpec(memory_space=pltpu.SMEM), vmem, vmem, hbm, hbm, hbm],
        out_shape=[jax.ShapeDtypeStruct((phenos, width), f32)]
        + [jax.ShapeDtypeStruct(shape, jnp.int32) for shape in integers],
        scratch_shapes=[
            pltpu.VMEM(index.shape, jnp.int32),
            pltpu.VMEM(resid.shape, f32),
            pltpu.VMEM((chunks, samples // chunks, width), bf16),
            pltpu.VMEM(index.shape, f32),
            pltpu.VMEM((1, fit), jnp.int32),
            pltpu.SemaphoreType.DMA((2 + chunks,)),
        ],
        compiler_params=LARGE,
        cost_estimate=pl.CostEstimate(
            flops=2 * phenos * samples * width, bytes_accessed=2 * samples * width, transcendentals=0
        ),
        name="screen",
    )(table, active_ids, admit_ids, index, resid, geno)


def select_kernel(
    own,
    skip,
    table_ref,
    packed_ref,
    index_ref,
    geno_hbm,
    out_ref,
    scales_ref,
    pick_ref,
    geno_ref,
    sems,
    piece_ref=None,
    out_sems=None,
):
    half = geno_hbm.shape[0] // 2
    chunks, rows = geno_ref.shape[:2]
    core = lax.axis_index("core")
    first = (core if own else 1 - core) * half + skip
    copies = []
    for n in range(chunks):
        at = pl.multiple_of(first + n * rows, rows)
        copies.append(
            pltpu.make_async_copy(geno_hbm.at[pl.ds(at, rows)], geno_ref.at[n], sems.at[n])
        )
        copies[n].start()
    look_up(table_ref, index_ref, scales_ref)
    wanted = column_row(packed_ref[...])

    @pl.loop(0, pick_ref.shape[0], step=ROWS)
    def _(at):
        here = iota((ROWS, pick_ref.shape[1]), 0) + (at + 1) == wanted
        pick_ref[pl.ds(pl.multiple_of(at, ROWS), ROWS), :] = here.astype(f32).astype(bf16)

    outs = []
    for n in range(chunks):
        copies[n].wait()
        x = dequantized(geno_ref.at[n], scales_ref, first + n * rows)
        piece = dot(x, pick_ref[...]).astype(bf16)
        there = pl.ds(n * rows, rows)
        if piece_ref is None:
            out_ref[there, :] = piece
        else:
            piece_ref[n] = piece
            outs.append(
                pltpu.make_async_copy(piece_ref.at[n], out_ref.at[there], out_sems.at[n])
            )
            outs[n].start()
    for out in outs:
        out.wait()


def select(own, part, parts, table, packed, geno, index, params):
    samples, width = geno.shape[0] // 2 // parts, geno.shape[1]
    held = packed.shape[0] * CAP
    chunks = 2
    rows = samples // chunks
    vmem = pl.BlockSpec(memory_space=pltpu.VMEM)
    pieces = [pltpu.VMEM((chunks, rows, held), bf16), pltpu.SemaphoreType.DMA((chunks,))]
    return pl.pallas_call(
        functools.partial(select_kernel, own, part * samples),
        in_specs=[
            pl.BlockSpec(memory_space=pltpu.SMEM),
            vmem,
            vmem,
            pl.BlockSpec(memory_space=pltpu.HBM),
        ],
        out_specs=pl.BlockSpec(memory_space=pltpu.HBM) if own else vmem,
        out_shape=jax.ShapeDtypeStruct((samples, held), bf16),
        scratch_shapes=[
            pltpu.VMEM(index.shape, f32),
            pltpu.VMEM((width, held), bf16),
            pltpu.VMEM((chunks, rows, width), bf16),
            pltpu.SemaphoreType.DMA((chunks,)),
            *(pieces if own else ()),
        ],
        compiler_params=params,
        cost_estimate=pl.CostEstimate(
            flops=2 * samples * width * held, bytes_accessed=2 * samples * width, transcendentals=0
        ),
        name="select",
    )(table, packed, index, geno)


def pick_kernel(
    inv_root, own_ref, one_ref, two_ref, three_ref, packed_ref, scores_ref, pay_ref
):
    scores = ((own_ref[...] + two_ref[...]) + (one_ref[...] + three_ref[...])) * inv_root
    scores_ref[...] = scores
    wanted = column_row(packed_ref[...])
    stacked = jnp.concatenate(thirds(scores), 0)
    phenos, width = scores.shape
    total = jnp.zeros((stacked.shape[0], wanted.shape[1]), f32)
    for at in range(0, width, ROWS):
        here = iota((ROWS, wanted.shape[1]), 0) + (at + 1) == wanted
        total += dot(stacked[:, at : at + ROWS], here.astype(f32).astype(bf16))
    held = total[:phenos] + total[phenos : 2 * phenos] + total[2 * phenos :]
    for t in range(wanted.shape[1] // LANES):
        pay_ref[8 * t : 8 * t + 8, :] = swapped(held[:, t * LANES : (t + 1) * LANES])


def pick(parts, packed, inv_root):
    return pl.pallas_call(
        functools.partial(pick_kernel, inv_root),
        out_shape=(
            jax.ShapeDtypeStruct(parts[0].shape, f32),
            jax.ShapeDtypeStruct((packed.shape[0] * HALF, LANES), f32),
        ),
        compiler_params=SMALL,
        name="pick",
    )(*parts, packed)


def direction_step(data, serial_ref, holder_ref, inverse_ref, advance, wide_ref, d_ref, pay_ref):
    fit = serial_ref.shape[1]
    holders = data.shape[0] // HALF
    spread, mask = slot_maps(serial_ref[...], holder_ref[...], holders)
    high, mid, low = thirds(data)
    placed = (dot(high, spread) + dot(mid, spread) + dot(low, spread)) * mask
    placed = jnp.sum(placed.reshape(-1, 2 * HALF, 2 * fit), 0)
    arrived = placed[:HALF] + placed[HALF:]
    inner = advance(arrived)
    wide_ref[:HALF, :] = inner[:, :fit]
    wide_ref[HALF:, :] = inner[:, fit:]
    blocks, size = inverse_ref.shape[0], inverse_ref.shape[1]
    for b in range(blocks):
        moved = dot_t(
            wide_ref[:, b * size : (b + 1) * size], inverse_ref[b], precision=lax.Precision.HIGHEST
        )
        moved = moved.astype(bf16).astype(f32)
        d_ref[:, b * size : (b + 1) * size] = moved[:HALF]
        d_ref[:, fit + b * size : fit + (b + 1) * size] = moved[HALF:]
    d = d_ref[...]
    d = jnp.concatenate([d, d], 0)
    d = jnp.broadcast_to(d[None], (holders * HALF // d.shape[0], *d.shape)).reshape(mask.shape)
    pay_ref[...] = dot_t((d * mask).astype(bf16), spread)


def first_owner_kernel(
    data_ref,
    serial_ref,
    holder_ref,
    inverse_ref,
    beta_ref,
    pay_ref,
    b_ref,
    d_ref,
    g_ref,
    wide_ref,
):
    fit = serial_ref.shape[1]
    active = beta_ref.shape[1]
    b_ref[...] = jnp.zeros_like(b_ref)
    b_ref[:, :active] = beta_ref[:HALF]
    b_ref[:, fit : fit + active] = beta_ref[HALF:]

    def advance(arrived):
        g_ref[...] = arrived
        return arrived - penalty * b_ref[...]

    direction_step(
        data_ref[...], serial_ref, holder_ref, inverse_ref, advance, wide_ref, d_ref, pay_ref
    )


def owner_kernel(
    data_ref,
    serial_ref,
    holder_ref,
    inverse_ref,
    b_in,
    d_in,
    g_in,
    resid_in,
    update_ref,
    pay_ref,
    b_ref,
    d_ref,
    resid_ref,
    g_ref,
    wide_ref,
    sum_ref,
    rows_ref,
    scalar_ref,
):
    fit = serial_ref.shape[1]
    chunk = sum_ref.shape[0]
    total = data_ref[:chunk, :]
    for at in range(chunk, data_ref.shape[0], chunk):
        total = total + data_ref[at : at + chunk, :]
    sum_ref[...] = total
    for k in range(chunk // (HALF + 1)):
        at = k * (HALF + 1)
        rows_ref[k * HALF : (k + 1) * HALF, :] = sum_ref[at : at + HALF, :]
        if k < scalar_ref.shape[0]:
            scalar_ref[k : k + 1, :] = sum_ref[at + HALF : at + HALF + 1, :]
    factor = scalar_ref[:, :1] / (scalar_ref[:, CAP : CAP + 1] + epsilon)
    resid_ref[...] = resid_in[...] - factor * update_ref[...]
    low = iota((HALF, 2 * fit), 1) < fit
    factor = jnp.where(low, factor[:HALF], factor[HALF:])

    def advance(arrived):
        g_ref[...] = g_in[...] - factor * arrived
        b_ref[...] = b_in[...] + factor * d_in[...]
        return g_ref[...] - penalty * b_ref[...]

    direction_step(
        rows_ref[...], serial_ref, holder_ref, inverse_ref, advance, wide_ref, d_ref, pay_ref
    )


def owner_first(data, serial, holder, inverse, beta):
    fit = serial.shape[1]
    held = jax.ShapeDtypeStruct((HALF, 2 * fit), f32)
    return pl.pallas_call(
        first_owner_kernel,
        out_shape=(jax.ShapeDtypeStruct(data.shape, f32), held, held, held),
        scratch_shapes=[pltpu.VMEM((2 * HALF, fit), f32)],
        compiler_params=SMALL,
        name="owner_first",
    )(data, serial, holder, inverse, beta)


def owner_next(data, serial, holder, inverse, state, resid, update, final):
    fit = serial.shape[1]
    phenos = resid.shape[0]
    held = jax.ShapeDtypeStruct((HALF, 2 * fit), f32)
    rows = lax.axis_size(VAR) * HALF
    pay = jax.ShapeDtypeStruct((rows, LANES), f32)
    new_resid = jax.ShapeDtypeStruct(resid.shape, f32)
    return pl.pallas_call(
        owner_kernel,
        out_shape=(pay, held, held, new_resid) + (() if final else (held,)),
        scratch_shapes=([pltpu.VMEM(held.shape, f32)] if final else [])
        + [
            pltpu.VMEM((phenos, fit), f32),
            pltpu.VMEM((rows // HALF * (HALF + 1), LANES), f32),
            pltpu.VMEM((rows, LANES), f32),
            pltpu.VMEM((phenos, LANES), f32),
        ],
        compiler_params=SMALL,
        name="owner_next",
    )(data, serial, holder, inverse, *state, resid, update)


def update_kernel(pay_ref, columns_ref, out_ref, ready=lambda at: None):
    packed = jnp.concatenate(
        [swapped(pay_ref[at : at + 8, :]) for at in range(0, pay_ref.shape[0], 8)], 1
    ).astype(bf16)
    for at in range(0, out_ref.shape[1], ROWS):
        ready(at)
        out_ref[:, at : at + ROWS] = dot_t(packed, columns_ref[at : at + ROWS, :])


def fetching_kernel(pay_ref, one_hbm, two_hbm, out_ref, columns_ref, sems):
    rows = one_hbm.shape[0]
    copies = {}
    for n, piece in enumerate((one_hbm, two_hbm)):
        for at in range(0, rows, ROWS):
            to = n * rows + at
            copies[to] = pltpu.make_async_copy(
                piece.at[pl.ds(at, ROWS)], columns_ref.at[pl.ds(to, ROWS)], sems.at[to // ROWS]
            )
            copies[to].start()
    update_kernel(pay_ref, columns_ref, out_ref, lambda at: copies[at].wait())


def first_update(pay, one, two):
    samples, held = 2 * one.shape[0], one.shape[1]
    vmem = pl.BlockSpec(memory_space=pltpu.VMEM)
    hbm = pl.BlockSpec(memory_space=pltpu.HBM)
    return pl.pallas_call(
        fetching_kernel,
        in_specs=[vmem, hbm, hbm],
        out_specs=(vmem, vmem),
        out_shape=(
            jax.ShapeDtypeStruct((2 * HALF, samples), f32),
            jax.ShapeDtypeStruct((samples, held), bf16),
        ),
        scratch_shapes=[pltpu.SemaphoreType.DMA((samples // ROWS,))],
        compiler_params=MEDIUM,
        cost_estimate=pl.CostEstimate(
            flops=512 * samples * held, bytes_accessed=2 * samples * held, transcendentals=0
        ),
        name="update_first",
    )(pay, one, two)


def partial_update(pay, columns):
    samples, held = columns.shape
    return pl.pallas_call(
        update_kernel,
        out_shape=jax.ShapeDtypeStruct((2 * HALF, samples), f32),
        compiler_params=SMALL,
        cost_estimate=pl.CostEstimate(
            flops=512 * samples * held, bytes_accessed=2 * samples * held, transcendentals=0
        ),
        name="update",
    )(pay, columns)


def spread_kernel(keep_ref, arrived_ref, out_ref):
    out_ref[...] = jnp.broadcast_to((keep_ref[...] + arrived_ref[...])[None], out_ref.shape)


def spread(keep, arrived, copies):
    return pl.pallas_call(
        spread_kernel,
        out_shape=jax.ShapeDtypeStruct((copies, *keep.shape), f32),
        compiler_params=SMALL,
        name="spread",
    )(keep, arrived)


def total_kernel(parts_ref, out_ref):
    total = parts_ref[0]
    for n in range(1, parts_ref.shape[0]):
        total = total + parts_ref[n]
    out_ref[...] = total


def total(parts):
    return pl.pallas_call(
        total_kernel,
        out_shape=jax.ShapeDtypeStruct(parts.shape[1:], f32),
        compiler_params=SMALL,
        name="total",
    )(parts)


def whole_update(inv_root, core_ref, mine_ref, other_ref):
    first = core_ref[:, :1] == 0
    mine, other = mine_ref[...] * inv_root, other_ref[...] * inv_root
    return jnp.concatenate([jnp.where(first, mine, other), jnp.where(first, other, mine)], 1)


def step_sums(resid, update):
    cross = jnp.sum(resid * update, 1, keepdims=True)
    square = jnp.sum(update * update, 1, keepdims=True)
    return jnp.where(iota((update.shape[0], LANES), 1) < CAP, cross, square)


def two_parts(update):
    high = update.astype(bf16)
    return jnp.concatenate([high, (update - high.astype(f32)).astype(bf16)], 0)


def gradient_kernel(inv_root, mine_ref, columns_ref, out_ref):
    out_ref[...] = dot(two_parts(mine_ref[...] * inv_root), columns_ref[...])


def own_gradient(mine, columns, inv_root):
    samples, held = columns.shape
    return pl.pallas_call(
        functools.partial(gradient_kernel, inv_root),
        out_shape=jax.ShapeDtypeStruct((2 * mine.shape[0], held), f32),
        compiler_params=SMALL,
        cost_estimate=pl.CostEstimate(
            flops=512 * samples * held, bytes_accessed=2 * samples * held, transcendentals=0
        ),
        name="gradient",
    )(mine, columns)


def descent_kernel(
    inv_root,
    rank_ref,
    core_ref,
    mine_ref,
    other_ref,
    resid_ref,
    own_ref,
    columns_ref,
    out_ref,
    update_ref,
):
    update = whole_update(inv_root, core_ref, mine_ref, other_ref)
    update_ref[...] = update
    phenos = update.shape[0]
    grad = own_ref[...] + dot(two_parts(other_ref[...] * inv_root), columns_ref[...])
    grad = (grad[:phenos] + grad[phenos:]) * inv_root
    both = step_sums(resid_ref[...], update)
    mine = iota(both.shape, 0) == lax.rem(rank_ref[...], phenos)
    row = jnp.sum(jnp.where(mine, both, 0.0), 0, keepdims=True)
    chunk = HALF + 1
    owners = grad.shape[1] // CAP
    copies = out_ref.shape[0] // (chunk * owners)
    for t in range(owners // 2):
        pair = swapped(grad[:, t * LANES : (t + 1) * LANES])
        for n in range(copies):
            at = (n * owners + 2 * t) * chunk
            out_ref[at : at + HALF, :] = pair[:HALF]
            out_ref[at + HALF : at + HALF + 1, :] = row
            out_ref[at + chunk : at + chunk + HALF, :] = pair[HALF:]
            out_ref[at + chunk + HALF : at + 2 * chunk, :] = row


def descent(rank, core, mine, other, resid, own, columns, inv_root, copies):
    out = (copies * (columns.shape[1] // CAP) * (HALF + 1), LANES)
    return pl.pallas_call(
        functools.partial(descent_kernel, inv_root),
        out_shape=(jax.ShapeDtypeStruct(out, f32), jax.ShapeDtypeStruct(resid.shape, f32)),
        compiler_params=SMALL,
        name="descent",
    )(rank, core, mine, other, resid, own, columns)


def settle_kernel(inv_root, core_ref, mine_ref, resid_ref, sums_ref):
    half = mine_ref.shape[1]
    resid = jnp.where(core_ref[:, :1] == 0, resid_ref[:, :half], resid_ref[:, half:])
    sums = step_sums(resid, mine_ref[...] * inv_root)
    sums_ref[...] = jnp.broadcast_to(sums[None], sums_ref.shape)


def settle(core, mine, resid, inv_root, copies):
    return pl.pallas_call(
        functools.partial(settle_kernel, inv_root),
        out_shape=jax.ShapeDtypeStruct((copies, resid.shape[0], LANES), f32),
        compiler_params=SMALL,
        name="settle",
    )(core, mine, resid)


def last_kernel(
    inv_root, sums_ref, core_ref, mine_ref, other_ref, b_ref, d_ref, resid_ref, coeffs_ref, out_ref
):
    phenos, fit = coeffs_ref.shape
    total = sums_ref[0]
    for j in range(1, sums_ref.shape[0]):
        total = total + sums_ref[j]
    factor = total[:, :1] / (total[:, CAP : CAP + 1] + epsilon)
    for half in range(2):
        rows = slice(half * HALF, (half + 1) * HALF)
        cols = slice(half * fit, (half + 1) * fit)
        coeffs_ref[rows, :] = b_ref[:, cols] + factor[rows] * d_ref[:, cols]
    update = whole_update(inv_root, core_ref, mine_ref, other_ref)
    out_ref[...] = resid_ref[...] - factor * update


def last(sums, core, mine, other, coeffs, direction, resid, inv_root):
    phenos = resid.shape[0]
    return pl.pallas_call(
        functools.partial(last_kernel, inv_root),
        out_shape=(
            jax.ShapeDtypeStruct((phenos, coeffs.shape[1] // 2), f32),
            jax.ShapeDtypeStruct(resid.shape, f32),
        ),
        compiler_params=SMALL,
        name="last",
    )(sums, core, mine, other, coeffs, direction, resid)


def exchange(pay, axes):
    count = lax.axis_size(axes)
    rows = pay.shape[0] // count
    shape = (count, rows, LANES) if rows == HALF else (count, 1, rows * LANES)
    return lax.all_to_all(
        pay.reshape(shape), axes, split_axis=0, concat_axis=0, tiled=True
    ).reshape(pay.shape)


def shifted(x, axis, by=1):
    size = lax.axis_size(axis)
    return lax.ppermute(x, axis, [(i, (i + by) % size) for i in range(size)])


def on_device(
    geno, scale_index, scale_table, residual, beta_active, block_inverse, active_ids, admit_ids
):
    holders = lax.axis_size(VAR)
    samples, width = geno.shape
    copies = lax.axis_size(SAMP)
    inv_root = 1.0 / math.sqrt(samples * copies)

    part, holder, serial, packed, rank, core = screen(
        scale_table, geno, scale_index, residual, active_ids, admit_ids
    )
    part = part + shifted(part, "y_hi")
    parts = [part] + [shifted(part, "x", n) for n in range(1, lax.axis_size("x"))]
    packed = lax.all_to_all(
        packed.reshape(holders, 1, LANES), VAR, split_axis=0, concat_axis=0, tiled=True
    ).reshape(holders, LANES)

    away = select(False, 0, 1, scale_table, packed, geno, scale_index, MEDIUM)
    parts, away = lax.optimization_barrier((parts, away))
    scores, pay = pick(parts, packed, inv_root)
    pay, packed = lax.optimization_barrier((pay, packed))
    one = select(True, 0, 2, scale_table, packed, geno, scale_index, WIDE)
    data, one = lax.optimization_barrier((exchange(pay, VAR), one))
    pay, *state = owner_first(data, serial, holder, block_inverse, beta_active)
    pay, packed = lax.optimization_barrier((pay, packed))
    two = select(True, 1, 2, scale_table, packed, geno, scale_index, WIDE)
    pay, two = lax.optimization_barrier((exchange(pay, VAR), two))
    current = residual
    for pass_index in range(PASSES):
        if pass_index > 0:
            pay = exchange(pay, VAR)
        arrived = shifted(partial_update(pay, away), "core")
        if pass_index > 0:
            keep = partial_update(pay, home)
        else:
            keep, home = first_update(pay, one, two)
        mine = spread(keep, arrived, lax.axis_size(CHIPS))
        mine = total(lax.all_to_all(mine, CHIPS, split_axis=0, concat_axis=0, tiled=True))
        other = shifted(mine, "core")
        if pass_index + 1 == PASSES:
            break
        own = own_gradient(mine, home, inv_root)
        data, update = descent(rank, core, mine, other, current, own, away, inv_root, copies)
        pay, coeffs, direction, current, *gradient = owner_next(
            exchange(data, SAMP + VAR),
            serial,
            holder,
            block_inverse,
            state,
            current,
            update,
            pass_index + 2 == PASSES,
        )
        state = (coeffs, direction, *gradient)

    sums = settle(core, mine, current, inv_root, 2 * copies)
    sums = lax.all_to_all(sums, ("core",) + SAMP, split_axis=0, concat_axis=0, tiled=True)
    return (scores, *last(sums, core, mine, other, coeffs, direction, current, inv_root))


def solution(mesh):
    torus = Mesh(mesh.devices.reshape(2, 4, 2, 2, 4), VAR + SAMP)
    placed = (
        P(SAMP, VAR),
        P(SAMP, VAR),
        P(),
        P(None, SAMP),
        P(None, VAR),
        P(VAR, None, None),
        P(VAR),
        P(VAR),
    )
    return jax.shard_map(
        on_device,
        mesh=torus,
        in_specs=placed,
        out_specs=(P(None, VAR), P(None, VAR), P(None, SAMP)),
        check_vma=False,
    )
```

```python
import functools
import math

import jax
import jax.numpy as jnp
from jax import lax
from jax.experimental import pallas as pl
from jax.experimental.pallas import tpu as pltpu
from jax.sharding import Mesh
from jax.sharding import PartitionSpec as P

PASSES = 3
VAR = ("y_lo", "z", "core")
SAMP = ("y_hi", "x")
CHIPS = ("y_lo", "z")

CAP = 64
LANES = 128
ROWS = 256
HALF = 4

penalty = 0.5
epsilon = 1e-06
SMALL = pltpu.CompilerParams(vmem_limit_bytes=12 * 1024 * 1024)
MEDIUM = pltpu.CompilerParams(vmem_limit_bytes=50 * 1024 * 1024)
WIDE = pltpu.CompilerParams(vmem_limit_bytes=52 * 1024 * 1024)
LARGE = pltpu.CompilerParams(vmem_limit_bytes=60 * 1024 * 1024)
f32 = jnp.float32
bf16 = jnp.bfloat16


def iota(shape, dim):
    return lax.broadcasted_iota(jnp.int32, shape, dim)


def dot(a, b, **kw):
    return jnp.dot(a, b, preferred_element_type=f32, **kw)


def dot_t(a, b, **kw):
    return lax.dot_general(a, b, (((1,), (1,)), ((), ())), preferred_element_type=f32, **kw)


def thirds(x):
    high = x.astype(bf16)
    rest = x - high.astype(f32)
    mid = rest.astype(bf16)
    return high, mid, (rest - mid.astype(f32)).astype(bf16)


def swapped(x):
    here = (iota(x.shape, 0) // HALF) == (iota(x.shape, 1) // CAP)
    return jnp.where(here, x, pltpu.roll(pltpu.roll(x, HALF, 0), CAP, 1))


def column_row(packed):
    low = iota((1, LANES), 1) < CAP
    return jnp.concatenate(
        [
            jnp.where(low, packed[t : t + 1], packed[t + 1 : t + 2])
            for t in range(0, packed.shape[0], 2)
        ],
        1,
    )


def slot_maps(serial, holder, holders):
    fit = serial.shape[1]
    serial2 = jnp.concatenate([serial, serial], 1)
    holder2 = jnp.concatenate([holder, holder], 1)
    shape = (2 * CAP, 2 * fit)
    rows, cols = iota(shape, 0), iota(shape, 1)
    spread = ((rows // CAP) == (cols // fit)) & ((rows % CAP) == serial2)
    mask = (iota((holders * HALF, 2 * fit), 0) // HALF) == holder2
    return spread.astype(f32).astype(bf16), mask.astype(f32)


def lay_out(width, active_ref, admit_ref, holder_ref, serial_ref, packed_ref, ids_ref):
    holders = packed_ref.shape[0]
    fit = holder_ref.shape[1]
    active = active_ref.shape[1]
    ids_ref[:, :active] = active_ref[...]
    ids_ref[:, active:] = admit_ref[...]
    ids = ids_ref[...]
    holder = ids // width
    holder_ref[...] = holder
    marks = (iota((holders, fit), 0) == holder).astype(f32)
    earlier = (iota((fit, fit), 0) < iota((fit, fit), 1)).astype(f32).astype(bf16)
    before = dot(marks.astype(bf16), earlier)
    serial = jnp.sum(before * marks, 0, keepdims=True).astype(jnp.int32)
    serial_ref[...] = serial
    spread, _ = slot_maps(serial, holder, holders)
    marks2 = jnp.concatenate([marks, marks], 1)
    column = ids - holder * width + 1
    parts = []
    for piece in (column // LANES, column % LANES):
        row = piece.astype(f32)
        row = jnp.concatenate([row, row], 1)
        parts.append(dot_t((marks2 * row).astype(bf16), spread))
    packed_ref[...] = (parts[0] * LANES + parts[1]).astype(jnp.int32)


def look_up(table_ref, index_ref, scales_ref):
    index = index_ref[...]
    scales = jnp.full(index.shape, table_ref[0], f32)
    for level in range(1, table_ref.shape[0]):
        scales = jnp.where(index == level, table_ref[level], scales)
    scales_ref[...] = scales


def dequantized(geno_ref, scales_ref, first):
    rows = geno_ref.shape[0]
    group = 128
    out = []
    for g in range(rows // group):
        scale = scales_ref[pl.ds(first // group + g, 1), :]
        wide = geno_ref[g * group : (g + 1) * group, :].astype(f32) * scale
        out.append(wide.astype(bf16))
    return jnp.concatenate(out, 0)


def screen_kernel(
    table_ref,
    active_ref,
    admit_ref,
    index_hbm,
    resid_hbm,
    geno_hbm,
    out_ref,
    holder_ref,
    serial_ref,
    packed_ref,
    rank_ref,
    core_ref,
    index_ref,
    resid_ref,
    geno_ref,
    scales_ref,
    ids_ref,
    sems,
):
    chunks, rows, width = geno_ref.shape
    pieces = [(index_hbm, index_ref), (resid_hbm, resid_ref)]
    pieces += [(geno_hbm.at[pl.ds(n * rows, rows)], geno_ref.at[n]) for n in range(chunks)]
    copies = [pltpu.make_async_copy(*piece, sems.at[n]) for n, piece in enumerate(pieces)]
    for copy in copies:
        copy.start()
    rank_ref[...] = jnp.full(rank_ref.shape, lax.axis_index(VAR), jnp.int32)
    core_ref[...] = jnp.full(core_ref.shape, lax.axis_index("core"), jnp.int32)
    lay_out(width, active_ref, admit_ref, holder_ref, serial_ref, packed_ref, ids_ref)
    copies[0].wait()
    look_up(table_ref, index_ref, scales_ref)
    copies[1].wait()
    scores = jnp.zeros(out_ref.shape, f32)
    for n in range(chunks):
        copies[2 + n].wait()
        x = dequantized(geno_ref.at[n], scales_ref, n * rows)
        scores += dot(resid_ref[:, n * rows : (n + 1) * rows].astype(bf16), x)
    out_ref[...] = scores


def screen(table, geno, index, resid, active_ids, admit_ids):
    samples, width = geno.shape
    phenos = resid.shape[0]
    active_ids, admit_ids = active_ids[None], admit_ids[None]
    fit = active_ids.size + admit_ids.size
    tile = (2 * HALF, LANES)
    integers = [(1, fit), (1, fit), (lax.axis_size(VAR), LANES), tile, tile]
    chunks = 8
    vmem = pl.BlockSpec(memory_space=pltpu.VMEM)
    hbm = pl.BlockSpec(memory_space=pltpu.HBM)
    return pl.pallas_call(
        screen_kernel,
        in_specs=[pl.BlockSpec(memory_space=pltpu.SMEM), vmem, vmem, hbm, hbm, hbm],
        out_shape=[jax.ShapeDtypeStruct((phenos, width), f32)]
        + [jax.ShapeDtypeStruct(shape, jnp.int32) for shape in integers],
        scratch_shapes=[
            pltpu.VMEM(index.shape, jnp.int32),
            pltpu.VMEM(resid.shape, f32),
            pltpu.VMEM((chunks, samples // chunks, width), bf16),
            pltpu.VMEM(index.shape, f32),
            pltpu.VMEM((1, fit), jnp.int32),
            pltpu.SemaphoreType.DMA((2 + chunks,)),
        ],
        compiler_params=LARGE,
        cost_estimate=pl.CostEstimate(
            flops=2 * phenos * samples * width, bytes_accessed=2 * samples * width, transcendentals=0
        ),
        name="screen",
    )(table, active_ids, admit_ids, index, resid, geno)


def select_kernel(
    own,
    table_ref,
    packed_ref,
    index_ref,
    geno_hbm,
    out_ref,
    scales_ref,
    pick_ref,
    geno_ref,
    sems,
    piece_ref=None,
    out_sems=None,
):
    samples = out_ref.shape[0]
    chunks, rows = geno_ref.shape[:2]
    core = lax.axis_index("core")
    first = (core if own else 1 - core) * samples
    copies = []
    for n in range(chunks):
        at = pl.multiple_of(first + n * rows, rows)
        copies.append(
            pltpu.make_async_copy(geno_hbm.at[pl.ds(at, rows)], geno_ref.at[n], sems.at[n])
        )
        copies[n].start()
    look_up(table_ref, index_ref, scales_ref)
    wanted = column_row(packed_ref[...])

    @pl.loop(0, pick_ref.shape[0], step=ROWS)
    def _(at):
        here = iota((ROWS, pick_ref.shape[1]), 0) + (at + 1) == wanted
        pick_ref[pl.ds(pl.multiple_of(at, ROWS), ROWS), :] = here.astype(f32).astype(bf16)

    outs = []
    for n in range(chunks):
        copies[n].wait()
        x = dequantized(geno_ref.at[n], scales_ref, first + n * rows)
        piece = dot(x, pick_ref[...]).astype(bf16)
        there = pl.ds(n * rows, rows)
        if piece_ref is None:
            out_ref[there, :] = piece
        else:
            piece_ref[n] = piece
            outs.append(
                pltpu.make_async_copy(piece_ref.at[n], out_ref.at[there], out_sems.at[n])
            )
            outs[n].start()
    for out in outs:
        out.wait()


def select(own, table, packed, geno, index, params):
    samples, width = geno.shape[0] // 2, geno.shape[1]
    held = packed.shape[0] * CAP
    chunks = 4 if own else 2
    rows = samples // chunks
    vmem = pl.BlockSpec(memory_space=pltpu.VMEM)
    pieces = [pltpu.VMEM((chunks, rows, held), bf16), pltpu.SemaphoreType.DMA((chunks,))]
    return pl.pallas_call(
        functools.partial(select_kernel, own),
        in_specs=[
            pl.BlockSpec(memory_space=pltpu.SMEM),
            vmem,
            vmem,
            pl.BlockSpec(memory_space=pltpu.HBM),
        ],
        out_specs=pl.BlockSpec(memory_space=pltpu.HBM) if own else vmem,
        out_shape=jax.ShapeDtypeStruct((samples, held), bf16),
        scratch_shapes=[
            pltpu.VMEM(index.shape, f32),
            pltpu.VMEM((width, held), bf16),
            pltpu.VMEM((chunks, rows, width), bf16),
            pltpu.SemaphoreType.DMA((chunks,)),
            *(pieces if own else ()),
        ],
        compiler_params=params,
        cost_estimate=pl.CostEstimate(
            flops=2 * samples * width * held, bytes_accessed=2 * samples * width, transcendentals=0
        ),
        name="select",
    )(table, packed, index, geno)


def pick_kernel(inv_root, own_ref, other_ref, packed_ref, scores_ref, pay_ref):
    scores = (own_ref[...] + other_ref[...]) * inv_root
    scores_ref[...] = scores
    wanted = column_row(packed_ref[...])
    stacked = jnp.concatenate(thirds(scores), 0)
    phenos, width = scores.shape
    total = jnp.zeros((stacked.shape[0], wanted.shape[1]), f32)
    for at in range(0, width, ROWS):
        here = iota((ROWS, wanted.shape[1]), 0) + (at + 1) == wanted
        total += dot(stacked[:, at : at + ROWS], here.astype(f32).astype(bf16))
    held = total[:phenos] + total[phenos : 2 * phenos] + total[2 * phenos :]
    for t in range(wanted.shape[1] // LANES):
        pay_ref[8 * t : 8 * t + 8, :] = swapped(held[:, t * LANES : (t + 1) * LANES])


def pick(parts, packed, inv_root):
    return pl.pallas_call(
        functools.partial(pick_kernel, inv_root),
        out_shape=(
            jax.ShapeDtypeStruct(parts[0].shape, f32),
            jax.ShapeDtypeStruct((packed.shape[0] * HALF, LANES), f32),
        ),
        compiler_params=SMALL,
        name="pick",
    )(*parts, packed)


def direction_step(data, serial_ref, holder_ref, inverse_ref, advance, wide_ref, d_ref, pay_ref):
    fit = serial_ref.shape[1]
    holders = data.shape[0] // HALF
    spread, mask = slot_maps(serial_ref[...], holder_ref[...], holders)
    high, mid, low = thirds(data)
    placed = (dot(high, spread) + dot(mid, spread) + dot(low, spread)) * mask
    placed = jnp.sum(placed.reshape(-1, 2 * HALF, 2 * fit), 0)
    arrived = placed[:HALF] + placed[HALF:]
    inner = advance(arrived)
    wide_ref[:HALF, :] = inner[:, :fit]
    wide_ref[HALF:, :] = inner[:, fit:]
    blocks, size = inverse_ref.shape[0], inverse_ref.shape[1]
    for b in range(blocks):
        moved = dot_t(
            wide_ref[:, b * size : (b + 1) * size], inverse_ref[b], precision=lax.Precision.HIGHEST
        )
        moved = moved.astype(bf16).astype(f32)
        d_ref[:, b * size : (b + 1) * size] = moved[:HALF]
        d_ref[:, fit + b * size : fit + (b + 1) * size] = moved[HALF:]
    d = d_ref[...]
    d = jnp.concatenate([d, d], 0)
    d = jnp.broadcast_to(d[None], (holders * HALF // d.shape[0], *d.shape)).reshape(mask.shape)
    pay_ref[...] = dot_t((d * mask).astype(bf16), spread)


def first_owner_kernel(
    data_ref,
    serial_ref,
    holder_ref,
    inverse_ref,
    beta_ref,
    columns_hbm,
    pay_ref,
    b_ref,
    d_ref,
    g_ref,
    columns_ref,
    wide_ref,
    sem,
):
    copy = pltpu.make_async_copy(columns_hbm, columns_ref, sem)
    copy.start()
    fit = serial_ref.shape[1]
    active = beta_ref.shape[1]
    b_ref[...] = jnp.zeros_like(b_ref)
    b_ref[:, :active] = beta_ref[:HALF]
    b_ref[:, fit : fit + active] = beta_ref[HALF:]

    def advance(arrived):
        g_ref[...] = arrived
        return arrived - penalty * b_ref[...]

    direction_step(
        data_ref[...], serial_ref, holder_ref, inverse_ref, advance, wide_ref, d_ref, pay_ref
    )
    copy.wait()


def owner_kernel(
    data_ref,
    serial_ref,
    holder_ref,
    inverse_ref,
    b_in,
    d_in,
    g_in,
    resid_in,
    update_ref,
    pay_ref,
    b_ref,
    d_ref,
    resid_ref,
    g_ref,
    wide_ref,
    sum_ref,
    rows_ref,
    scalar_ref,
):
    fit = serial_ref.shape[1]
    chunk = sum_ref.shape[0]
    total = data_ref[:chunk, :]
    for at in range(chunk, data_ref.shape[0], chunk):
        total = total + data_ref[at : at + chunk, :]
    sum_ref[...] = total
    for k in range(chunk // (HALF + 1)):
        at = k * (HALF + 1)
        rows_ref[k * HALF : (k + 1) * HALF, :] = sum_ref[at : at + HALF, :]
        if k < scalar_ref.shape[0]:
            scalar_ref[k : k + 1, :] = sum_ref[at + HALF : at + HALF + 1, :]
    factor = scalar_ref[:, :1] / (scalar_ref[:, CAP : CAP + 1] + epsilon)
    resid_ref[...] = resid_in[...] - factor * update_ref[...]
    low = iota((HALF, 2 * fit), 1) < fit
    factor = jnp.where(low, factor[:HALF], factor[HALF:])

    def advance(arrived):
        g_ref[...] = g_in[...] - factor * arrived
        b_ref[...] = b_in[...] + factor * d_in[...]
        return g_ref[...] - penalty * b_ref[...]

    direction_step(
        rows_ref[...], serial_ref, holder_ref, inverse_ref, advance, wide_ref, d_ref, pay_ref
    )


def owner_first(data, serial, holder, inverse, beta, columns):
    fit = serial.shape[1]
    held = jax.ShapeDtypeStruct((HALF, 2 * fit), f32)
    vmem = pl.BlockSpec(memory_space=pltpu.VMEM)
    return pl.pallas_call(
        first_owner_kernel,
        in_specs=[vmem] * 5 + [pl.BlockSpec(memory_space=pltpu.HBM)],
        out_specs=(vmem,) * 5,
        out_shape=(
            jax.ShapeDtypeStruct(data.shape, f32),
            held,
            held,
            held,
            jax.ShapeDtypeStruct(columns.shape, columns.dtype),
        ),
        scratch_shapes=[pltpu.VMEM((2 * HALF, fit), f32), pltpu.SemaphoreType.DMA],
        compiler_params=MEDIUM,
        name="owner_first",
    )(data, serial, holder, inverse, beta, columns)


def owner_next(data, serial, holder, inverse, state, resid, update, final):
    fit = serial.shape[1]
    phenos = resid.shape[0]
    held = jax.ShapeDtypeStruct((HALF, 2 * fit), f32)
    rows = lax.axis_size(VAR) * HALF
    pay = jax.ShapeDtypeStruct((rows, LANES), f32)
    new_resid = jax.ShapeDtypeStruct(resid.shape, f32)
    return pl.pallas_call(
        owner_kernel,
        out_shape=(pay, held, held, new_resid) + (() if final else (held,)),
        scratch_shapes=([pltpu.VMEM(held.shape, f32)] if final else [])
        + [
            pltpu.VMEM((phenos, fit), f32),
            pltpu.VMEM((rows // HALF * (HALF + 1), LANES), f32),
            pltpu.VMEM((rows, LANES), f32),
            pltpu.VMEM((phenos, LANES), f32),
        ],
        compiler_params=SMALL,
        name="owner_next",
    )(data, serial, holder, inverse, *state, resid, update)


def update_kernel(pay_ref, columns_ref, out_ref):
    packed = jnp.concatenate(
        [swapped(pay_ref[at : at + 8, :]) for at in range(0, pay_ref.shape[0], 8)], 1
    ).astype(bf16)
    for at in range(0, out_ref.shape[1], ROWS):
        out_ref[:, at : at + ROWS] = dot_t(packed, columns_ref[at : at + ROWS, :])


def partial_update(pay, columns):
    samples, held = columns.shape
    return pl.pallas_call(
        update_kernel,
        out_shape=jax.ShapeDtypeStruct((2 * HALF, samples), f32),
        compiler_params=SMALL,
        cost_estimate=pl.CostEstimate(
            flops=512 * samples * held, bytes_accessed=2 * samples * held, transcendentals=0
        ),
        name="update",
    )(pay, columns)


def spread_kernel(keep_ref, arrived_ref, out_ref):
    out_ref[...] = jnp.broadcast_to((keep_ref[...] + arrived_ref[...])[None], out_ref.shape)


def spread(keep, arrived, copies):
    return pl.pallas_call(
        spread_kernel,
        out_shape=jax.ShapeDtypeStruct((copies, *keep.shape), f32),
        compiler_params=SMALL,
        name="spread",
    )(keep, arrived)


def total_kernel(parts_ref, out_ref):
    total = parts_ref[0]
    for n in range(1, parts_ref.shape[0]):
        total = total + parts_ref[n]
    out_ref[...] = total


def total(parts):
    return pl.pallas_call(
        total_kernel,
        out_shape=jax.ShapeDtypeStruct(parts.shape[1:], f32),
        compiler_params=SMALL,
        name="total",
    )(parts)


def whole_update(inv_root, core_ref, mine_ref, other_ref):
    first = core_ref[:, :1] == 0
    mine, other = mine_ref[...] * inv_root, other_ref[...] * inv_root
    return jnp.concatenate([jnp.where(first, mine, other), jnp.where(first, other, mine)], 1)


def step_sums(resid, update):
    cross = jnp.sum(resid * update, 1, keepdims=True)
    square = jnp.sum(update * update, 1, keepdims=True)
    return jnp.where(iota((update.shape[0], LANES), 1) < CAP, cross, square)


def two_parts(update):
    high = update.astype(bf16)
    return jnp.concatenate([high, (update - high.astype(f32)).astype(bf16)], 0)


def gradient_kernel(inv_root, mine_ref, columns_ref, out_ref):
    out_ref[...] = dot(two_parts(mine_ref[...] * inv_root), columns_ref[...])


def own_gradient(mine, columns, inv_root):
    samples, held = columns.shape
    return pl.pallas_call(
        functools.partial(gradient_kernel, inv_root),
        out_shape=jax.ShapeDtypeStruct((2 * mine.shape[0], held), f32),
        compiler_params=SMALL,
        cost_estimate=pl.CostEstimate(
            flops=512 * samples * held, bytes_accessed=2 * samples * held, transcendentals=0
        ),
        name="gradient",
    )(mine, columns)


def descent_kernel(
    inv_root,
    rank_ref,
    core_ref,
    mine_ref,
    other_ref,
    resid_ref,
    own_ref,
    columns_ref,
    out_ref,
    update_ref,
):
    update = whole_update(inv_root, core_ref, mine_ref, other_ref)
    update_ref[...] = update
    phenos = update.shape[0]
    grad = own_ref[...] + dot(two_parts(other_ref[...] * inv_root), columns_ref[...])
    grad = (grad[:phenos] + grad[phenos:]) * inv_root
    both = step_sums(resid_ref[...], update)
    mine = iota(both.shape, 0) == lax.rem(rank_ref[...], phenos)
    row = jnp.sum(jnp.where(mine, both, 0.0), 0, keepdims=True)
    chunk = HALF + 1
    owners = grad.shape[1] // CAP
    copies = out_ref.shape[0] // (chunk * owners)
    for t in range(owners // 2):
        pair = swapped(grad[:, t * LANES : (t + 1) * LANES])
        for n in range(copies):
            at = (n * owners + 2 * t) * chunk
            out_ref[at : at + HALF, :] = pair[:HALF]
            out_ref[at + HALF : at + HALF + 1, :] = row
            out_ref[at + chunk : at + chunk + HALF, :] = pair[HALF:]
            out_ref[at + chunk + HALF : at + 2 * chunk, :] = row


def descent(rank, core, mine, other, resid, own, columns, inv_root, copies):
    out = (copies * (columns.shape[1] // CAP) * (HALF + 1), LANES)
    return pl.pallas_call(
        functools.partial(descent_kernel, inv_root),
        out_shape=(jax.ShapeDtypeStruct(out, f32), jax.ShapeDtypeStruct(resid.shape, f32)),
        compiler_params=SMALL,
        name="descent",
    )(rank, core, mine, other, resid, own, columns)


def settle_kernel(inv_root, core_ref, mine_ref, resid_ref, sums_ref):
    half = mine_ref.shape[1]
    resid = jnp.where(core_ref[:, :1] == 0, resid_ref[:, :half], resid_ref[:, half:])
    sums = step_sums(resid, mine_ref[...] * inv_root)
    sums_ref[...] = jnp.broadcast_to(sums[None], sums_ref.shape)


def settle(core, mine, resid, inv_root, copies):
    return pl.pallas_call(
        functools.partial(settle_kernel, inv_root),
        out_shape=jax.ShapeDtypeStruct((copies, resid.shape[0], LANES), f32),
        compiler_params=SMALL,
        name="settle",
    )(core, mine, resid)


def last_kernel(
    inv_root, sums_ref, core_ref, mine_ref, other_ref, b_ref, d_ref, resid_ref, coeffs_ref, out_ref
):
    phenos, fit = coeffs_ref.shape
    total = sums_ref[0]
    for j in range(1, sums_ref.shape[0]):
        total = total + sums_ref[j]
    factor = total[:, :1] / (total[:, CAP : CAP + 1] + epsilon)
    for half in range(2):
        rows = slice(half * HALF, (half + 1) * HALF)
        cols = slice(half * fit, (half + 1) * fit)
        coeffs_ref[rows, :] = b_ref[:, cols] + factor[rows] * d_ref[:, cols]
    update = whole_update(inv_root, core_ref, mine_ref, other_ref)
    out_ref[...] = resid_ref[...] - factor * update


def last(sums, core, mine, other, coeffs, direction, resid, inv_root):
    phenos = resid.shape[0]
    return pl.pallas_call(
        functools.partial(last_kernel, inv_root),
        out_shape=(
            jax.ShapeDtypeStruct((phenos, coeffs.shape[1] // 2), f32),
            jax.ShapeDtypeStruct(resid.shape, f32),
        ),
        compiler_params=SMALL,
        name="last",
    )(sums, core, mine, other, coeffs, direction, resid)


def exchange(pay, axes):
    count = lax.axis_size(axes)
    rows = pay.shape[0] // count
    shape = (count, rows, LANES) if rows == HALF else (count, 1, rows * LANES)
    return lax.all_to_all(
        pay.reshape(shape), axes, split_axis=0, concat_axis=0, tiled=True
    ).reshape(pay.shape)


def shifted(x, axis, by=1):
    size = lax.axis_size(axis)
    return lax.ppermute(x, axis, [(i, (i + by) % size) for i in range(size)])


def on_device(
    geno, scale_index, scale_table, residual, beta_active, block_inverse, active_ids, admit_ids
):
    holders = lax.axis_size(VAR)
    samples, width = geno.shape
    copies = lax.axis_size(SAMP)
    inv_root = 1.0 / math.sqrt(samples * copies)

    part, holder, serial, packed, rank, core = screen(
        scale_table, geno, scale_index, residual, active_ids, admit_ids
    )
    part = (part + shifted(part, "x", 2)) + (shifted(part, "x", 1) + shifted(part, "x", 3))
    parts = (part, shifted(part, "y_hi"))
    packed = lax.all_to_all(
        packed.reshape(holders, 1, LANES), VAR, split_axis=0, concat_axis=0, tiled=True
    ).reshape(holders, LANES)

    away = select(False, scale_table, packed, geno, scale_index, MEDIUM)
    parts, away = lax.optimization_barrier((parts, away))
    scores, pay = pick(parts, packed, inv_root)
    pay, packed = lax.optimization_barrier((pay, packed))
    home = select(True, scale_table, packed, geno, scale_index, WIDE)
    pay, *state, home = owner_first(
        exchange(pay, VAR), serial, holder, block_inverse, beta_active, home
    )
    current = residual
    for pass_index in range(PASSES):
        pay = exchange(pay, VAR)
        arrived = shifted(partial_update(pay, away), "core")
        mine = spread(partial_update(pay, home), arrived, lax.axis_size(CHIPS))
        mine = total(lax.all_to_all(mine, CHIPS, split_axis=0, concat_axis=0, tiled=True))
        other = shifted(mine, "core")
        if pass_index + 1 == PASSES:
            break
        own = own_gradient(mine, home, inv_root)
        data, update = descent(rank, core, mine, other, current, own, away, inv_root, copies)
        pay, coeffs, direction, current, *gradient = owner_next(
            exchange(data, SAMP + VAR),
            serial,
            holder,
            block_inverse,
            state,
            current,
            update,
            pass_index + 2 == PASSES,
        )
        state = (coeffs, direction, *gradient)

    sums = settle(core, mine, current, inv_root, 2 * copies)
    sums = lax.all_to_all(sums, ("core",) + SAMP, split_axis=0, concat_axis=0, tiled=True)
    return (scores, *last(sums, core, mine, other, coeffs, direction, current, inv_root))


def solution(mesh):
    torus = Mesh(mesh.devices.reshape(2, 4, 2, 2, 4), VAR + SAMP)
    placed = (
        P(SAMP, VAR),
        P(SAMP, VAR),
        P(),
        P(None, SAMP),
        P(None, VAR),
        P(VAR, None, None),
        P(VAR),
        P(VAR),
    )
    return jax.shard_map(
        on_device,
        mesh=torus,
        in_specs=placed,
        out_specs=(P(None, VAR), P(None, VAR), P(None, SAMP)),
        check_vma=False,
    )
```
